32 devices in a mesh: ctx: 8 (over y, x, core), shard: 4 (over z).
Axes of the slice: x: 2, y: 2, z: 4, core: 2. Of those that a mesh axis runs over, the one named last changes fastest.
Arguments:
- hidden_in: bfloat16 [8, 4096, 576], P('shard', 'ctx'), may hold values from -6 to 6
- out_grad: bfloat16 [8, 4096, 576], P('shard', 'ctx'), may hold values from -6 to 6
- block_slot: int32 [8, 8], P('shard'), may hold values from 0 to 7, as said below
- rope_pos: int32 [8, 4096], P('shard', 'ctx'), may hold values from 0 to 8190, as said below
- w_query: bfloat16 [576, 576], P('shard'), may hold values from -0.25 to 0.25
- w_key: bfloat16 [576, 192], P('shard'), may hold values from -0.25 to 0.25
- w_value: bfloat16 [576, 192], P('shard'), may hold values from -0.25 to 0.25
- w_out: bfloat16 [576, 576], P('shard'), may hold values from -1 to 1
- w_gate: bfloat16 [576, 1536], P('shard'), may hold values from -0.25 to 0.25
- w_up: bfloat16 [576, 1536], P('shard'), may hold values from -0.25 to 0.25
- w_down: bfloat16 [1536, 576], P('shard'), may hold values from -0.15625 to 0.15625
- gain_attn: bfloat16 [576], P('shard'), may hold values from 0.5 to 1.5
- gain_mlp: bfloat16 [576], P('shard'), may hold values from 0.5 to 1.5
Outputs:
- block_out: bfloat16 [8, 4096, 576], P('shard', 'ctx')
- in_grad: bfloat16 [8, 4096, 576], P('shard', 'ctx')
- grad_query: float32 [576, 576], P('shard')
- grad_key: float32 [576, 192], P('shard')
- grad_value: float32 [576, 192], P('shard')
- grad_out: float32 [576, 576], P('shard')
- grad_gate: float32 [576, 1536], P('shard')
- grad_up: float32 [576, 1536], P('shard')
- grad_down: float32 [1536, 576], P('shard')
- grad_gain_attn: float32 [576], P('shard')
- grad_gain_mlp: float32 [576], P('shard')
The draws below stay inside these ranges and needn't reach their ends.
Inputs may be any that keep to these rules, and one draw needn't show every extreme that they name: `block_slot`: each row is an ordering of the 8 blocks of one sequence: entry r names the block stored at cycle position r. rope_pos of a row is 512 times its block plus its index in the block, plus one offset of 0 to 4095 for each sequence; one sequence has offset 0 and another offset 4095.
All inputs are finite; a program needn't handle non-finite values.
Results may differ from the reference program's by a relative error of at most 0.024.
Values may be sent and summed in bfloat16 or wider, within the bound.
No kernel may reach another device: no remote copies, remote signals or barrier semaphores. Data moves between devices by JAX's collectives and lax.ppermute only.
A program may use at most 128 MiB of HBM per device.

```python
import math
import jax
import jax.numpy as jnp
from jax import lax

D = 576
FF = 1536
HEADS = 9
KV_HEADS = 3
HEAD = 64
BLK = 512
L = 4096
SEQS = 8


def block_order(key):
    block_count = L // BLK
    seed_keys = jax.random.split(key, SEQS)
    return jax.vmap(lambda seed_key: jax.random.permutation(seed_key, block_count))(seed_keys).astype(jnp.int32)


def draw_block_slot(key, part):
    ordering = block_order(key)
    return ordering


def draw_rope_pos(key, part):
    ordering = block_order(key)
    key = jax.random.fold_in(key, 5)
    offset_key, low_key, step_key = jax.random.split(key, 3)
    offsets = jax.random.randint(offset_key, (SEQS, 1), 0, 4096, dtype=jnp.int32)
    lowest = jax.random.randint(low_key, (), 0, SEQS, dtype=jnp.int32)
    highest = (lowest + jax.random.randint(step_key, (), 1, SEQS, dtype=jnp.int32)) % SEQS
    rows = jnp.arange(SEQS, dtype=jnp.int32)[:, None]
    offsets = jnp.where(rows == lowest, 0, offsets)
    offsets = jnp.where(rows == highest, 4095, offsets)
    within = jnp.arange(BLK, dtype=jnp.int32)
    places = (ordering[:, :, None] * BLK + within[None, None, :]).reshape(SEQS, L)
    return (places + offsets).astype(jnp.int32)


def steps_of(key, extent, shards, smallest, top_value):
    level, own = 1.0, jax.random.fold_in(key, 6)
    for dim, shards_of in shards:
        steps = jnp.exp(jax.random.uniform(jax.random.fold_in(own, dim), (shards_of,), jnp.float32, smallest / len(shards), top_value / len(shards)))
        level = level * jnp.repeat(steps, extent[dim] // shards_of).reshape([-1 if axis == dim else 1 for axis in range(len(extent))])
    return level


def bell_draw(own_key, dims, scale, most, cuts=(), held_as=jnp.bfloat16):
    level = steps_of(own_key, dims, cuts, -0.22, 0.18) if cuts else 1.0
    result = jax.random.normal(own_key, dims, jnp.float32) * scale * level
    return jnp.minimum(jnp.maximum(result, -most), most).astype(held_as)


def setup_inputs(seed: int = 0) -> dict:
    arg_keys = jax.random.split(jax.random.key(seed), 14)
    return {
        "hidden_in": bell_draw(arg_keys[0], (SEQS, L, D), 1.0, 6.0, ((0, 4), (1, 8))),
        "out_grad": bell_draw(arg_keys[1], (SEQS, L, D), 1.0, 6.0, ((0, 4), (1, 8))),
        "block_slot": draw_block_slot(jax.random.fold_in(arg_keys[13], 71), 0),
        "rope_pos": draw_rope_pos(jax.random.fold_in(arg_keys[13], 71), 0),
        "w_query": bell_draw(arg_keys[4], (D, D), D ** -0.5, 0.25, ((0, 4),)),
        "w_key": bell_draw(arg_keys[5], (D, KV_HEADS * HEAD), D ** -0.5, 0.25, ((0, 4),)),
        "w_value": bell_draw(arg_keys[6], (D, KV_HEADS * HEAD), D ** -0.5, 0.25, ((0, 4),)),
        "w_out": bell_draw(arg_keys[7], (D, D), (D // 16) ** -0.5, 1.0, ((0, 4),)),
        "w_gate": bell_draw(arg_keys[8], (D, FF), D ** -0.5, 0.25, ((0, 4),)),
        "w_up": bell_draw(arg_keys[9], (D, FF), D ** -0.5, 0.25, ((0, 4),)),
        "w_down": bell_draw(arg_keys[10], (FF, D), FF ** -0.5, 0.15625, ((0, 4),)),
        "gain_attn": jnp.clip(1.0 + 0.1 * jax.random.normal(arg_keys[11], (D,), jnp.float32), 0.5, 1.5).astype(jnp.bfloat16),
        "gain_mlp": jnp.clip(1.0 + 0.1 * jax.random.normal(arg_keys[12], (D,), jnp.float32), 0.5, 1.5).astype(jnp.bfloat16),
    }


@jax.custom_vjp
def low(v):
    return lax.optimization_barrier(v.astype(jnp.bfloat16)).astype(jnp.float32)

@jax.custom_vjp
def low_back(v):
    return v

def low_keep(v):
    return (low(v), None)

def low_pass(kept, grad):
    return (grad,)

def back_keep(v):
    return (v, None)

def back_low(kept, grad):
    return (low(grad),)
low.defvjp(low_keep, low_pass)
low_back.defvjp(back_keep, back_low)
HIGHEST_PRECISION = lax.Precision.HIGHEST
NORM_EPSILON = 1e-05
ROPE_BASE = 100000.0
MASKED_SCORE = -1e+30

def matmul(left, right):
    return jnp.dot(left, right, precision=HIGHEST_PRECISION, preferred_element_type=jnp.float32)

def rms_scale(values, gain):
    inverse = lax.rsqrt(lax.optimization_barrier(jnp.mean(values * values, axis=-1, keepdims=True)) + NORM_EPSILON)
    return values * inverse * gain

def rotate(values, positions):
    half = values.shape[-1] // 2
    freqs = ROPE_BASE ** (-jnp.arange(half, dtype=jnp.float32) * 2.0 / values.shape[-1])
    angle = positions.astype(jnp.float32)[:, None] * freqs[None, :]
    cosine = jnp.cos(angle)[:, None, :]
    sine = jnp.sin(angle)[:, None, :]
    first = values[..., :half]
    second = values[..., half:]
    return jnp.concatenate([first * cosine - second * sine, second * cosine + first * sine], axis=-1)

def attend_block(queries, query_order, keys_rot, values_rot, key_order):
    scores = jnp.einsum('qgjd,kgd->gjqk', queries, keys_rot, precision=HIGHEST_PRECISION)
    scores = low_back(scores)
    allowed = key_order[None, :] <= query_order[:, None]
    scores = jnp.where(allowed[None, None], scores, MASKED_SCORE)
    row_max = lax.optimization_barrier(jnp.max(scores, axis=-1, keepdims=True))
    weights = jnp.exp(scores - row_max)
    probs = low(weights / lax.optimization_barrier(jnp.sum(weights, axis=-1, keepdims=True)))
    return jnp.einsum('gjqk,kgd->qgjd', probs, values_rot, precision=HIGHEST_PRECISION)

def layer(inputs, params, order, positions):
    w_query, w_key, w_value, w_out, w_gate, w_up, w_down, gain_attn, gain_mlp = params
    group = HEADS // KV_HEADS
    normed = low(rms_scale(inputs, gain_attn))
    query_lin = low_back(matmul(normed, w_query)).reshape(L, HEADS, HEAD)
    key_lin = low_back(matmul(normed, w_key)).reshape(L, KV_HEADS, HEAD)
    values_rot = low(low_back(matmul(normed, w_value))).reshape(L, KV_HEADS, HEAD)
    queries = low(rotate(query_lin, positions) * 0.125)
    keys_rot = low(rotate(key_lin, positions))
    block_rows = math.gcd(L, 512)
    pieces = (queries.reshape(L // block_rows, block_rows, KV_HEADS, group, HEAD), order.reshape(L // block_rows, block_rows))
    attend = jax.checkpoint(attend_block)
    mixed = lax.map(lambda piece: attend(piece[0], piece[1], keys_rot, values_rot, order), pieces)
    mixed = low(low_back(mixed.reshape(L, D)))
    middle = inputs + low_back(matmul(mixed, w_out))
    normed_mlp = low(rms_scale(middle, gain_mlp))
    gate = low_back(matmul(normed_mlp, w_gate))
    upward = low_back(matmul(normed_mlp, w_up))
    hidden = low(jax.nn.silu(gate) * upward)
    return middle + low_back(matmul(hidden, w_down))

def reference(hidden_in, out_grad, block_slot, rope_pos, w_query, w_key, w_value, w_out, w_gate, w_up, w_down, gain_attn, gain_mlp):
    params = tuple((weight.astype(jnp.float32) for weight in (w_query, w_key, w_value, w_out, w_gate, w_up, w_down, gain_attn, gain_mlp)))
    within = jnp.arange(L, dtype=jnp.int32) % BLK

    def per_sequence(totals, sequence):
        rows_in, cot_rows, slots, positions = sequence
        order = jnp.repeat(slots, BLK, total_repeat_length=L).astype(jnp.int32) * BLK + within
        outputs, pullback = jax.vjp(lambda rows, weights: layer(rows, weights, order, positions), rows_in.astype(jnp.float32), params)
        row_grad, weight_grads = pullback(cot_rows.astype(jnp.float32))
        totals = tuple((total + grad for total, grad in zip(totals, weight_grads)))
        return (totals, (outputs.astype(jnp.bfloat16), row_grad.astype(jnp.bfloat16)))
    zeros = tuple((jnp.zeros_like(weight) for weight in params))
    grads, (outputs, row_grads) = lax.scan(per_sequence, zeros, (hidden_in, out_grad, block_slot, rope_pos))
    return (outputs, row_grads, grads[0], grads[1], grads[2], grads[3], grads[4], grads[5], grads[6], grads[7], grads[8])
```

```python
import functools

import jax
import jax.numpy as jnp
from jax import lax
from jax.experimental import pallas as pl
from jax.experimental.pallas import tpu as pltpu
from jax.sharding import PartitionSpec as P

HEADS = 9
KV_HEADS = 3
HEAD = 64
GROUP = HEADS // KV_HEADS
PAIR = 2 * HEAD
HALF = HEAD // 2

NORM_EPSILON = 1e-05
ROPE_BASE = 100000.0
MASKED_SCORE = -1e30
VMEM_BYTES = 56 * 1024 * 1024

F32 = jnp.float32
BF16 = jnp.bfloat16


def params():
    return pltpu.CompilerParams(vmem_limit_bytes=VMEM_BYTES)


def matmul(left, right):
    return jnp.dot(left, right, preferred_element_type=F32)


def matmul_lead(left, right):
    return lax.dot_general(left, right, (((0,), (0,)), ((), ())), preferred_element_type=F32)


def matmul_trail(left, right):
    return lax.dot_general(left, right, (((1,), (1,)), ((), ())), preferred_element_type=F32)


def rms_forward(rows, gain):
    inverse = lax.rsqrt(jnp.mean(rows * rows, axis=-1, keepdims=True) + NORM_EPSILON)
    return (rows * inverse * gain, inverse)


def rms_backward(rows, inverse, gain, grad):
    scaled = grad * gain
    row_grad = inverse * scaled - rows * inverse**3 * jnp.mean(
        scaled * rows, axis=-1, keepdims=True
    )
    gain_grad = jnp.sum(grad * rows * inverse, axis=0)
    return (row_grad, gain_grad)


def flip(value, axis, bit):
    peers = lax.axis_size(axis)
    return lax.ppermute(value, axis, [(i, i ^ bit) for i in range(peers)])


def shift(value, axis):
    peers = lax.axis_size(axis)
    return lax.ppermute(value, axis, [(i, (i + 1) % peers) for i in range(peers)])


def ring_pieces(piece, axis):
    pieces = [piece]
    for _ in range(lax.axis_size(axis) - 1):
        pieces.append(shift(pieces[-1], axis))
    return pieces


def gather_flipped(own):
    peers = lax.axis_size("ctx")
    if peers == 8:
        half = own.shape[0] // 2
        by_x = flip(own, "ctx", 2)
        by_y = flip(own, "ctx", 4)
        first = flip(by_y[:half], "ctx", 2)
        second = flip(by_x[half:], "ctx", 4)
        diagonal = jnp.concatenate([first, second], axis=0)
        same_core = [own, by_x, by_y, diagonal]
        other_core = [flip(a, "ctx", 1) for a in same_core]
        return [b for pair in zip(same_core, other_core) for b in pair]
    blocks = [own]
    bit = 1
    while bit < peers:
        blocks = blocks + [flip(b, "ctx", bit) for b in blocks]
        bit *= 2
    return blocks


def add_sent(kept, arrived):
    return (kept.astype(F32) + arrived.astype(F32)).astype(BF16)


def scatter_flipped(parts):
    peers = len(parts)
    if peers == 8:
        half = parts[0].shape[0] // 2
        sums = [add_sent(parts[k], flip(parts[k + 1], "ctx", 1)) for k in (0, 2, 4, 6)]
        own, by_x, by_y, diagonal = sums
        first = flip(diagonal[:half], "ctx", 2)
        second = flip(diagonal[half:], "ctx", 4)
        by_y = jnp.concatenate([add_sent(by_y[:half], first), by_y[half:]], axis=0)
        by_x = jnp.concatenate([by_x[:half], add_sent(by_x[half:], second)], axis=0)
        from_x = flip(by_x, "ctx", 2).astype(F32)
        from_y = flip(by_y, "ctx", 4).astype(F32)
        return own.astype(F32) + from_x + from_y
    while peers > 1:
        peers //= 2
        parts = [add_sent(parts[k], flip(parts[k + peers], "ctx", peers)) for k in range(peers)]
    return parts[0].astype(F32)


def entry_kernel(shards, width, place_ref, *refs):
    piece_refs = refs[: 2 * shards]
    (x_ref, cos_t_ref, sin_t_ref, cos_ref, low_ref, high_ref) = refs[2 * shards : 2 * shards + 6]
    q_ref, kv_ref, normed_ref, packed_ref, gains_ref = refs[2 * shards + 6 : 2 * shards + 11]
    (weight,) = refs[2 * shards + 11 :]
    depth = piece_refs[0].shape[0]
    cols = piece_refs[0].shape[1]

    @pl.when(pl.program_id(0) == 0)
    def assemble():
        shard, side = place_ref[0], place_ref[1]
        for t in range(shards):
            row = pl.multiple_of(lax.rem(shard - t + shards, shards) * depth, 16)
            mine = pl.multiple_of(side * cols, 128)
            other = pl.multiple_of((1 - side) * cols, 128)
            weight[pl.ds(row, depth), pl.ds(mine, cols)] = piece_refs[t][...]
            weight[pl.ds(row, depth), pl.ds(other, cols)] = piece_refs[shards + t][...]
        packed_ref[...] = weight[...]
        gains_ref[...] = weight[:, 512:640].astype(F32).T[64:72, :]

    rows = x_ref[...].astype(F32)
    inverse = lax.rsqrt(jnp.mean(rows * rows, axis=-1, keepdims=True) + NORM_EPSILON)
    normed = (rows * inverse * gains_ref[0:1, :]).astype(BF16)
    normed_ref[...] = normed
    cos_t = cos_t_ref[...]
    sin_t = sin_t_ref[...]
    for chunk in range(5):
        lin = matmul(normed, weight[:, chunk * PAIR : (chunk + 1) * PAIR]).T
        for part in range(2):
            head = 2 * chunk + part
            if head < HEADS:
                first = lin[part * HEAD : part * HEAD + HALF]
                second = lin[part * HEAD + HALF : (part + 1) * HEAD]
                q_ref[head * HEAD : head * HEAD + HALF, :] = (
                    (first * cos_t - second * sin_t) * 0.125
                ).astype(BF16)
                q_ref[head * HEAD + HALF : (head + 1) * HEAD, :] = (
                    (second * cos_t + first * sin_t) * 0.125
                ).astype(BF16)
    for group in range(KV_HEADS):
        at = 5 * PAIR + group * PAIR
        lin = matmul(normed, weight[:, at : at + PAIR])
        turned = (
            lin * cos_ref[...]
            + pltpu.roll(lin, HALF, 1) * low_ref[...]
            + pltpu.roll(lin, PAIR - HALF, 1) * high_ref[...]
        )
        kv_ref[group] = turned.astype(BF16)


def entry(place, pieces, inputs, tables, block_len):
    shards = len(pieces) // 2
    rows, width = inputs.shape
    cos_t, sin_t, cos, low, high = tables
    depth, cols = pieces[0].shape
    steps = rows // block_len
    fixed = lambda shape: pl.BlockSpec(shape, lambda s, place: (0,) * len(shape))
    return pl.pallas_call(
        functools.partial(entry_kernel, shards, width),
        grid_spec=pltpu.PrefetchScalarGridSpec(
            num_scalar_prefetch=1,
            grid=(steps,),
            in_specs=[fixed((depth, cols)) for _ in pieces]
            + [pl.BlockSpec((block_len, width), lambda s, place: (s, 0))]
            + [pl.BlockSpec((HALF, block_len), lambda s, place: (0, s))] * 2
            + [pl.BlockSpec((block_len, PAIR), lambda s, place: (s, 0))] * 3,
            out_specs=[
                pl.BlockSpec((HEADS * HEAD, block_len), lambda s, place: (0, s)),
                pl.BlockSpec((KV_HEADS, block_len, PAIR), lambda s, place: (0, s, 0)),
                pl.BlockSpec((block_len, width), lambda s, place: (s, 0)),
                fixed((width, 2 * cols)),
                fixed((8, width)),
            ],
            scratch_shapes=[pltpu.VMEM((width, 2 * cols), BF16)],
        ),
        out_shape=[
            jax.ShapeDtypeStruct((HEADS * HEAD, rows), BF16),
            jax.ShapeDtypeStruct((KV_HEADS, rows, PAIR), BF16),
            jax.ShapeDtypeStruct((rows, width), BF16),
            jax.ShapeDtypeStruct((width, 2 * cols), BF16),
            jax.ShapeDtypeStruct((8, width), F32),
        ],
        compiler_params=params(),
        name="entry",
    )(place, *pieces, inputs, cos_t, sin_t, cos, low, high)


def key_mask(length):
    keys = lax.broadcasted_iota(jnp.int32, (length, length), 0)
    queries = lax.broadcasted_iota(jnp.int32, (length, length), 1)
    return keys <= queries


def forward_kernel(peers, info_ref, q_ref, *refs):
    kv_refs = refs[:peers]
    out_ref, out16_ref, lse_ref = refs[peers : peers + 3]
    blocks, queries, row_max, row_sum, total = refs[peers + 3 :]
    seq = pl.program_id(0)
    length = q_ref.shape[1]
    for k in range(peers):
        blocks[k] = kv_refs[k][...]
    for h in range(GROUP):
        queries[h, :HEAD, :] = q_ref[h * HEAD : (h + 1) * HEAD, :]
        queries[h, HEAD:, :] = jnp.zeros((HEAD, length), BF16)

    def visit(k, first):
        kv = blocks[k]
        values_t = kv.T[HEAD:]
        for h in range(GROUP):
            scores = matmul(kv, queries[h])
            if first:
                scores = jnp.where(key_mask(length), scores, MASKED_SCORE)
                new_max = jnp.max(scores, axis=0, keepdims=True)
                weights = jnp.exp(scores - new_max)
                row_max[h] = new_max
                row_sum[h] = jnp.sum(weights, axis=0, keepdims=True)
                total[h] = matmul(values_t, weights.astype(BF16))
            else:
                old_max = row_max[h]
                new_max = jnp.maximum(old_max, jnp.max(scores, axis=0, keepdims=True))
                weights = jnp.exp(scores - new_max)
                fading = jnp.exp(old_max - new_max)
                row_max[h] = new_max
                row_sum[h] = row_sum[h] * fading + jnp.sum(weights, axis=0, keepdims=True)
                total[h] = total[h] * fading + matmul(values_t, weights.astype(BF16))

    visit(0, True)

    @pl.loop(0, info_ref[seq, peers])
    def _(r):
        visit(info_ref[seq, r], False)

    for h in range(GROUP):
        result = total[h] / row_sum[h]
        out_ref[h * HEAD : (h + 1) * HEAD, :] = result
        out16_ref[h * HEAD : (h + 1) * HEAD, :] = result.astype(BF16)
        lse_ref[h : h + 1, :] = row_max[h] + jnp.log(row_sum[h])


def attend(info, q_t, blocks, block_len):
    peers = len(blocks)
    rows = q_t.shape[1]
    steps = rows // block_len
    across = lambda height: pl.BlockSpec((height, block_len), lambda s, info: (0, s))
    return pl.pallas_call(
        functools.partial(forward_kernel, peers),
        grid_spec=pltpu.PrefetchScalarGridSpec(
            num_scalar_prefetch=1,
            grid=(steps,),
            in_specs=[across(GROUP * HEAD)]
            + [pl.BlockSpec((block_len, PAIR), lambda s, info: (s, 0))] * peers,
            out_specs=[across(GROUP * HEAD), across(GROUP * HEAD), across(8)],
            scratch_shapes=[
                pltpu.VMEM((peers, block_len, PAIR), BF16),
                pltpu.VMEM((GROUP, PAIR, block_len), BF16),
                pltpu.VMEM((GROUP, 1, block_len), F32),
                pltpu.VMEM((GROUP, 1, block_len), F32),
                pltpu.VMEM((GROUP, HEAD, block_len), F32),
            ],
        ),
        out_shape=[
            jax.ShapeDtypeStruct((GROUP * HEAD, rows), F32),
            jax.ShapeDtypeStruct((GROUP * HEAD, rows), BF16),
            jax.ShapeDtypeStruct((8, rows), F32),
        ],
        compiler_params=params(),
        name="attend",
    )(info, q_t, *blocks)


def backward_kernel(peers, info_ref, q_ref, dout_ref, out_ref, lse_ref, cos_ref, sin_ref, *refs):
    kv_refs = refs[:peers]
    dq_ref = refs[peers]
    dkv_refs = refs[peers + 1 : 2 * peers + 1]
    blocks, grads, queries, douts, q_rows, dout_rows, delta, dq = refs[2 * peers + 1 :]
    seq = pl.program_id(0)
    length = q_ref.shape[1]
    for k in range(peers):
        blocks[k] = kv_refs[k][...]
        grads[k] = jnp.zeros((length, PAIR), BF16)
    for h in range(GROUP):
        head = slice(h * HEAD, (h + 1) * HEAD)
        zeros = jnp.zeros((HEAD, length), BF16)
        dout = dout_ref[head, :]
        queries[h, :HEAD, :] = q_ref[head, :]
        queries[h, HEAD:, :] = zeros
        douts[h, :HEAD, :] = zeros
        douts[h, HEAD:, :] = dout
        q_rows[h] = queries[h].T
        dout_rows[h] = douts[h].T
        delta[h] = jnp.sum(dout.astype(F32) * out_ref[head, :], axis=0, keepdims=True)
        dq[h] = jnp.zeros((HEAD, length), F32)

    def visit(k, masked):
        kv = blocks[k]
        keys_t = kv.T[:HEAD]
        dkv = jnp.zeros((length, PAIR), F32)
        for h in range(GROUP):
            probs = jnp.exp(matmul(kv, queries[h]) - lse_ref[h : h + 1, :])
            if masked:
                probs = jnp.where(key_mask(length), probs, 0.0)
            dscores = (probs * (matmul(kv, douts[h]) - delta[h])).astype(BF16)
            dkv = dkv + matmul(probs.astype(BF16), dout_rows[h]) + matmul(dscores, q_rows[h])
            dq[h] = dq[h] + matmul(keys_t, dscores)
        grads[k] = dkv.astype(BF16)

    visit(0, True)

    @pl.loop(0, info_ref[seq, peers])
    def _(r):
        visit(info_ref[seq, r], False)

    cos, sin = cos_ref[...], sin_ref[...]
    for h in range(GROUP):
        first = dq[h, :HALF, :] * 0.125
        second = dq[h, HALF:, :] * 0.125
        dq_ref[h * HEAD : h * HEAD + HALF, :] = (first * cos + second * sin).astype(BF16)
        dq_ref[h * HEAD + HALF : (h + 1) * HEAD, :] = (second * cos - first * sin).astype(BF16)
    for k in range(peers):
        dkv_refs[k][...] = grads[k]


def attend_back(info, q_t, dout_t, out_t, lse, tables, blocks, block_len):
    peers = len(blocks)
    rows = q_t.shape[1]
    steps = rows // block_len
    across = lambda height: pl.BlockSpec((height, block_len), lambda s, info: (0, s))
    down = pl.BlockSpec((block_len, PAIR), lambda s, info: (s, 0))
    pair_t = pltpu.VMEM((GROUP, PAIR, block_len), BF16)
    pair_rows = pltpu.VMEM((GROUP, block_len, PAIR), BF16)
    return pl.pallas_call(
        functools.partial(backward_kernel, peers),
        grid_spec=pltpu.PrefetchScalarGridSpec(
            num_scalar_prefetch=1,
            grid=(steps,),
            in_specs=[across(GROUP * HEAD)] * 3 + [across(8)] + [across(HALF)] * 2 + [down] * peers,
            out_specs=[across(GROUP * HEAD)] + [down] * peers,
            scratch_shapes=[
                pltpu.VMEM((peers, block_len, PAIR), BF16),
                pltpu.VMEM((peers, block_len, PAIR), BF16),
                pair_t,
                pair_t,
                pair_rows,
                pair_rows,
                pltpu.VMEM((GROUP, 1, block_len), F32),
                pltpu.VMEM((GROUP, HEAD, block_len), F32),
            ],
        ),
        out_shape=[jax.ShapeDtypeStruct((GROUP * HEAD, rows), BF16)]
        + [jax.ShapeDtypeStruct((rows, PAIR), BF16)] * peers,
        compiler_params=params(),
        name="attend_back",
    )(info, q_t, dout_t, out_t, lse, *tables, *blocks)


def pack_kv(key_part, value_part):
    depth = key_part.shape[0]
    both = jnp.stack(
        [key_part.reshape(depth, KV_HEADS, HEAD), value_part.reshape(depth, KV_HEADS, HEAD)], axis=2
    )
    return both.reshape(depth, KV_HEADS * PAIR)


def unpack_kv(packed):
    depth = packed.shape[0]
    both = packed.reshape(depth, KV_HEADS, 2, HEAD)
    return (
        both[:, :, 0].reshape(depth, KV_HEADS * HEAD),
        both[:, :, 1].reshape(depth, KV_HEADS * HEAD),
    )


def rope_tables(positions):
    freqs = ROPE_BASE ** (-jnp.arange(HALF, dtype=F32) * 2.0 / HEAD)
    angle = positions.reshape(-1).astype(F32)[:, None] * freqs
    cos, sin = jnp.cos(angle), jnp.sin(angle)
    nothing = jnp.zeros_like(cos)
    ones = jnp.ones_like(cos)
    return (
        cos.T,
        sin.T,
        jnp.concatenate([cos, cos, ones, ones], axis=1),
        jnp.concatenate([nothing, sin, nothing, nothing], axis=1),
        jnp.concatenate([-sin, nothing, nothing, nothing], axis=1),
    )


def per_device(
    hidden_in,
    out_grad,
    block_slot,
    rope_pos,
    w_query,
    w_key,
    w_value,
    w_out,
    w_gate,
    w_up,
    w_down,
    gain_attn,
    gain_mlp,
):
    seq_count, block_len, width = hidden_in.shape
    row_count = seq_count * block_len
    hidden_width = w_gate.shape[1]
    depth = w_query.shape[0]
    cycle_index = lax.axis_index("ctx")
    cycle_size = lax.axis_size("ctx")
    shard_index = lax.axis_index("shard")
    shards = lax.axis_size("shard")
    side = cycle_index % 2

    def whole(parts):
        rows = parts[0].shape[0]
        out = jnp.zeros((shards * rows,) + parts[0].shape[1:], parts[0].dtype)
        for t, part in enumerate(parts):
            out = lax.dynamic_update_slice_in_dim(out, part, ((shard_index - t) % shards) * rows, 0)
        return out

    packed = jnp.concatenate(
        [
            w_query,
            gain_attn[:, None],
            gain_mlp[:, None],
            jnp.zeros((depth, HEAD - 2), BF16),
            pack_kv(w_key, w_value),
        ],
        axis=1,
    )
    cols = packed.shape[1] // 2
    mine = ring_pieces(lax.dynamic_slice_in_dim(packed, side * cols, cols, 1), "shard")
    pieces = mine + [flip(a, "ctx", 1) for a in mine]
    place = jnp.stack([shard_index, side]).astype(jnp.int32)
    if depth % 16:
        pieces = [whole(pieces[:shards]), whole(pieces[shards:])]
        place = jnp.stack([jnp.zeros_like(side), side]).astype(jnp.int32)

    down_half = w_down.shape[0] // 2
    gate_or_up = ring_pieces(jnp.where(side == 0, w_gate, w_up), "shard")
    down_part = ring_pieces(
        lax.dynamic_slice_in_dim(w_down, side * down_half, down_half, 0), "shard"
    )
    out_part = ring_pieces(w_out, "shard")

    tables = rope_tables(rope_pos)
    cycle = jnp.arange(cycle_size, dtype=jnp.int32)
    at_slot = jnp.sum(
        jnp.where(block_slot[:, :, None] == cycle[None, None, :], (cycle ^ cycle_index)[None, :, None], 0),
        axis=1,
    )
    own_slot = lax.dynamic_index_in_dim(block_slot, cycle_index, 1, keepdims=True)
    info = jnp.concatenate([at_slot, own_slot], axis=1).astype(jnp.int32)

    flat_in = hidden_in.reshape(row_count, width)
    q_t, kv, normed_attn, full_packed, gains = entry(place, pieces, flat_in, tables, block_len)
    gain_one, gain_two = gains[0], gains[1]

    blocks = [gather_flipped(kv[g]) for g in range(KV_HEADS)]
    size = GROUP * HEAD
    attended = [
        attend(info, q_t[g * size : (g + 1) * size], blocks[g], block_len) for g in range(KV_HEADS)
    ]
    mixed_t = jnp.concatenate([a[1] for a in attended], axis=0)

    own_side = whole(gate_or_up)
    other_side = flip(own_side, "ctx", 1)
    full_gate = jnp.where(side == 0, own_side, other_side)
    full_up = jnp.where(side == 0, other_side, own_side)
    own_down = whole(down_part).reshape(shards, down_half, width)
    other_down = flip(own_down, "ctx", 1)
    full_down = jnp.where(
        side == 0,
        jnp.stack([own_down, other_down], axis=1),
        jnp.stack([other_down, own_down], axis=1),
    ).reshape(shards * 2 * down_half, width)
    full_out = whole(out_part)

    inputs = flat_in.astype(F32)
    middle = inputs + matmul_lead(mixed_t, full_out)
    normed_mlp, inverse_mlp = rms_forward(middle, gain_two)
    normed_mlp = normed_mlp.astype(BF16)
    gate = matmul(normed_mlp, full_gate)
    upward = matmul(normed_mlp, full_up)
    sigmoid_gate = jax.nn.sigmoid(gate)
    hidden = (gate * sigmoid_gate * upward).astype(BF16)
    block_out = (middle + matmul(hidden, full_down)).astype(BF16).reshape(hidden_in.shape)
    down_in = out_grad.reshape(row_count, width)
    grad_down = matmul_lead(hidden, down_in)
    hidden_grad = matmul_trail(down_in, full_down)
    gate_grad = (hidden_grad * upward * sigmoid_gate * (1.0 + gate * (1.0 - sigmoid_gate))).astype(
        BF16
    )
    up_grad = (hidden_grad * gate * sigmoid_gate).astype(BF16)
    grad_gate = matmul_lead(normed_mlp, gate_grad)
    grad_up = matmul_lead(normed_mlp, up_grad)
    normed_grad = matmul_trail(gate_grad, full_gate) + matmul_trail(up_grad, full_up)
    rows_back, grad_gain_mlp = rms_backward(middle, inverse_mlp, gain_two, normed_grad)
    middle_grad = down_in.astype(F32) + rows_back
    branch_grad = middle_grad.astype(BF16)
    grad_out = matmul(mixed_t, branch_grad)
    dout_t = matmul_trail(full_out, branch_grad).astype(BF16)

    ff_part = hidden_width // shards
    early = jnp.concatenate(
        [
            grad_gate.astype(BF16).reshape(shards, depth, hidden_width),
            grad_up.astype(BF16).reshape(shards, depth, hidden_width),
        ],
        axis=1,
    )
    early_narrow = jnp.concatenate(
        [
            grad_down.astype(BF16).reshape(shards, ff_part, width),
            grad_out.astype(BF16).reshape(shards, depth, width),
        ],
        axis=1,
    )
    early = lax.psum_scatter(early, "shard", scatter_dimension=0, tiled=False)
    early_narrow = lax.psum_scatter(early_narrow, "shard", scatter_dimension=0, tiled=False)
    early, early_narrow = lax.psum((early, early_narrow), "ctx")

    dq_parts = []
    dkv_parts = []
    for g in range(KV_HEADS):
        rows = slice(g * size, (g + 1) * size)
        result = attend_back(
            info,
            q_t[rows],
            dout_t[rows],
            attended[g][0],
            attended[g][2],
            tables[:2],
            blocks[g],
            block_len,
        )
        dq_parts.append(result[0])
        dkv = scatter_flipped(list(result[1:]))
        turned = (
            dkv * tables[2]
            - jnp.roll(dkv, HALF, 1) * tables[3]
            - jnp.roll(dkv, -HALF, 1) * tables[4]
        )
        dkv_parts.append(turned.astype(BF16))
    dq_t = jnp.concatenate(dq_parts, axis=0)
    dkv = jnp.concatenate(dkv_parts, axis=1)
    kv_at = full_packed.shape[1] - KV_HEADS * PAIR
    grad_query = lax.dot_general(
        normed_attn, dq_t, (((0,), (1,)), ((), ())), preferred_element_type=F32
    )
    grad_kv = matmul_lead(normed_attn, dkv)
    attn_grad = lax.dot_general(
        dq_t, full_packed[:, : HEADS * HEAD], (((0,), (1,)), ((), ())), preferred_element_type=F32
    ) + matmul_trail(dkv, full_packed[:, kv_at:])
    inverse_attn = lax.rsqrt(jnp.mean(inputs * inputs, axis=-1, keepdims=True) + NORM_EPSILON)
    rows_first, grad_gain_attn = rms_backward(inputs, inverse_attn, gain_one, attn_grad)
    in_grad = (middle_grad + rows_first).astype(BF16).reshape(hidden_in.shape)

    late = jnp.concatenate(
        [
            grad_query.astype(BF16),
            grad_gain_attn.astype(BF16)[:, None],
            grad_gain_mlp.astype(BF16)[:, None],
            jnp.zeros((width, HEAD - 2), BF16),
            grad_kv.astype(BF16),
        ],
        axis=1,
    )
    late = lax.psum_scatter(late, "shard", scatter_dimension=0, tiled=True)
    late = lax.psum(late, "ctx").astype(F32)
    grad_key, grad_value = unpack_kv(late[:, kv_at:])
    early = early.astype(F32)
    early_narrow = early_narrow.astype(F32)
    return (
        block_out,
        in_grad,
        late[:, : HEADS * HEAD],
        grad_key,
        grad_value,
        early_narrow[ff_part:],
        early[:depth],
        early[depth:],
        early_narrow[:ff_part],
        late[:, HEADS * HEAD],
        late[:, HEADS * HEAD + 1],
    )


def solution(mesh):
    rows = P("shard", "ctx", None)
    split = P("shard", None)
    return jax.shard_map(
        per_device,
        mesh=mesh,
        in_specs=(rows, rows, split, P("shard", "ctx")) + (split,) * 7 + (P("shard"),) * 2,
        out_specs=(rows, rows) + (split,) * 7 + (P("shard"),) * 2,
        check_vma=False,
    )
```

```python
import functools

import jax
import jax.numpy as jnp
from jax import lax
from jax.experimental import pallas as pl
from jax.experimental.pallas import tpu as pltpu
from jax.sharding import Mesh
from jax.sharding import PartitionSpec as P

HEADS = 9
KV_HEADS = 3
HEAD = 64
GROUP = HEADS // KV_HEADS
PAIR = 2 * HEAD
HALF = HEAD // 2

NORM_EPSILON = 1e-05
ROPE_BASE = 100000.0
MASKED_SCORE = -1e30
VMEM_BYTES = 56 * 1024 * 1024

CHIPS = ("cy", "cx")
CTX = CHIPS + ("core",)

F32 = jnp.float32
BF16 = jnp.bfloat16


def params():
    return pltpu.CompilerParams(vmem_limit_bytes=VMEM_BYTES)


def matmul(left, right):
    return jnp.dot(left, right, preferred_element_type=F32)


def matmul_lead(left, right):
    return lax.dot_general(left, right, (((0,), (0,)), ((), ())), preferred_element_type=F32)


def matmul_trail(left, right):
    return lax.dot_general(left, right, (((1,), (1,)), ((), ())), preferred_element_type=F32)


def rms_forward(rows, gain):
    inverse = lax.rsqrt(jnp.mean(rows * rows, axis=-1, keepdims=True) + NORM_EPSILON)
    return (rows * inverse * gain, inverse)


def rms_backward(rows, inverse, gain, grad):
    scaled = grad * gain
    row_grad = inverse * scaled - rows * inverse**3 * jnp.mean(
        scaled * rows, axis=-1, keepdims=True
    )
    gain_grad = jnp.sum(grad * rows * inverse, axis=0)
    return (row_grad, gain_grad)


def flip(value, bit):
    peers = lax.axis_size(CTX)
    return lax.ppermute(value, CTX, [(i, i ^ bit) for i in range(peers)])


def shift(value, axis, by=1):
    peers = lax.axis_size(axis)
    return lax.ppermute(value, axis, [(i, (i + by) % peers) for i in range(peers)])


def ring_pieces(piece, axis):
    pieces = [piece]
    for _ in range(lax.axis_size(axis) - 1):
        pieces.append(shift(pieces[-1], axis))
    return pieces


def after(value, *others):
    return lax.optimization_barrier((value,) + others)[0]


def gather_flipped(own):
    peers = lax.axis_size(CTX)
    if peers == 8:
        by_x = flip(own, 2)
        by_y = flip(own, 4)
        first = flip(by_y[:1], 2)
        second = flip(by_x[1:], 4)
        diagonal = jnp.concatenate([first, second], axis=0)
        same_core = [own, by_x, by_y, diagonal]
        other_core = [flip(a, 1) for a in same_core]
        return [b for pair in zip(same_core, other_core) for b in pair]
    blocks = [own]
    bit = 1
    while bit < peers:
        blocks = blocks + [flip(b, bit) for b in blocks]
        bit *= 2
    return blocks


def add_sent(kept, arrived):
    return (kept.astype(F32) + arrived.astype(F32)).astype(BF16)


def scatter_flipped(parts):
    peers = len(parts)
    if peers == 8:
        own, by_x, by_y, diagonal = [
            add_sent(parts[k], flip(parts[k + 1], 1)) for k in (6, 4, 2, 0)
        ][::-1]
        first = flip(diagonal[:1], 2)
        second = flip(diagonal[1:], 4)
        by_y = jnp.concatenate([add_sent(by_y[:1], first), by_y[1:]], axis=0)
        by_x = jnp.concatenate([by_x[:1], add_sent(by_x[1:], second)], axis=0)
        from_x = flip(by_x, 2).astype(F32)
        from_y = flip(by_y, 4).astype(F32)
        return own.astype(F32) + from_x + from_y
    while peers > 1:
        peers //= 2
        parts = [add_sent(parts[k], flip(parts[k + peers], peers)) for k in range(peers)]
    return parts[0].astype(F32)


def entry_kernel(shards, width, place_ref, *refs):
    piece_refs = refs[: 2 * shards]
    (x_ref, cos_t_ref, sin_t_ref, cos_ref, low_ref, high_ref) = refs[2 * shards : 2 * shards + 6]
    kept_ref, sent_ref, kv_ref, normed_ref, packed_ref, gains_ref = refs[
        2 * shards + 6 : 2 * shards + 12
    ]
    (weight,) = refs[2 * shards + 12 :]
    half = kept_ref.shape[1]
    depth = piece_refs[0].shape[0]
    cols = piece_refs[0].shape[1]

    @pl.when(pl.program_id(0) == 0)
    def assemble():
        shard, side = place_ref[0], place_ref[1]
        for t in range(shards):
            row = pl.multiple_of(lax.rem(shard - t + shards, shards) * depth, 16)
            mine = pl.multiple_of(side * cols, 128)
            other = pl.multiple_of((1 - side) * cols, 128)
            weight[pl.ds(row, depth), pl.ds(mine, cols)] = piece_refs[t][...]
            weight[pl.ds(row, depth), pl.ds(other, cols)] = piece_refs[shards + t][...]
        packed_ref[...] = weight[...]
        gains_ref[...] = weight[:, 512:640].astype(F32).T[64:72, :]

    rows = x_ref[...].astype(F32)
    inverse = lax.rsqrt(jnp.mean(rows * rows, axis=-1, keepdims=True) + NORM_EPSILON)
    normed = (rows * inverse * gains_ref[0:1, :]).astype(BF16)
    normed_ref[...] = normed
    cos_t = cos_t_ref[...]
    sin_t = sin_t_ref[...]
    for chunk in range(5):
        lin = matmul(normed, weight[:, chunk * PAIR : (chunk + 1) * PAIR]).T
        for part in range(2):
            head = 2 * chunk + part
            if head < HEADS:
                first = lin[part * HEAD : part * HEAD + HALF]
                second = lin[part * HEAD + HALF : (part + 1) * HEAD]
                turned = jnp.concatenate(
                    [first * cos_t - second * sin_t, second * cos_t + first * sin_t], axis=0
                )
                turned = (turned * 0.125).astype(BF16)
                kept_ref[head * HEAD : (head + 1) * HEAD, :] = turned[:, :half]
                sent_ref[head * HEAD : (head + 1) * HEAD, :] = turned[:, half:]
    for group in range(KV_HEADS):
        at = 5 * PAIR + group * PAIR
        lin = matmul(normed, weight[:, at : at + PAIR])
        turned = (
            lin * cos_ref[...]
            + pltpu.roll(lin, HALF, 1) * low_ref[...]
            + pltpu.roll(lin, PAIR - HALF, 1) * high_ref[...]
        )
        kv_ref[0, group] = turned.astype(BF16)


def entry(place, pieces, inputs, tables, block_len):
    shards = len(pieces) // 2
    rows, width = inputs.shape
    cos_t, sin_t, cos, low, high = tables
    depth, cols = pieces[0].shape
    steps = rows // block_len
    fixed = lambda shape: pl.BlockSpec(shape, lambda s, place: (0,) * len(shape))
    return pl.pallas_call(
        functools.partial(entry_kernel, shards, width),
        grid_spec=pltpu.PrefetchScalarGridSpec(
            num_scalar_prefetch=1,
            grid=(steps,),
            in_specs=[fixed((depth, cols)) for _ in pieces]
            + [pl.BlockSpec((block_len, width), lambda s, place: (s, 0))]
            + [pl.BlockSpec((HALF, block_len), lambda s, place: (0, s))] * 2
            + [pl.BlockSpec((block_len, PAIR), lambda s, place: (s, 0))] * 3,
            out_specs=[
                pl.BlockSpec((HEADS * HEAD, block_len // 2), lambda s, place: (0, s)),
                pl.BlockSpec((HEADS * HEAD, block_len // 2), lambda s, place: (0, s)),
                pl.BlockSpec((1, KV_HEADS, block_len, PAIR), lambda s, place: (s, 0, 0, 0)),
                pl.BlockSpec((block_len, width), lambda s, place: (s, 0)),
                fixed((width, 2 * cols)),
                fixed((8, width)),
            ],
            scratch_shapes=[pltpu.VMEM((width, 2 * cols), BF16)],
        ),
        out_shape=[
            jax.ShapeDtypeStruct((HEADS * HEAD, rows // 2), BF16),
            jax.ShapeDtypeStruct((HEADS * HEAD, rows // 2), BF16),
            jax.ShapeDtypeStruct((steps, KV_HEADS, block_len, PAIR), BF16),
            jax.ShapeDtypeStruct((rows, width), BF16),
            jax.ShapeDtypeStruct((width, 2 * cols), BF16),
            jax.ShapeDtypeStruct((8, width), F32),
        ],
        compiler_params=params(),
        name="entry",
    )(place, *pieces, inputs, cos_t, sin_t, cos, low, high)


def key_mask(keys, queries, first_query):
    key = lax.broadcasted_iota(jnp.int32, (keys, queries), 0)
    query = lax.broadcasted_iota(jnp.int32, (keys, queries), 1)
    return key <= query + first_query


def visits(peers, info_ref, seq, half, visit):
    visit(0, pl.ds(0, half), half, half, 0)
    visit(1, pl.ds(half, half), half, 2 * half, half)

    @pl.loop(0, info_ref[seq, peers])
    def _(r):
        visit(info_ref[seq, r], pl.ds(0, 2 * half), 2 * half, 2 * half, None)

    @pl.loop(info_ref[seq, peers], info_ref[seq, peers + 1])
    def _(r):
        start = pl.multiple_of(info_ref[seq, peers + 2] * half, 128)
        visit(info_ref[seq, r], pl.ds(start, half), half, 2 * half, None)


def forward_kernel(peers, info_ref, kept_ref, got_ref, *refs):
    kv_refs = refs[:peers]
    out_ref, kept16_ref, got16_ref, lse_ref = refs[peers : peers + 4]
    blocks, queries, row_max, row_sum, total = refs[peers + 4 :]
    seq = pl.program_id(0)
    half = kept_ref.shape[1]
    for k in range(peers):
        blocks[k] = kv_refs[k][0, 0]
    for h in range(GROUP):
        head = slice(h * HEAD, (h + 1) * HEAD)
        queries[h, :HEAD, :half] = kept_ref[head, :]
        queries[h, :HEAD, half:] = got_ref[head, :]
        queries[h, HEAD:, :] = jnp.zeros((HEAD, 2 * half), BF16)

    def visit(k, lanes, width, keys, diagonal):
        kv = blocks[k, :keys, :]
        values_t = kv.T[HEAD:]
        for h in range(GROUP):
            scores = matmul(kv, queries[h, :, lanes])
            if diagonal is not None:
                scores = jnp.where(key_mask(keys, width, diagonal), scores, MASKED_SCORE)
                new_max = jnp.max(scores, axis=0, keepdims=True)
                weights = jnp.exp(scores - new_max)
                row_max[h, :, lanes] = new_max
                row_sum[h, :, lanes] = jnp.sum(weights, axis=0, keepdims=True)
                total[h, :, lanes] = matmul(values_t, weights.astype(BF16))
            else:
                old_max = row_max[h, :, lanes]
                new_max = jnp.maximum(old_max, jnp.max(scores, axis=0, keepdims=True))
                weights = jnp.exp(scores - new_max)
                fading = jnp.exp(old_max - new_max)
                row_max[h, :, lanes] = new_max
                row_sum[h, :, lanes] = row_sum[h, :, lanes] * fading + jnp.sum(
                    weights, axis=0, keepdims=True
                )
                total[h, :, lanes] = total[h, :, lanes] * fading + matmul(
                    values_t, weights.astype(BF16)
                )

    visits(peers, info_ref, seq, half, visit)
    for h in range(GROUP):
        head = slice(h * HEAD, (h + 1) * HEAD)
        result = total[h] / row_sum[h]
        out_ref[head, :] = result
        kept16_ref[head, :] = result[:, :half].astype(BF16)
        got16_ref[head, :] = result[:, half:].astype(BF16)
        lse_ref[h : h + 1, :] = row_max[h] + jnp.log(row_sum[h])


def attention_specs(group, half):
    across = lambda height: pl.BlockSpec((height, 2 * half), lambda s, info: (0, s))
    across_half = lambda height, at=0: pl.BlockSpec((height, half), lambda s, info: (at, s))
    block = pl.BlockSpec((1, 1, 2 * half, PAIR), lambda s, info: (s, group, 0, 0))
    return across, across_half, block


def attend(info, kept, got, blocks, group):
    peers = len(blocks)
    steps, _, block_len, _ = blocks[0].shape
    half = block_len // 2
    rows = steps * block_len
    size = GROUP * HEAD
    across, across_half, block = attention_specs(group, half)
    work = steps * GROUP * block_len * peers * block_len
    return pl.pallas_call(
        functools.partial(forward_kernel, peers),
        grid_spec=pltpu.PrefetchScalarGridSpec(
            num_scalar_prefetch=1,
            grid=(steps,),
            in_specs=[across_half(size, group)] * 2 + [block] * peers,
            out_specs=[across(size), across_half(size), across_half(size), across(8)],
            scratch_shapes=[
                pltpu.VMEM((peers, block_len, PAIR), BF16),
                pltpu.VMEM((GROUP, PAIR, block_len), BF16),
                pltpu.VMEM((GROUP, 1, block_len), F32),
                pltpu.VMEM((GROUP, 1, block_len), F32),
                pltpu.VMEM((GROUP, HEAD, block_len), F32),
            ],
        ),
        out_shape=[
            jax.ShapeDtypeStruct((size, rows), F32),
            jax.ShapeDtypeStruct((size, rows // 2), BF16),
            jax.ShapeDtypeStruct((size, rows // 2), BF16),
            jax.ShapeDtypeStruct((8, rows), F32),
        ],
        compiler_params=params(),
        cost_estimate=pl.CostEstimate(
            flops=2 * 2 * 256 * work, bytes_accessed=4 * size * rows, transcendentals=work
        ),
        name="attend",
    )(info, kept, got, *blocks)


def backward_kernel(peers, shared, info_ref, *refs):
    (kept_ref, got_ref, dkept_ref, dgot_ref, out_ref, lse_ref) = refs[:6]
    (cos_kept, sin_kept, cos_got, sin_got) = refs[6:10]
    kv_refs = refs[10 : 10 + peers]
    results = refs[10 + peers + shared :]
    dq_kept, dq_got = results[:2]
    dkv_refs = results[2 : 2 + peers]
    blocks, grads, queries, douts, q_rows, dout_rows, delta, dq = results[2 + peers :]
    seq = pl.program_id(0)
    half = kept_ref.shape[1]
    for k in range(peers):
        blocks[k] = kv_refs[k][0, 0]
        grads[k] = jnp.zeros((2 * half, PAIR), F32)
    for h in range(GROUP):
        head = slice(h * HEAD, (h + 1) * HEAD)
        zeros = jnp.zeros((HEAD, 2 * half), BF16)
        dout = jnp.concatenate([dkept_ref[head, :], dgot_ref[head, :]], axis=1)
        queries[h, :HEAD, :half] = kept_ref[head, :]
        queries[h, :HEAD, half:] = got_ref[head, :]
        queries[h, HEAD:, :] = zeros
        douts[h, :HEAD, :] = zeros
        douts[h, HEAD:, :] = dout
        q_rows[h] = queries[h].T
        dout_rows[h] = douts[h].T
        delta[h] = jnp.sum(dout.astype(F32) * out_ref[head, :], axis=0, keepdims=True)
        dq[h] = jnp.zeros((HEAD, 2 * half), F32)

    def visit(k, lanes, width, keys, diagonal):
        kv = blocks[k, :keys, :]
        keys_t = kv.T[:HEAD]
        dkv = grads[k, :keys, :]
        for h in range(GROUP):
            probs = jnp.exp(matmul(kv, queries[h, :, lanes]) - lse_ref[h : h + 1, lanes])
            if diagonal is not None:
                probs = jnp.where(key_mask(keys, width, diagonal), probs, 0.0)
            dscores = (probs * (matmul(kv, douts[h, :, lanes]) - delta[h, :, lanes])).astype(BF16)
            dkv = (
                dkv
                + matmul(probs.astype(BF16), dout_rows[h, lanes, :])
                + matmul(dscores, q_rows[h, lanes, :])
            )
            dq[h, :, lanes] = dq[h, :, lanes] + matmul(keys_t, dscores)
        grads[k, :keys, :] = dkv

    visits(peers, info_ref, seq, half, visit)
    for h in range(GROUP):
        for at, dq_ref, cos_ref, sin_ref in (
            (0, dq_kept, cos_kept, sin_kept),
            (half, dq_got, cos_got, sin_got),
        ):
            first = dq[h, :HALF, at : at + half] * 0.125
            second = dq[h, HALF:, at : at + half] * 0.125
            cos, sin = cos_ref[...], sin_ref[...]
            dq_ref[h * HEAD : h * HEAD + HALF, :] = (first * cos + second * sin).astype(BF16)
            dq_ref[h * HEAD + HALF : (h + 1) * HEAD, :] = (second * cos - first * sin).astype(BF16)
    for k in range(peers):
        dkv_refs[k][0, 0] = grads[k].astype(BF16)


def attend_back(info, kept, got, dkept, dgot, out, lse, tables, blocks, group, shared):
    peers = len(blocks)
    steps, _, block_len, _ = blocks[0].shape
    half = block_len // 2
    rows = steps * block_len
    size = GROUP * HEAD
    across, across_half, block = attention_specs(group, half)
    pair_t = pltpu.VMEM((GROUP, PAIR, block_len), BF16)
    pair_rows = pltpu.VMEM((GROUP, block_len, PAIR), BF16)
    work = steps * GROUP * block_len * peers * block_len
    inputs = (info, kept, got, dkept, dgot, out, lse, *tables, *blocks)
    return pl.pallas_call(
        functools.partial(backward_kernel, peers, len(shared)),
        grid_spec=pltpu.PrefetchScalarGridSpec(
            num_scalar_prefetch=1,
            grid=(steps,),
            in_specs=[across_half(size, group)] * 4
            + [across(size), across(8)]
            + [across_half(HALF)] * 4
            + [block] * peers
            + [pl.BlockSpec(memory_space=pl.ANY)] * len(shared),
            out_specs=[across_half(size)] * 2 + [block] * peers,
            scratch_shapes=[
                pltpu.VMEM((peers, block_len, PAIR), BF16),
                pltpu.VMEM((peers, block_len, PAIR), F32),
                pair_t,
                pair_t,
                pair_rows,
                pair_rows,
                pltpu.VMEM((GROUP, 1, block_len), F32),
                pltpu.VMEM((GROUP, HEAD, block_len), F32),
            ],
        ),
        out_shape=[jax.ShapeDtypeStruct((size, rows // 2), BF16)] * 2
        + [jax.ShapeDtypeStruct(b.shape, BF16) for b in blocks],
        input_output_aliases={len(inputs) + i: 2 + i for i in range(len(shared))},
        compiler_params=params(),
        cost_estimate=pl.CostEstimate(
            flops=5 * 2 * 256 * work, bytes_accessed=4 * size * rows, transcendentals=work
        ),
        name="attend_back",
    )(*inputs, *shared)


def pack_kv(key_part, value_part):
    depth = key_part.shape[0]
    both = jnp.stack(
        [key_part.reshape(depth, KV_HEADS, HEAD), value_part.reshape(depth, KV_HEADS, HEAD)], axis=2
    )
    return both.reshape(depth, KV_HEADS * PAIR)


def unpack_kv(packed):
    depth = packed.shape[0]
    both = packed.reshape(depth, KV_HEADS, 2, HEAD)
    return (
        both[:, :, 0].reshape(depth, KV_HEADS * HEAD),
        both[:, :, 1].reshape(depth, KV_HEADS * HEAD),
    )


def rope_tables(positions):
    freqs = ROPE_BASE ** (-jnp.arange(HALF, dtype=F32) * 2.0 / HEAD)
    angle = positions.reshape(-1).astype(F32)[:, None] * freqs
    cos, sin = jnp.cos(angle), jnp.sin(angle)
    nothing = jnp.zeros_like(cos)
    ones = jnp.ones_like(cos)
    return (
        cos.T,
        sin.T,
        jnp.concatenate([cos, cos, ones, ones], axis=1),
        jnp.concatenate([nothing, sin, nothing, nothing], axis=1),
        jnp.concatenate([-sin, nothing, nothing, nothing], axis=1),
    )


def per_device(
    hidden_in,
    out_grad,
    block_slot,
    rope_pos,
    w_query,
    w_key,
    w_value,
    w_out,
    w_gate,
    w_up,
    w_down,
    gain_attn,
    gain_mlp,
):
    seq_count, block_len, width = hidden_in.shape
    row_count = seq_count * block_len
    hidden_width = w_gate.shape[1]
    depth = w_query.shape[0]
    cycle_index = lax.axis_index(CTX)
    cycle_size = lax.axis_size(CTX)
    shard_index = lax.axis_index("shard")
    shards = lax.axis_size("shard")
    side = lax.axis_index("core")

    def whole(parts):
        rows = parts[0].shape[0]
        out = jnp.zeros((shards * rows,) + parts[0].shape[1:], parts[0].dtype)
        for t, part in enumerate(parts):
            out = lax.dynamic_update_slice_in_dim(out, part, ((shard_index - t) % shards) * rows, 0)
        return out

    packed = jnp.concatenate(
        [
            w_query,
            gain_attn[:, None],
            gain_mlp[:, None],
            jnp.zeros((depth, HEAD - 2), BF16),
            pack_kv(w_key, w_value),
        ],
        axis=1,
    )
    cols = packed.shape[1] // 2
    mine = ring_pieces(lax.dynamic_slice_in_dim(packed, side * cols, cols, 1), "shard")
    pieces = mine + [flip(a, 1) for a in mine]
    place = jnp.stack([shard_index, side]).astype(jnp.int32)
    if depth % 16:
        pieces = [whole(pieces[:shards]), whole(pieces[shards:])]
        place = jnp.stack([jnp.zeros_like(side), side]).astype(jnp.int32)

    down_half = w_down.shape[0] // 2
    wide = after(jnp.where(side == 0, w_gate, w_up), mine[-1])
    narrow = jnp.concatenate(
        [lax.dynamic_slice_in_dim(w_down, side * down_half, down_half, 0), w_out], axis=0
    )
    narrow = after(narrow, mine[-1])
    wide = lax.all_gather(wide, "shard", axis=0, tiled=True)
    narrow = lax.all_gather(narrow, "shard", axis=0, tiled=False)

    tables = rope_tables(rope_pos)
    cycle = jnp.arange(cycle_size, dtype=jnp.int32)
    at_slot = jnp.sum(
        jnp.where(
            block_slot[:, :, None] == cycle[None, None, :],
            (cycle ^ cycle_index)[None, :, None],
            0,
        ),
        axis=1,
    )
    own_slot = lax.dynamic_index_in_dim(block_slot, cycle_index, 1, keepdims=True)
    near_slot = lax.dynamic_index_in_dim(block_slot, cycle_index ^ 1, 1, keepdims=True)
    info = jnp.concatenate(
        [
            at_slot,
            jnp.minimum(own_slot, near_slot),
            jnp.maximum(own_slot, near_slot),
            (near_slot > own_slot).astype(jnp.int32),
        ],
        axis=1,
    ).astype(jnp.int32)

    half = block_len // 2

    def halves(value):
        parts = value.reshape(value.shape[0], seq_count, 2, half)
        return (
            parts[:, :, 0].reshape(value.shape[0], row_count // 2),
            parts[:, :, 1].reshape(value.shape[0], row_count // 2),
        )

    def joined(first, second):
        parts = [a.reshape(a.shape[0], seq_count, 1, half) for a in (first, second)]
        return jnp.concatenate(parts, axis=2).reshape(first.shape[0], row_count)

    cos_kept, cos_sent = halves(tables[0])
    sin_kept, sin_sent = halves(tables[1])
    turns_got = flip(jnp.concatenate([cos_sent, sin_sent], axis=0), 1)
    turns = (cos_kept, sin_kept, turns_got[:HALF], turns_got[HALF:])

    flat_in = hidden_in.reshape(row_count, width)
    q_kept, q_sent, kv, normed_attn, full_packed, gains = entry(
        place, pieces, flat_in, tables, block_len
    )
    gain_one, gain_two = gains[0], gains[1]

    q_got = flip(q_sent, 1)
    blocks = gather_flipped(kv)
    attended = [attend(info, q_kept, q_got, blocks, g) for g in range(KV_HEADS)]
    mixed_t = jnp.concatenate([joined(a[1], flip(a[2], 1)) for a in attended], axis=0)

    other_wide = flip(wide, 1)
    full_gate = jnp.where(side == 0, wide, other_wide)
    full_up = jnp.where(side == 0, other_wide, wide)
    own_down = narrow[:, :down_half]
    other_down = flip(own_down, 1)
    full_down = jnp.where(
        side == 0,
        jnp.stack([own_down, other_down], axis=1),
        jnp.stack([other_down, own_down], axis=1),
    ).reshape(shards * 2 * down_half, width)
    full_out = narrow[:, down_half:].reshape(width, width)

    inputs = flat_in.astype(F32)
    middle = inputs + matmul_lead(mixed_t, full_out)
    normed_mlp, inverse_mlp = rms_forward(middle, gain_two)
    normed_mlp = normed_mlp.astype(BF16)
    gate = matmul(normed_mlp, full_gate)
    upward = matmul(normed_mlp, full_up)
    sigmoid_gate = jax.nn.sigmoid(gate)
    hidden = (gate * sigmoid_gate * upward).astype(BF16)
    block_out = (middle + matmul(hidden, full_down)).astype(BF16).reshape(hidden_in.shape)
    down_in = out_grad.reshape(row_count, width)
    grad_down = matmul_lead(hidden, down_in)
    hidden_grad = matmul_trail(down_in, full_down)
    gate_grad = (hidden_grad * upward * sigmoid_gate * (1.0 + gate * (1.0 - sigmoid_gate))).astype(
        BF16
    )
    up_grad = (hidden_grad * gate * sigmoid_gate).astype(BF16)
    grad_gate = matmul_lead(normed_mlp, gate_grad)
    grad_up = matmul_lead(normed_mlp, up_grad)
    normed_grad = matmul_trail(gate_grad, full_gate) + matmul_trail(up_grad, full_up)
    rows_back, grad_gain_mlp = rms_backward(middle, inverse_mlp, gain_two, normed_grad)
    middle_grad = down_in.astype(F32) + rows_back
    branch_grad = middle_grad.astype(BF16)
    grad_out = matmul(mixed_t, branch_grad)
    dout_t = matmul_trail(full_out, branch_grad).astype(BF16)

    grad_gate = grad_gate.astype(BF16)
    grad_up = grad_up.astype(BF16)
    grad_down = grad_down.astype(BF16).reshape(shards, 2, down_half, width)
    grad_out = grad_out.astype(BF16)
    early_wide = add_sent(
        jnp.where(side == 0, grad_gate, grad_up), flip(jnp.where(side == 0, grad_up, grad_gate), 1)
    )
    down_kept = lax.dynamic_index_in_dim(grad_down, side, 1, keepdims=False)
    down_sent = lax.dynamic_index_in_dim(grad_down, 1 - side, 1, keepdims=False)
    early_narrow = jnp.concatenate(
        [
            add_sent(down_kept, flip(down_sent, 1)),
            add_sent(grad_out, flip(grad_out, 1)).reshape(shards, depth, width),
        ],
        axis=1,
    )
    early_wide, early_narrow, dout_t = lax.optimization_barrier((early_wide, early_narrow, dout_t))
    early_wide = lax.psum_scatter(early_wide, "shard", scatter_dimension=0, tiled=True)
    early_narrow = lax.psum_scatter(early_narrow, "shard", scatter_dimension=0, tiled=False)

    dout_kept, dout_sent = halves(dout_t)
    dout_got = flip(dout_sent, 1)
    dq_parts = []
    dkv_parts = []
    for g in range(KV_HEADS):
        if g == KV_HEADS - 1:
            early_wide, early_narrow, dout_kept = lax.optimization_barrier(
                (early_wide, early_narrow, dout_kept)
            )
            early_wide, early_narrow = lax.psum((early_wide, early_narrow), CHIPS)
        dq_kept, dq_sent, *dkv_parts = attend_back(
            info,
            q_kept,
            q_got,
            dout_kept,
            dout_got,
            attended[g][0],
            attended[g][3],
            turns,
            blocks,
            g,
            dkv_parts,
        )
        dq_parts.append(joined(dq_kept, flip(dq_sent, 1)))
    dkv = scatter_flipped(dkv_parts)
    dkv = dkv.transpose(0, 2, 1, 3).reshape(row_count, KV_HEADS, PAIR)
    dkv = (
        dkv * tables[2][:, None]
        - jnp.roll(dkv, HALF, 2) * tables[3][:, None]
        - jnp.roll(dkv, -HALF, 2) * tables[4][:, None]
    )
    dkv = dkv.astype(BF16).reshape(row_count, KV_HEADS * PAIR)
    dq_t = jnp.concatenate(dq_parts, axis=0)
    kv_at = full_packed.shape[1] - KV_HEADS * PAIR
    grad_query = lax.dot_general(
        normed_attn, dq_t, (((0,), (1,)), ((), ())), preferred_element_type=F32
    )
    grad_kv = matmul_lead(normed_attn, dkv)
    attn_grad = lax.dot_general(
        dq_t, full_packed[:, : HEADS * HEAD], (((0,), (1,)), ((), ())), preferred_element_type=F32
    ) + matmul_trail(dkv, full_packed[:, kv_at:])
    inverse_attn = lax.rsqrt(jnp.mean(inputs * inputs, axis=-1, keepdims=True) + NORM_EPSILON)
    rows_first, grad_gain_attn = rms_backward(inputs, inverse_attn, gain_one, attn_grad)
    in_grad = (middle_grad + rows_first).astype(BF16).reshape(hidden_in.shape)

    late = jnp.concatenate(
        [
            grad_query.astype(BF16),
            grad_gain_attn.astype(BF16)[:, None],
            grad_gain_mlp.astype(BF16)[:, None],
            jnp.zeros((width, HEAD - 2), BF16),
            grad_kv.astype(BF16),
        ],
        axis=1,
    )
    late_half = lambda at: lax.dynamic_slice_in_dim(late, at * cols, cols, 1)
    late = add_sent(late_half(side), flip(late_half(1 - side), 1)).reshape(shards, depth, cols)
    share = lambda by: lax.dynamic_index_in_dim(late, (shard_index + by) % shards, 0, keepdims=False)
    arrived = [shift(share(by), "shard", by) for by in range(1, shards)]
    late = sum((a.astype(F32) for a in arrived), share(0).astype(F32)).astype(BF16)
    bit = 2
    while bit < cycle_size:
        late = add_sent(late, flip(late, bit))
        bit *= 2
    other = flip(late, 1)
    late = jnp.where(
        side == 0,
        jnp.concatenate([late, other], axis=1),
        jnp.concatenate([other, late], axis=1),
    ).astype(F32)
    grad_key, grad_value = unpack_kv(late[:, kv_at:])
    other_wide = flip(early_wide, 1)
    down_own = early_narrow[:down_half]
    down_other = flip(down_own, 1)
    grad_down = jnp.where(
        side == 0,
        jnp.concatenate([down_own, down_other], axis=0),
        jnp.concatenate([down_other, down_own], axis=0),
    )
    return (
        block_out,
        in_grad,
        late[:, : HEADS * HEAD],
        grad_key,
        grad_value,
        early_narrow[down_half:].astype(F32),
        jnp.where(side == 0, early_wide, other_wide).astype(F32),
        jnp.where(side == 0, other_wide, early_wide).astype(F32),
        grad_down.astype(F32),
        late[:, HEADS * HEAD],
        late[:, HEADS * HEAD + 1],
    )


def solution(mesh):
    ctx, shards = mesh.shape["ctx"], mesh.shape["shard"]
    split_mesh = Mesh(mesh.devices.reshape(ctx // 4, 2, 2, shards), CTX + ("shard",))
    rows = P("shard", CTX, None)
    split = P("shard", None)
    return jax.shard_map(
        per_device,
        mesh=split_mesh,
        in_specs=(rows, rows, split, P("shard", CTX)) + (split,) * 7 + (P("shard"),) * 2,
        out_specs=(rows, rows) + (split,) * 7 + (P("shard"),) * 2,
        check_vma=False,
    )
```

```python
import functools

import jax
import jax.numpy as jnp
from jax import lax
from jax.experimental import pallas as pl
from jax.experimental.pallas import tpu as pltpu
from jax.sharding import Mesh
from jax.sharding import PartitionSpec as P

HEADS = 9
KV_HEADS = 3
HEAD = 64
GROUP = HEADS // KV_HEADS
PAIR = 2 * HEAD
HALF = HEAD // 2

NORM_EPSILON = 1e-05
ROPE_BASE = 100000.0
LOG2_E = 1.4426950408889634
LN_2 = 0.6931471805599453
MASKED_SCORE = -1e30
SUM_ROWS = 16
VMEM_BYTES = 56 * 1024 * 1024

CHIPS = ("cy", "cx")
CTX = CHIPS + ("core",)

F32 = jnp.float32
BF16 = jnp.bfloat16


def params():
    return pltpu.CompilerParams(vmem_limit_bytes=VMEM_BYTES)


def matmul(left, right):
    return jnp.dot(left, right, preferred_element_type=F32)


def matmul_lead(left, right):
    return lax.dot_general(left, right, (((0,), (0,)), ((), ())), preferred_element_type=F32)


def matmul_trail(left, right):
    return lax.dot_general(left, right, (((1,), (1,)), ((), ())), preferred_element_type=F32)


def flip(value, bit):
    peers = lax.axis_size(CTX)
    return lax.ppermute(value, CTX, [(i, i ^ bit) for i in range(peers)])


def shift(value, axis, by=1):
    peers = lax.axis_size(axis)
    return lax.ppermute(value, axis, [(i, (i + by) % peers) for i in range(peers)])


def ring_pieces(piece, axis):
    pieces = [piece]
    for _ in range(lax.axis_size(axis) - 1):
        pieces.append(shift(pieces[-1], axis))
    return pieces


def after(value, *others):
    return lax.optimization_barrier((value,) + others)[0]


def gather_flipped(own):
    peers = lax.axis_size(CTX)
    if peers == 8:
        by_x = flip(own, 2)
        by_y = flip(own, 4)
        first = flip(by_y[:1], 2)
        second = flip(by_x[1:], 4)
        same_core = [(own,), (by_x,), (by_y,), (first, second)]
        other_core = [tuple(flip(a, 1) for a in block) for block in same_core]
        return [b for pair in zip(same_core, other_core) for b in pair]
    blocks = [own]
    bit = 1
    while bit < peers:
        blocks = blocks + [flip(b, bit) for b in blocks]
        bit *= 2
    return [(b,) for b in blocks]


def add_sent(kept, arrived):
    return (kept.astype(F32) + arrived.astype(F32)).astype(BF16)


def scatter_flipped(parts):
    peers = len(parts)
    if peers == 8:
        near = {k: flip(parts[k + 1], 1) for k in (6, 2, 4, 0)}
        seq = lambda k, i: add_sent(parts[k][i : i + 1], near[k][i : i + 1])
        far_x = flip(seq(6, 0), 2)
        far_y = flip(seq(6, 1), 4)
        x_first = flip(seq(2, 0), 2)
        y_second = flip(seq(4, 1), 4)
        y_first = flip(add_sent(seq(4, 0), far_x), 4)
        x_second = flip(add_sent(seq(2, 1), far_y), 2)
        return [(add_sent(parts[0], near[0]),), (x_first, x_second), (y_first, y_second)]
    while peers > 1:
        peers //= 2
        parts = [add_sent(parts[k], flip(parts[k + peers], peers)) for k in range(peers)]
    return [(parts[0],)]


def entry_kernel(shards, width, place_ref, *refs):
    piece_refs = refs[: 2 * shards]
    (x_ref, cos_t_ref, sin_t_ref, cos_ref, low_ref, high_ref) = refs[2 * shards : 2 * shards + 6]
    kept_ref, sent_ref, kv_ref, normed_ref, packed_ref, gains_ref = refs[
        2 * shards + 6 : 2 * shards + 12
    ]
    (weight,) = refs[2 * shards + 12 :]
    half = kept_ref.shape[1]
    depth = piece_refs[0].shape[0]
    cols = piece_refs[0].shape[1]

    @pl.when(pl.program_id(0) == 0)
    def assemble():
        shard, side = place_ref[0], place_ref[1]
        for t in range(shards):
            row = pl.multiple_of(lax.rem(shard - t + shards, shards) * depth, 16)
            mine = pl.multiple_of(side * cols, 128)
            other = pl.multiple_of((1 - side) * cols, 128)
            weight[pl.ds(row, depth), pl.ds(mine, cols)] = piece_refs[t][...]
            weight[pl.ds(row, depth), pl.ds(other, cols)] = piece_refs[shards + t][...]
        packed_ref[...] = weight[...]
        gains_ref[...] = weight[:, 512:640].astype(F32).T[64:72, :]

    rows = x_ref[...].astype(F32)
    inverse = lax.rsqrt(jnp.mean(rows * rows, axis=-1, keepdims=True) + NORM_EPSILON)
    normed = (rows * inverse * gains_ref[0:1, :]).astype(BF16)
    normed_ref[...] = normed
    cos_t = cos_t_ref[...]
    sin_t = sin_t_ref[...]
    for chunk in range(5):
        lin = matmul(normed, weight[:, chunk * PAIR : (chunk + 1) * PAIR]).T
        for part in range(2):
            head = 2 * chunk + part
            if head < HEADS:
                first = lin[part * HEAD : part * HEAD + HALF]
                second = lin[part * HEAD + HALF : (part + 1) * HEAD]
                turned = jnp.concatenate(
                    [first * cos_t - second * sin_t, second * cos_t + first * sin_t], axis=0
                )
                turned = (turned * (0.125 * LOG2_E)).astype(BF16)
                kept_ref[head * HEAD : (head + 1) * HEAD, :] = turned[:, :half]
                sent_ref[head * HEAD : (head + 1) * HEAD, :] = turned[:, half:]
    for group in range(KV_HEADS):
        at = 5 * PAIR + group * PAIR
        lin = matmul(normed, weight[:, at : at + PAIR])
        turned = (
            lin * cos_ref[...]
            + pltpu.roll(lin, HALF, 1) * low_ref[...]
            + pltpu.roll(lin, PAIR - HALF, 1) * high_ref[...]
        )
        kv_ref[0, group] = turned.astype(BF16)


def choose(refs, seq):
    if len(refs) == 1:
        return refs[0][...]
    return jnp.where(seq == 0, refs[0][...], refs[1][...])


def entry(place, pieces, inputs, tables, block_len):
    shards = len(pieces) // 2
    rows, width = inputs.shape
    cos_t, sin_t, cos, low, high = tables
    depth, cols = pieces[0].shape
    steps = rows // block_len
    fixed = lambda shape: pl.BlockSpec(shape, lambda s, place: (0,) * len(shape))
    return pl.pallas_call(
        functools.partial(entry_kernel, shards, width),
        grid_spec=pltpu.PrefetchScalarGridSpec(
            num_scalar_prefetch=1,
            grid=(steps,),
            in_specs=[fixed((depth, cols)) for _ in pieces]
            + [pl.BlockSpec((block_len, width), lambda s, place: (s, 0))]
            + [pl.BlockSpec((HALF, block_len), lambda s, place: (0, s))] * 2
            + [pl.BlockSpec((block_len, PAIR), lambda s, place: (s, 0))] * 3,
            out_specs=[
                pl.BlockSpec((HEADS * HEAD, block_len // 2), lambda s, place: (0, s)),
                pl.BlockSpec((HEADS * HEAD, block_len // 2), lambda s, place: (0, s)),
                pl.BlockSpec((1, KV_HEADS, block_len, PAIR), lambda s, place: (s, 0, 0, 0)),
                pl.BlockSpec((block_len, width), lambda s, place: (s, 0)),
                fixed((width, 2 * cols)),
                fixed((8, width)),
            ],
            scratch_shapes=[pltpu.VMEM((width, 2 * cols), BF16)],
        ),
        out_shape=[
            jax.ShapeDtypeStruct((HEADS * HEAD, rows // 2), BF16),
            jax.ShapeDtypeStruct((HEADS * HEAD, rows // 2), BF16),
            jax.ShapeDtypeStruct((steps, KV_HEADS, block_len, PAIR), BF16),
            jax.ShapeDtypeStruct((rows, width), BF16),
            jax.ShapeDtypeStruct((width, 2 * cols), BF16),
            jax.ShapeDtypeStruct((8, width), F32),
        ],
        compiler_params=params(),
        name="entry",
    )(place, *pieces, inputs, cos_t, sin_t, cos, low, high)


def key_mask(keys, queries, first_query):
    key = lax.broadcasted_iota(jnp.int32, (keys, queries), 0)
    query = lax.broadcasted_iota(jnp.int32, (keys, queries), 1)
    return key <= query + first_query


def visits(peers, info_ref, seq, half, visit):
    visit(0, pl.ds(0, half), half, half, 0)
    visit(1, pl.ds(half, half), half, 2 * half, half)

    @pl.loop(0, info_ref[seq, peers])
    def _(r):
        visit(info_ref[seq, r], pl.ds(0, 2 * half), 2 * half, 2 * half, None)

    @pl.loop(info_ref[seq, peers], info_ref[seq, peers + 1])
    def _(r):
        start = pl.multiple_of(info_ref[seq, peers + 2] * half, 128)
        visit(info_ref[seq, r], pl.ds(start, half), half, 2 * half, None)


def load_blocks(blocks, counts, refs, seq):
    at = 0
    for k, count in enumerate(counts):
        blocks[k] = choose(refs[at : at + count], seq)[0, 0]
        at += count


def forward_kernel(counts, info_ref, kept_ref, got_ref, *refs):
    peers, arrays = len(counts), sum(counts)
    kv_refs = refs[:arrays]
    out_ref, kept16_ref, got16_ref, lse_ref = refs[arrays : arrays + 4]
    blocks, queries, row_max, total = refs[arrays + 4 :]
    seq = pl.program_id(0)
    half = kept_ref.shape[1]
    load_blocks(blocks, counts, kv_refs, seq)
    for h in range(GROUP):
        head = slice(h * HEAD, (h + 1) * HEAD)
        queries[h, :HEAD, :half] = kept_ref[head, :]
        queries[h, :HEAD, half:] = got_ref[head, :]
        queries[h, HEAD:, :] = jnp.zeros((HEAD, 2 * half), BF16)

    def visit(k, lanes, width, keys, diagonal):
        kv = blocks[k, :keys, :]
        ones = jnp.ones((SUM_ROWS, keys), BF16)
        values_t = jnp.concatenate([kv.T[HEAD:], ones], axis=0)
        for h in range(GROUP):
            scores = matmul(kv, queries[h, :, lanes])
            if diagonal is not None:
                scores = jnp.where(key_mask(keys, width, diagonal), scores, MASKED_SCORE)
                new_max = jnp.max(scores, axis=0, keepdims=True)
                weights = jnp.exp2(scores - new_max).astype(BF16)
                row_max[h, :, lanes] = new_max
                total[h, :, lanes] = matmul(values_t, weights)
            else:
                old_max = row_max[h, :, lanes]
                new_max = jnp.maximum(old_max, jnp.max(scores, axis=0, keepdims=True))
                weights = jnp.exp2(scores - new_max).astype(BF16)
                fading = jnp.exp2(old_max - new_max)
                row_max[h, :, lanes] = new_max
                total[h, :, lanes] = total[h, :, lanes] * fading + matmul(values_t, weights)

    visits(peers, info_ref, seq, half, visit)
    for h in range(GROUP):
        head = slice(h * HEAD, (h + 1) * HEAD)
        row_sum = total[h, HEAD : HEAD + 1, :]
        result = total[h, :HEAD, :] / row_sum
        out_ref[head, :] = result
        kept16_ref[head, :] = result[:, :half].astype(BF16)
        got16_ref[head, :] = result[:, half:].astype(BF16)
        lse_ref[h : h + 1, :] = row_max[h] + jnp.log2(row_sum)


def attention_specs(group, half):
    across = lambda height: pl.BlockSpec((height, 2 * half), lambda s, info: (0, s))
    across_half = lambda height, at=0: pl.BlockSpec((height, half), lambda s, info: (at, s))

    def block(whole):
        return pl.BlockSpec(
            (1, 1, 2 * half, PAIR), lambda s, info: (s if whole else 0, group, 0, 0)
        )

    return across, across_half, block


def attend(info, kept, got, blocks, group):
    peers = len(blocks)
    counts = tuple(len(b) for b in blocks)
    arrays = [a for b in blocks for a in b]
    steps, _, block_len, _ = arrays[0].shape
    half = block_len // 2
    rows = steps * block_len
    size = GROUP * HEAD
    across, across_half, block = attention_specs(group, half)
    work = steps * GROUP * block_len * peers * block_len
    return pl.pallas_call(
        functools.partial(forward_kernel, counts),
        grid_spec=pltpu.PrefetchScalarGridSpec(
            num_scalar_prefetch=1,
            grid=(steps,),
            in_specs=[across_half(size, group)] * 2 + [block(len(b) == 1) for b in blocks for _ in b],
            out_specs=[across(size), across_half(size), across_half(size), across(8)],
            scratch_shapes=[
                pltpu.VMEM((peers, block_len, PAIR), BF16),
                pltpu.VMEM((GROUP, PAIR, block_len), BF16),
                pltpu.VMEM((GROUP, 1, block_len), F32),
                pltpu.VMEM((GROUP, HEAD + SUM_ROWS, block_len), F32),
            ],
        ),
        out_shape=[
            jax.ShapeDtypeStruct((size, rows), F32),
            jax.ShapeDtypeStruct((size, rows // 2), BF16),
            jax.ShapeDtypeStruct((size, rows // 2), BF16),
            jax.ShapeDtypeStruct((8, rows), F32),
        ],
        compiler_params=params(),
        cost_estimate=pl.CostEstimate(
            flops=2 * 2 * 256 * work, bytes_accessed=4 * size * rows, transcendentals=work
        ),
        name="attend",
    )(info, kept, got, *arrays)


def backward_kernel(counts, shared, info_ref, *refs):
    peers, arrays = len(counts), sum(counts)
    (kept_ref, got_ref, dkept_ref, dgot_ref, out_ref, lse_ref) = refs[:6]
    (cos_kept, sin_kept, cos_got, sin_got) = refs[6:10]
    kv_refs = refs[10 : 10 + arrays]
    results = refs[10 + arrays + shared :]
    dq_kept, dq_got = results[:2]
    dkv_refs = results[2 : 2 + peers]
    blocks, grads, queries, douts, q_rows, dout_rows, delta, dq = results[2 + peers :]
    seq = pl.program_id(0)
    half = kept_ref.shape[1]
    load_blocks(blocks, counts, kv_refs, seq)
    for k in range(peers):
        grads[k] = jnp.zeros((2 * half, PAIR), F32)
    for h in range(GROUP):
        head = slice(h * HEAD, (h + 1) * HEAD)
        zeros = jnp.zeros((HEAD, 2 * half), BF16)
        dout = jnp.concatenate([dkept_ref[head, :], dgot_ref[head, :]], axis=1)
        queries[h, :HEAD, :half] = kept_ref[head, :]
        queries[h, :HEAD, half:] = got_ref[head, :]
        queries[h, HEAD:, :] = zeros
        douts[h, :HEAD, :] = zeros
        douts[h, HEAD:, :] = dout
        q_rows[h] = queries[h].T
        dout_rows[h] = douts[h].T
        delta[h] = jnp.sum(dout.astype(F32) * out_ref[head, :], axis=0, keepdims=True)
        dq[h] = jnp.zeros((HEAD, 2 * half), F32)

    def visit(k, lanes, width, keys, diagonal):
        kv = blocks[k, :keys, :]
        keys_t = kv.T[:HEAD]
        dkv = grads[k, :keys, :]
        for h in range(GROUP):
            probs = jnp.exp2(matmul(kv, queries[h, :, lanes]) - lse_ref[h : h + 1, lanes])
            if diagonal is not None:
                probs = jnp.where(key_mask(keys, width, diagonal), probs, 0.0)
            dscores = (probs * (matmul(kv, douts[h, :, lanes]) - delta[h, :, lanes])).astype(BF16)
            dkv = (
                dkv
                + matmul(probs.astype(BF16), dout_rows[h, lanes, :])
                + matmul(dscores, q_rows[h, lanes, :])
            )
            dq[h, :, lanes] = dq[h, :, lanes] + matmul(keys_t, dscores)
        grads[k, :keys, :] = dkv

    visits(peers, info_ref, seq, half, visit)
    for h in range(GROUP):
        for at, dq_ref, cos_ref, sin_ref in (
            (0, dq_kept, cos_kept, sin_kept),
            (half, dq_got, cos_got, sin_got),
        ):
            first = dq[h, :HALF, at : at + half] * 0.125
            second = dq[h, HALF:, at : at + half] * 0.125
            cos, sin = cos_ref[...], sin_ref[...]
            dq_ref[h * HEAD : h * HEAD + HALF, :] = (first * cos + second * sin).astype(BF16)
            dq_ref[h * HEAD + HALF : (h + 1) * HEAD, :] = (second * cos - first * sin).astype(BF16)
    lane = lax.broadcasted_iota(jnp.int32, (1, PAIR), 1)
    unit = jnp.where(lane < HEAD, LN_2, 1.0)
    for k in range(peers):
        dkv_refs[k][0, 0] = (grads[k] * unit).astype(BF16)


def attend_back(info, kept, got, dkept, dgot, out, lse, tables, blocks, group, shared):
    peers = len(blocks)
    counts = tuple(len(b) for b in blocks)
    arrays = [a for b in blocks for a in b]
    steps, _, block_len, _ = arrays[0].shape
    half = block_len // 2
    rows = steps * block_len
    size = GROUP * HEAD
    across, across_half, block = attention_specs(group, half)
    pair_t = pltpu.VMEM((GROUP, PAIR, block_len), BF16)
    pair_rows = pltpu.VMEM((GROUP, block_len, PAIR), BF16)
    work = steps * GROUP * block_len * peers * block_len
    inputs = (info, kept, got, dkept, dgot, out, lse, *tables, *arrays)
    return pl.pallas_call(
        functools.partial(backward_kernel, counts, len(shared)),
        grid_spec=pltpu.PrefetchScalarGridSpec(
            num_scalar_prefetch=1,
            grid=(steps,),
            in_specs=[across_half(size, group)] * 4
            + [across(size), across(8)]
            + [across_half(HALF)] * 4
            + [block(len(b) == 1) for b in blocks for _ in b]
            + [pl.BlockSpec(memory_space=pl.ANY)] * len(shared),
            out_specs=[across_half(size)] * 2 + [block(True)] * peers,
            scratch_shapes=[
                pltpu.VMEM((peers, block_len, PAIR), BF16),
                pltpu.VMEM((peers, block_len, PAIR), F32),
                pair_t,
                pair_t,
                pair_rows,
                pair_rows,
                pltpu.VMEM((GROUP, 1, block_len), F32),
                pltpu.VMEM((GROUP, HEAD, block_len), F32),
            ],
        ),
        out_shape=[jax.ShapeDtypeStruct((size, rows // 2), BF16)] * 2
        + [jax.ShapeDtypeStruct((steps, KV_HEADS, block_len, PAIR), BF16)] * peers,
        input_output_aliases={len(inputs) + i: 2 + i for i in range(len(shared))},
        compiler_params=params(),
        cost_estimate=pl.CostEstimate(
            flops=5 * 2 * 256 * work, bytes_accessed=4 * size * rows, transcendentals=work
        ),
        name="attend_back",
    )(*inputs, *shared)


def norm_back(rows, inverse, gain, grad):
    scaled = grad * gain
    mean = jnp.mean(scaled * rows, axis=-1, keepdims=True)
    row_grad = inverse * scaled - rows * (inverse * inverse * inverse) * mean
    return row_grad, jnp.sum(grad * rows * inverse, axis=0, keepdims=True)


def middle_kernel(down_half, side_ref, *refs):
    kept_refs, back_refs = refs[:KV_HEADS], refs[KV_HEADS : 2 * KV_HEADS]
    x_ref, dy_ref, gains_ref, wide_ref, other_ref, narrow_ref, other_down_ref, wo_ref = refs[
        2 * KV_HEADS : 2 * KV_HEADS + 8
    ]
    (
        out_ref,
        dh_ref,
        dkept_ref,
        dsent_ref,
        wide_kept,
        wide_sent,
        narrow_kept,
        narrow_sent,
        gain_ref,
    ) = refs[2 * KV_HEADS + 8 : 2 * KV_HEADS + 17]
    ff_weight, down_weight, mixed, ff_grad, down_grad, out_acc = refs[2 * KV_HEADS + 17 :]
    shards = narrow_ref.shape[0]
    hidden_width = ff_weight.shape[2]
    depth = narrow_ref.shape[1] - down_half
    half = kept_refs[0].shape[1]
    size = GROUP * HEAD
    step = pl.program_id(0)
    side = side_ref[0]

    @pl.when(step == 0)
    def assemble():
        ff_weight[side] = wide_ref[...]
        ff_weight[1 - side] = other_ref[...]
        for z in range(shards):
            mine = pl.multiple_of((2 * z + side) * down_half, 16)
            other = pl.multiple_of((2 * z + 1 - side) * down_half, 16)
            down_weight[pl.ds(mine, down_half), :] = narrow_ref[z, :down_half, :]
            down_weight[pl.ds(other, down_half), :] = other_down_ref[z]
        ff_grad[...] = jnp.zeros(ff_grad.shape, F32)
        down_grad[...] = jnp.zeros(down_grad.shape, F32)
        out_acc[...] = jnp.zeros(out_acc.shape, F32)
        gain_ref[...] = jnp.zeros(gain_ref.shape, F32)

    for g in range(KV_HEADS):
        mixed[g * size : (g + 1) * size, :half] = kept_refs[g][...]
        mixed[g * size : (g + 1) * size, half:] = back_refs[g][...]
    weight_out = wo_ref[...]
    gain = gains_ref[1:2, :]
    rows = x_ref[...].astype(F32) + matmul_lead(mixed[...], weight_out)
    inverse = lax.rsqrt(jnp.mean(rows * rows, axis=-1, keepdims=True) + NORM_EPSILON)
    normed = (rows * inverse * gain).astype(BF16)
    normed_t = normed.T
    dy = dy_ref[...]
    result = rows
    dnormed = jnp.zeros(rows.shape, F32)
    chunk = 512
    for at in range(0, hidden_width, chunk):
        part = slice(at, at + chunk)
        gate = matmul(normed, ff_weight[0, :, part])
        upward = matmul(normed, ff_weight[1, :, part])
        dhidden = matmul_trail(dy, down_weight[part, :])
        sigmoid = jax.nn.sigmoid(gate)
        silu = gate * sigmoid
        hidden = (silu * upward).astype(BF16)
        dgate = (dhidden * upward * sigmoid * (1.0 + gate * (1.0 - sigmoid))).astype(BF16)
        dup = (dhidden * silu).astype(BF16)
        result = result + matmul(hidden, down_weight[part, :])
        down_grad[part, :] += matmul_lead(hidden, dy)
        ff_grad[0, :, part] += matmul(normed_t, dgate)
        ff_grad[1, :, part] += matmul(normed_t, dup)
        dnormed = dnormed + (
            matmul_trail(dgate, ff_weight[0, :, part]) + matmul_trail(dup, ff_weight[1, :, part])
        )
    out_ref[...] = result.astype(BF16)
    row_grad, gain_grad = norm_back(rows, inverse, gain, dnormed)
    gain_ref[0:1, :] += gain_grad
    drows = dy.astype(F32) + row_grad
    dh_ref[...] = drows
    drows = drows.astype(BF16)
    out_acc[...] += matmul(mixed[...], drows)
    dout = matmul_trail(weight_out, drows).astype(BF16)
    dkept_ref[...] = dout[:, :half]
    dsent_ref[...] = dout[:, half:]

    @pl.when(step == pl.num_programs(0) - 1)
    def emit():
        wide_kept[...] = ff_grad[side].astype(BF16)
        wide_sent[...] = ff_grad[1 - side].astype(BF16)
        for z in range(shards):
            mine = pl.multiple_of((2 * z + side) * down_half, 8)
            other = pl.multiple_of((2 * z + 1 - side) * down_half, 8)
            narrow_kept[z, :down_half, :] = down_grad[pl.ds(mine, down_half), :].astype(BF16)
            narrow_sent[z, :down_half, :] = down_grad[pl.ds(other, down_half), :].astype(BF16)
            out_rows = out_acc[z * depth : (z + 1) * depth, :].astype(BF16)
            narrow_kept[z, down_half:, :] = out_rows
            narrow_sent[z, down_half:, :] = out_rows


def middle(side, kept, back, inputs, dy, gains, wide, other_wide, narrow, other_down, wo, block_len):
    rows, width = inputs.shape
    hidden_width = wide.shape[1]
    down_half = other_down.shape[1]
    size = GROUP * HEAD
    steps = rows // block_len
    half = block_len // 2
    fixed = lambda a: pl.BlockSpec(a.shape, lambda s, side: (0,) * a.ndim)
    across = lambda height: pl.BlockSpec((height, half), lambda s, side: (0, s))
    down = pl.BlockSpec((block_len, width), lambda s, side: (s, 0))
    shape = jax.ShapeDtypeStruct
    work = 3 * 2 * rows * width * (3 * hidden_width + width)
    return pl.pallas_call(
        functools.partial(middle_kernel, down_half),
        grid_spec=pltpu.PrefetchScalarGridSpec(
            num_scalar_prefetch=1,
            grid=(steps,),
            in_specs=[across(size)] * (2 * KV_HEADS)
            + [down, down]
            + [fixed(a) for a in (gains, wide, other_wide, narrow, other_down, wo)],
            out_specs=[down, down, across(HEADS * HEAD), across(HEADS * HEAD)]
            + [fixed(a) for a in (wide, wide, narrow, narrow, gains)],
            scratch_shapes=[
                pltpu.VMEM((2, width, hidden_width), BF16),
                pltpu.VMEM((hidden_width, width), BF16),
                pltpu.VMEM((HEADS * HEAD, block_len), BF16),
                pltpu.VMEM((2, width, hidden_width), F32),
                pltpu.VMEM((hidden_width, width), F32),
                pltpu.VMEM((HEADS * HEAD, width), F32),
            ],
        ),
        out_shape=[
            shape((rows, width), BF16),
            shape((rows, width), F32),
            shape((HEADS * HEAD, rows // 2), BF16),
            shape((HEADS * HEAD, rows // 2), BF16),
            shape(wide.shape, BF16),
            shape(wide.shape, BF16),
            shape(narrow.shape, BF16),
            shape(narrow.shape, BF16),
            shape(gains.shape, F32),
        ],
        compiler_params=params(),
        cost_estimate=pl.CostEstimate(
            flops=work, bytes_accessed=30 * 1024 * 1024, transcendentals=rows * hidden_width
        ),
        name="middle",
    )(side, *kept, *back, inputs, dy, gains, wide, other_wide, narrow, other_down, wo)


def exit_query_kernel(*refs):
    kept_refs, back_refs = refs[:KV_HEADS], refs[KV_HEADS : 2 * KV_HEADS]
    normed_ref, weight_ref, grad_ref, da_ref, dq = refs[2 * KV_HEADS :]
    half = kept_refs[0].shape[1]
    size = GROUP * HEAD
    for g in range(KV_HEADS):
        dq[g * size : (g + 1) * size, :half] = kept_refs[g][...]
        dq[g * size : (g + 1) * size, half:] = back_refs[g][...]
    rows = dq[...].T
    da_ref[...] = matmul_trail(rows, weight_ref[:, : HEADS * HEAD])
    grad = matmul_lead(normed_ref[...], rows)

    @pl.when(pl.program_id(0) == 0)
    def _():
        grad_ref[...] = grad

    @pl.when(pl.program_id(0) > 0)
    def _():
        grad_ref[...] += grad


def exit_query(kept, back, normed, weight, block_len):
    rows, width = normed.shape
    size = GROUP * HEAD
    half = block_len // 2
    down = pl.BlockSpec((block_len, width), lambda s: (s, 0))
    return pl.pallas_call(
        exit_query_kernel,
        grid=(rows // block_len,),
        in_specs=[pl.BlockSpec((size, half), lambda s: (0, s))] * (2 * KV_HEADS)
        + [down, pl.BlockSpec(weight.shape, lambda s: (0, 0))],
        out_specs=[pl.BlockSpec((width, HEADS * HEAD), lambda s: (0, 0)), down],
        out_shape=[
            jax.ShapeDtypeStruct((width, HEADS * HEAD), F32),
            jax.ShapeDtypeStruct((rows, width), F32),
        ],
        scratch_shapes=[pltpu.VMEM((HEADS * HEAD, block_len), BF16)],
        compiler_params=params(),
        name="exit_query",
    )(*kept, *back, normed, weight)


def exit_kernel(counts, side_ref, *refs):
    arrays = sum(counts)
    part_refs = refs[:arrays]
    (normed_ref, weight_ref, gq_ref, da_ref, x_ref, dh_ref, gains_ref, gain_mlp_ref) = refs[
        arrays : arrays + 8
    ]
    cos_ref, low_ref, high_ref, dx_ref, kept_ref, sent_ref, grad, gain_acc = refs[arrays + 8 :]
    step = pl.program_id(0)
    side = side_ref[0]
    cols = kept_ref.shape[1]
    wide = HEADS * HEAD

    @pl.when(step == 0)
    def _():
        grad[...] = jnp.zeros(grad.shape, F32)
        gain_acc[...] = jnp.zeros(gain_acc.shape, F32)

    parts = []
    at = 0
    for count in counts:
        parts.append(choose(part_refs[at : at + count], step))
        at += count
    normed = normed_ref[...]
    dnormed = da_ref[...]
    kv_at = weight_ref.shape[1] - KV_HEADS * PAIR
    for g in range(KV_HEADS):
        dkv = sum((part[0, g].astype(F32) for part in parts[1:]), parts[0][0, g].astype(F32))
        turned = (
            dkv * cos_ref[...]
            - pltpu.roll(dkv, HALF, 1) * low_ref[...]
            - pltpu.roll(dkv, PAIR - HALF, 1) * high_ref[...]
        ).astype(BF16)
        here = slice(kv_at + g * PAIR, kv_at + (g + 1) * PAIR)
        dnormed = dnormed + matmul_trail(turned, weight_ref[:, here])
        grad[:, g * PAIR : (g + 1) * PAIR] += matmul_lead(normed, turned)
    rows = x_ref[...].astype(F32)
    inverse = lax.rsqrt(jnp.mean(rows * rows, axis=-1, keepdims=True) + NORM_EPSILON)
    row_grad, gain_grad = norm_back(rows, inverse, gains_ref[0:1, :], dnormed)
    gain_acc[0:1, :] += gain_grad
    dx_ref[...] = (dh_ref[...] + row_grad).astype(BF16)

    @pl.when(step == pl.num_programs(0) - 1)
    def _():
        width = normed.shape[1]
        gains = jnp.concatenate(
            [
                jnp.zeros((HEAD, width), F32),
                gain_acc[0:1, :],
                gain_mlp_ref[0:1, :],
                jnp.zeros((HEAD - 2, width), F32),
            ],
            axis=0,
        ).T

        def write_low(ref):
            ref[...] = gq_ref[:, :cols].astype(BF16)

        def write_high(ref):
            ref[:, :PAIR] = gains.astype(BF16)
            ref[:, : wide - cols] = gq_ref[:, cols:].astype(BF16)
            ref[:, PAIR:] = grad[...].astype(BF16)

        @pl.when(side == 0)
        def _():
            write_low(kept_ref)
            write_high(sent_ref)

        @pl.when(side != 0)
        def _():
            write_high(kept_ref)
            write_low(sent_ref)


def leave(side, parts, normed, weight, grad_query, da, inputs, dh, gains, gain_mlp, tables, block_len):
    rows, width = normed.shape
    cols = weight.shape[1] // 2
    counts = tuple(len(p) for p in parts)
    arrays = [a for p in parts for a in p]
    down = pl.BlockSpec((block_len, width), lambda s, side: (s, 0))
    fixed = lambda shape: pl.BlockSpec(shape, lambda s, side: (0,) * len(shape))

    def block(whole):
        return pl.BlockSpec(
            (1, KV_HEADS, block_len, PAIR), lambda s, side: (s if whole else 0, 0, 0, 0)
        )

    table = pl.BlockSpec((block_len, PAIR), lambda s, side: (s, 0))
    return pl.pallas_call(
        functools.partial(exit_kernel, counts),
        grid_spec=pltpu.PrefetchScalarGridSpec(
            num_scalar_prefetch=1,
            grid=(rows // block_len,),
            in_specs=[block(len(p) == 1) for p in parts for _ in p]
            + [down, fixed(weight.shape), fixed(grad_query.shape), down, down, down]
            + [fixed(gains.shape), fixed(gain_mlp.shape)]
            + [table] * 3,
            out_specs=[down, fixed((width, cols)), fixed((width, cols))],
            scratch_shapes=[
                pltpu.VMEM((width, KV_HEADS * PAIR), F32),
                pltpu.VMEM((8, width), F32),
            ],
        ),
        out_shape=[
            jax.ShapeDtypeStruct((rows, width), BF16),
            jax.ShapeDtypeStruct((width, cols), BF16),
            jax.ShapeDtypeStruct((width, cols), BF16),
        ],
        compiler_params=params(),
        name="leave",
    )(side, *arrays, normed, weight, grad_query, da, inputs, dh, gains, gain_mlp, *tables)


def pack_kv(key_part, value_part):
    depth = key_part.shape[0]
    both = jnp.stack(
        [key_part.reshape(depth, KV_HEADS, HEAD), value_part.reshape(depth, KV_HEADS, HEAD)], axis=2
    )
    return both.reshape(depth, KV_HEADS * PAIR)


def unpack_kv(packed):
    depth = packed.shape[0]
    both = packed.reshape(depth, KV_HEADS, 2, HEAD)
    return (
        both[:, :, 0].reshape(depth, KV_HEADS * HEAD),
        both[:, :, 1].reshape(depth, KV_HEADS * HEAD),
    )


def rope_tables(positions):
    freqs = ROPE_BASE ** (-jnp.arange(HALF, dtype=F32) * 2.0 / HEAD)
    angle = positions.reshape(1, -1).astype(F32) * freqs[:, None]
    cos_t, sin_t = jnp.cos(angle), jnp.sin(angle)
    cos, sin = cos_t.T, sin_t.T
    nothing = jnp.zeros_like(cos)
    ones = jnp.ones_like(cos)
    return (
        cos_t,
        sin_t,
        jnp.concatenate([cos, cos, ones, ones], axis=1),
        jnp.concatenate([nothing, sin, nothing, nothing], axis=1),
        jnp.concatenate([-sin, nothing, nothing, nothing], axis=1),
    )


def per_device(
    hidden_in,
    out_grad,
    block_slot,
    rope_pos,
    w_query,
    w_key,
    w_value,
    w_out,
    w_gate,
    w_up,
    w_down,
    gain_attn,
    gain_mlp,
):
    seq_count, block_len, width = hidden_in.shape
    row_count = seq_count * block_len
    hidden_width = w_gate.shape[1]
    depth = w_query.shape[0]
    cycle_index = lax.axis_index(CTX)
    cycle_size = lax.axis_size(CTX)
    shard_index = lax.axis_index("shard")
    shards = lax.axis_size("shard")
    side = lax.axis_index("core")

    def whole(parts):
        rows = parts[0].shape[0]
        out = jnp.zeros((shards * rows,) + parts[0].shape[1:], parts[0].dtype)
        for t, part in enumerate(parts):
            out = lax.dynamic_update_slice_in_dim(out, part, ((shard_index - t) % shards) * rows, 0)
        return out

    packed = jnp.concatenate(
        [
            w_query,
            gain_attn[:, None],
            gain_mlp[:, None],
            jnp.zeros((depth, HEAD - 2), BF16),
            pack_kv(w_key, w_value),
        ],
        axis=1,
    )
    cols = packed.shape[1] // 2
    mine = ring_pieces(lax.dynamic_slice_in_dim(packed, side * cols, cols, 1), "shard")
    pieces = mine + [flip(a, 1) for a in mine]
    place = jnp.stack([shard_index, side]).astype(jnp.int32)
    if depth % 16:
        pieces = [whole(pieces[:shards]), whole(pieces[shards:])]
        place = jnp.stack([jnp.zeros_like(side), side]).astype(jnp.int32)

    down_half = w_down.shape[0] // 2
    wide = after(jnp.where(side == 0, w_gate, w_up), mine[-1])
    narrow = jnp.concatenate(
        [lax.dynamic_slice_in_dim(w_down, side * down_half, down_half, 0), w_out], axis=0
    )
    narrow = after(narrow, mine[-1])
    wide = lax.all_gather(wide, "shard", axis=0, tiled=True)
    narrow = lax.all_gather(narrow, "shard", axis=0, tiled=False)

    tables = rope_tables(rope_pos)
    cycle = jnp.arange(cycle_size, dtype=jnp.int32)
    at_slot = jnp.sum(
        jnp.where(
            block_slot[:, :, None] == cycle[None, None, :],
            (cycle ^ cycle_index)[None, :, None],
            0,
        ),
        axis=1,
    )
    own_slot = lax.dynamic_index_in_dim(block_slot, cycle_index, 1, keepdims=True)
    near_slot = lax.dynamic_index_in_dim(block_slot, cycle_index ^ 1, 1, keepdims=True)
    info = jnp.concatenate(
        [
            at_slot,
            jnp.minimum(own_slot, near_slot),
            jnp.maximum(own_slot, near_slot),
            (near_slot > own_slot).astype(jnp.int32),
        ],
        axis=1,
    ).astype(jnp.int32)

    half = block_len // 2

    def halves(value, second):
        starts = range(second * half, row_count, block_len)
        return jnp.concatenate([value[:, at : at + half] for at in starts], axis=1)

    turns = jnp.concatenate(tables[:2], axis=0)
    turns_got = flip(halves(turns, 1), 1)
    turns = halves(turns, 0)
    turns = (turns[:HALF], turns[HALF:], turns_got[:HALF], turns_got[HALF:])

    flat_in = hidden_in.reshape(row_count, width)
    q_kept, q_sent, kv, normed_attn, full_packed, gains = entry(
        place, pieces, flat_in, tables, block_len
    )
    q_got = flip(q_sent, 1)
    blocks = gather_flipped(kv)
    attended = [attend(info, q_kept, q_got, blocks, g) for g in range(KV_HEADS)]
    back = [flip(a[2], 1) for a in attended]

    side_ref = side.reshape(1).astype(jnp.int32)
    other_wide = flip(wide, 1)
    other_down = flip(narrow[:, :down_half], 1)
    full_out = narrow[:, down_half:].reshape(width, width)
    (
        block_out,
        middle_grad,
        dout_kept,
        dout_sent,
        wide_kept,
        wide_sent,
        narrow_kept,
        narrow_sent,
        gain_mlp_grad,
    ) = middle(
        side_ref,
        [a[1] for a in attended],
        back,
        flat_in,
        out_grad.reshape(row_count, width),
        gains,
        wide,
        other_wide,
        narrow,
        other_down,
        full_out,
        block_len,
    )

    dout_got = flip(dout_sent, 1)
    early_wide = add_sent(wide_kept, flip(wide_sent, 1))
    early_narrow = add_sent(narrow_kept, flip(narrow_sent, 1))
    early_wide, early_narrow, dout_kept = lax.optimization_barrier(
        (early_wide, early_narrow, dout_kept)
    )
    early_wide = lax.psum_scatter(early_wide, "shard", scatter_dimension=0, tiled=True)
    early_narrow = lax.psum_scatter(early_narrow, "shard", scatter_dimension=0, tiled=False)

    dq_kept, dq_back = [], []
    dkv_parts = []
    for g in range(KV_HEADS):
        if g == KV_HEADS - 1:
            early_wide, early_narrow, dout_kept = lax.optimization_barrier(
                (early_wide, early_narrow, dout_kept)
            )
            sent_wide, sent_narrow = flip(early_wide, 2), flip(early_narrow, 4)
        kept, sent, *dkv_parts = attend_back(
            info,
            q_kept,
            q_got,
            dout_kept,
            dout_got,
            attended[g][0],
            attended[g][3],
            turns,
            blocks,
            g,
            dkv_parts,
        )
        dq_kept.append(kept)
        dq_back.append(flip(sent, 1))
    early_wide = add_sent(early_wide, sent_wide)
    early_narrow = add_sent(early_narrow, sent_narrow)
    early_wide = add_sent(early_wide, flip(early_wide, 4))
    early_narrow = add_sent(early_narrow, flip(early_narrow, 2))
    bit = 8
    while bit < cycle_size:
        early_wide = add_sent(early_wide, flip(early_wide, bit))
        early_narrow = add_sent(early_narrow, flip(early_narrow, bit))
        bit *= 2
    parts = scatter_flipped(dkv_parts)
    grad_query, attn_grad = exit_query(dq_kept, dq_back, normed_attn, full_packed, block_len)
    in_grad, late_kept, late_sent = leave(
        side_ref,
        parts,
        normed_attn,
        full_packed,
        grad_query,
        attn_grad,
        flat_in,
        middle_grad,
        gains,
        gain_mlp_grad,
        tables[2:],
        block_len,
    )
    in_grad = in_grad.reshape(hidden_in.shape)
    block_out = block_out.reshape(hidden_in.shape)
    kv_at = full_packed.shape[1] - KV_HEADS * PAIR
    late = add_sent(late_kept, flip(late_sent, 1)).reshape(shards, depth, cols)
    share = lambda by: lax.dynamic_index_in_dim(late, (shard_index + by) % shards, 0, keepdims=False)
    arrived = [shift(share(by), "shard", by) for by in range(1, shards)]
    late = sum((a.astype(F32) for a in arrived), share(0).astype(F32)).astype(BF16)
    bit = 2
    while bit < cycle_size:
        late = add_sent(late, flip(late, bit))
        bit *= 2
    other = flip(late, 1)
    late = jnp.where(
        side == 0,
        jnp.concatenate([late, other], axis=1),
        jnp.concatenate([other, late], axis=1),
    ).astype(F32)
    grad_key, grad_value = unpack_kv(late[:, kv_at:])
    other_wide = flip(early_wide, 1)
    down_own = early_narrow[:down_half]
    down_other = flip(down_own, 1)
    grad_down = jnp.where(
        side == 0,
        jnp.concatenate([down_own, down_other], axis=0),
        jnp.concatenate([down_other, down_own], axis=0),
    )
    return (
        block_out,
        in_grad,
        late[:, : HEADS * HEAD],
        grad_key,
        grad_value,
        early_narrow[down_half:].astype(F32),
        jnp.where(side == 0, early_wide, other_wide).astype(F32),
        jnp.where(side == 0, other_wide, early_wide).astype(F32),
        grad_down.astype(F32),
        late[:, HEADS * HEAD],
        late[:, HEADS * HEAD + 1],
    )


def solution(mesh):
    ctx, shards = mesh.shape["ctx"], mesh.shape["shard"]
    split_mesh = Mesh(mesh.devices.reshape(ctx // 4, 2, 2, shards), CTX + ("shard",))
    rows = P("shard", CTX, None)
    split = P("shard", None)
    return jax.shard_map(
        per_device,
        mesh=split_mesh,
        in_specs=(rows, rows, split, P("shard", CTX)) + (split,) * 7 + (P("shard"),) * 2,
        out_specs=(rows, rows) + (split,) * 7 + (P("shard"),) * 2,
        check_vma=False,
    )
```

```python
import functools

import jax
import jax.numpy as jnp
from jax import lax
from jax.experimental import pallas as pl
from jax.experimental.pallas import tpu as pltpu
from jax.sharding import Mesh
from jax.sharding import PartitionSpec as P

HEADS = 9
KV_HEADS = 3
HEAD = 64
GROUP = HEADS // KV_HEADS
PAIR = 2 * HEAD
HALF = HEAD // 2

NORM_EPSILON = 1e-05
ROPE_BASE = 100000.0
LOG2_E = 1.4426950408889634
LN_2 = 0.6931471805599453
MASKED_SCORE = -1e30
SUM_ROWS = 16
VMEM_BYTES = 56 * 1024 * 1024

CHIPS = ("cy", "cx")
CTX = CHIPS + ("core",)

F32 = jnp.float32
BF16 = jnp.bfloat16


def params():
    return pltpu.CompilerParams(vmem_limit_bytes=VMEM_BYTES)


def matmul(left, right):
    return jnp.dot(left, right, preferred_element_type=F32)


def matmul_lead(left, right):
    return lax.dot_general(left, right, (((0,), (0,)), ((), ())), preferred_element_type=F32)


def matmul_trail(left, right):
    return lax.dot_general(left, right, (((1,), (1,)), ((), ())), preferred_element_type=F32)


def flip(value, bit):
    peers = lax.axis_size(CTX)
    return lax.ppermute(value, CTX, [(i, i ^ bit) for i in range(peers)])


def shift(value, axis, by=1):
    peers = lax.axis_size(axis)
    return lax.ppermute(value, axis, [(i, (i + by) % peers) for i in range(peers)])


def ring_pieces(piece, axis):
    return [piece] + [shift(piece, axis, by) for by in range(1, lax.axis_size(axis))]


def after(value, *others):
    return lax.optimization_barrier((value,) + others)[0]


def gather_flipped(own, beside):
    peers = lax.axis_size(CTX)
    if peers == 8:
        by_x = flip(own, 2)
        by_y = flip(own, 4)
        near = flip(own, 1)
        result = beside(own, near)
        by_x, by_y, result = lax.optimization_barrier((by_x, by_y, result))
        first = flip(by_y[:1], 2)
        second = flip(by_x[1:], 4)
        same_core = [(own,), (by_x,), (by_y,), (first, second)]
        other_core = [(near,)] + [tuple(flip(a, 1) for a in block) for block in same_core[1:]]
        return result, [b for pair in zip(same_core, other_core) for b in pair]
    blocks = [own]
    bit = 1
    while bit < peers:
        blocks = blocks + [flip(b, bit) for b in blocks]
        bit *= 2
    return beside(blocks[0], blocks[1]), [(b,) for b in blocks]


def add_sent(kept, arrived):
    return (kept.astype(F32) + arrived.astype(F32)).astype(BF16)


def tied(value, *others):
    return lax.optimization_barrier((value,) + others)


def scatter_flipped(parts, info, steps):
    peers = len(parts) + 2
    result = ()
    if peers == 8:
        near = {k: flip(parts[k - 1], 1) for k in (6, 2, 4)}
        seq = lambda k, i: add_sent(parts[k - 2][i : i + 1], near[k][i : i + 1])
        info, *sent = tied(info, seq(6, 0), seq(2, 0), seq(6, 1), seq(4, 1))
        arrived = [flip(a, bit) for a, bit in zip(sent, (2, 2, 4, 4))]
        for step in steps[:-1]:
            result = step(info, result)
        result, *arrived = tied(result, *arrived)
        far_x, x_first, far_y, y_second = arrived
        info, y_sent, x_sent = tied(info, add_sent(seq(4, 0), far_x), add_sent(seq(2, 1), far_y))
        y_first, x_second = flip(y_sent, 4), flip(x_sent, 2)
        own, own_sent, *result = steps[-1](info, result)
        own = add_sent(own, flip(own_sent, 1))
        return result, [(own,), (x_first, x_second), (y_first, y_second)]
    for step in steps:
        result = step(info, result)
    own, own_sent, *result = result
    parts = [own, own_sent] + parts
    while peers > 1:
        peers //= 2
        parts = [add_sent(parts[k], flip(parts[k + peers], peers)) for k in range(peers)]
    return result, [(parts[0],)]


def entry_kernel(shards, width, place_ref, *refs):
    piece_refs = refs[: 2 * shards]
    (x_ref, cos_t_ref, sin_t_ref, cos_ref, low_ref, high_ref) = refs[2 * shards : 2 * shards + 6]
    kept_ref, sent_ref, kv_ref, normed_ref, packed_ref, gains_ref = refs[
        2 * shards + 6 : 2 * shards + 12
    ]
    (weight,) = refs[2 * shards + 12 :]
    half = kept_ref.shape[1]
    depth = piece_refs[0].shape[0]
    cols = piece_refs[0].shape[1]

    @pl.when(pl.program_id(0) == 0)
    def assemble():
        shard, side = place_ref[0], place_ref[1]
        for t in range(shards):
            row = pl.multiple_of(lax.rem(shard - t + shards, shards) * depth, 16)
            mine = pl.multiple_of(side * cols, 128)
            other = pl.multiple_of((1 - side) * cols, 128)
            weight[pl.ds(row, depth), pl.ds(mine, cols)] = piece_refs[t][...]
            weight[pl.ds(row, depth), pl.ds(other, cols)] = piece_refs[shards + t][...]
        packed_ref[...] = weight[...]
        gains_ref[...] = weight[:, 512:640].astype(F32).T[64:72, :]

    rows = x_ref[...].astype(F32)
    inverse = lax.rsqrt(jnp.mean(rows * rows, axis=-1, keepdims=True) + NORM_EPSILON)
    normed = (rows * inverse * gains_ref[0:1, :]).astype(BF16)
    normed_ref[...] = normed
    cos_t = cos_t_ref[...]
    sin_t = sin_t_ref[...]
    for chunk in range(5):
        lin = matmul(normed, weight[:, chunk * PAIR : (chunk + 1) * PAIR]).T
        for part in range(2):
            head = 2 * chunk + part
            if head < HEADS:
                first = lin[part * HEAD : part * HEAD + HALF]
                second = lin[part * HEAD + HALF : (part + 1) * HEAD]
                turned = jnp.concatenate(
                    [first * cos_t - second * sin_t, second * cos_t + first * sin_t], axis=0
                )
                turned = (turned * (0.125 * LOG2_E)).astype(BF16)
                kept_ref[head * HEAD : (head + 1) * HEAD, :] = turned[:, :half]
                sent_ref[head * HEAD : (head + 1) * HEAD, :] = turned[:, half:]
    for group in range(KV_HEADS):
        at = 5 * PAIR + group * PAIR
        lin = matmul(normed, weight[:, at : at + PAIR])
        turned = (
            lin * cos_ref[...]
            + pltpu.roll(lin, HALF, 1) * low_ref[...]
            + pltpu.roll(lin, PAIR - HALF, 1) * high_ref[...]
        )
        kv_ref[0, group] = turned.astype(BF16)


def choose(refs, seq):
    if len(refs) == 1:
        return refs[0][...]
    return jnp.where(seq == 0, refs[0][...], refs[1][...])


def entry(place, pieces, inputs, tables, block_len):
    shards = len(pieces) // 2
    rows, width = inputs.shape
    cos_t, sin_t, cos, low, high = tables
    depth, cols = pieces[0].shape
    steps = rows // block_len
    fixed = lambda shape: pl.BlockSpec(shape, lambda s, place: (0,) * len(shape))
    return pl.pallas_call(
        functools.partial(entry_kernel, shards, width),
        grid_spec=pltpu.PrefetchScalarGridSpec(
            num_scalar_prefetch=1,
            grid=(steps,),
            in_specs=[fixed((depth, cols)) for _ in pieces]
            + [pl.BlockSpec((block_len, width), lambda s, place: (s, 0))]
            + [pl.BlockSpec((HALF, block_len), lambda s, place: (0, s))] * 2
            + [pl.BlockSpec((block_len, PAIR), lambda s, place: (s, 0))] * 3,
            out_specs=[
                pl.BlockSpec((HEADS * HEAD, block_len // 2), lambda s, place: (0, s)),
                pl.BlockSpec((HEADS * HEAD, block_len // 2), lambda s, place: (0, s)),
                pl.BlockSpec((1, KV_HEADS, block_len, PAIR), lambda s, place: (s, 0, 0, 0)),
                pl.BlockSpec((block_len, width), lambda s, place: (s, 0)),
                fixed((width, 2 * cols)),
                fixed((8, width)),
            ],
            scratch_shapes=[pltpu.VMEM((width, 2 * cols), BF16)],
        ),
        out_shape=[
            jax.ShapeDtypeStruct((HEADS * HEAD, rows // 2), BF16),
            jax.ShapeDtypeStruct((HEADS * HEAD, rows // 2), BF16),
            jax.ShapeDtypeStruct((steps, KV_HEADS, block_len, PAIR), BF16),
            jax.ShapeDtypeStruct((rows, width), BF16),
            jax.ShapeDtypeStruct((width, 2 * cols), BF16),
            jax.ShapeDtypeStruct((8, width), F32),
        ],
        compiler_params=params(),
        name="entry",
    )(place, *pieces, inputs, cos_t, sin_t, cos, low, high)


def key_mask(keys, queries, first_query):
    key = lax.broadcasted_iota(jnp.int32, (keys, queries), 0)
    query = lax.broadcasted_iota(jnp.int32, (keys, queries), 1)
    return key <= query + first_query


def own_visits(peers, info_ref, seq, half, visit):
    visit(0, pl.ds(0, half), half, half, 0)
    visit(1, pl.ds(half, half), half, 2 * half, half)
    later = info_ref[seq, peers + 2]
    visit(1 - later, pl.ds(pl.multiple_of(later * half, 128), half), half, 2 * half, None)


def other_visits(peers, info_ref, seq, half, visit):
    first, second = info_ref[seq, peers], info_ref[seq, peers + 1]

    @pl.loop(0, first)
    def _(r):
        visit(info_ref[seq, r], pl.ds(0, 2 * half), 2 * half, 2 * half, None)

    @pl.loop(first + 1, second)
    def _(r):
        start = pl.multiple_of(info_ref[seq, peers + 2] * half, 128)
        visit(info_ref[seq, r], pl.ds(start, half), half, 2 * half, None)


def load_blocks(blocks, counts, refs, seq):
    at = 0
    for k, count in enumerate(counts):
        blocks[k] = choose(refs[at : at + count], seq)[0, 0]
        at += count


def load_queries(queries, kept_ref, got_ref):
    half = kept_ref.shape[1]
    for h in range(GROUP):
        head = slice(h * HEAD, (h + 1) * HEAD)
        queries[h, :HEAD, :half] = kept_ref[head, :]
        queries[h, :HEAD, half:] = got_ref[head, :]
        queries[h, HEAD:, :] = jnp.zeros((HEAD, 2 * half), BF16)


def forward_visit(blocks, queries, row_max, total, k, lanes, width, keys, diagonal):
    kv = blocks[k, :keys, :]
    values_t = jnp.concatenate([kv.T[HEAD:], jnp.ones((SUM_ROWS, keys), BF16)], axis=0)
    scores = [matmul(kv, queries[h, :, lanes]) for h in range(GROUP)]
    if diagonal is not None:
        mask = key_mask(keys, width, diagonal)
        scores = [jnp.where(mask, a, MASKED_SCORE) for a in scores]
    weights, fading = [], []
    for h in range(GROUP):
        new_max = jnp.max(scores[h], axis=0, keepdims=True)
        if diagonal is None:
            old_max = row_max[h, :, lanes]
            new_max = jnp.maximum(old_max, new_max)
            fading.append(jnp.exp2(old_max - new_max))
        row_max[h, :, lanes] = new_max
        weights.append(jnp.exp2(scores[h] - new_max).astype(BF16))
    for h in range(GROUP):
        product = matmul(values_t, weights[h])
        if diagonal is None:
            product = total[h, :, lanes] * fading[h] + product
        total[h, :, lanes] = product


def near_kernel(peers, info_ref, kept_ref, got_ref, own_ref, near_ref, max_ref, total_ref, blocks, queries):
    seq = pl.program_id(0)
    half = kept_ref.shape[1]
    blocks[0] = own_ref[0, 0]
    blocks[1] = near_ref[0, 0]
    load_queries(queries, kept_ref, got_ref)
    visit = functools.partial(forward_visit, blocks, queries, max_ref.at[0], total_ref.at[0])
    own_visits(peers, info_ref, seq, half, visit)


def attend_near(info, kept, got, own, near):
    steps, _, block_len, _ = own.shape
    peers = info.shape[1] - 3
    half = block_len // 2
    size = GROUP * HEAD
    height = HEAD + SUM_ROWS
    queries = pl.BlockSpec((size, half), lambda s, g, info: (g, s))
    block = pl.BlockSpec((1, 1, block_len, PAIR), lambda s, g, info: (s, g, 0, 0))
    state = lambda height: pl.BlockSpec(
        (1, GROUP, height, block_len), lambda s, g, info: (g, 0, 0, s)
    )
    work = steps * HEADS * block_len * block_len
    return pl.pallas_call(
        functools.partial(near_kernel, peers),
        grid_spec=pltpu.PrefetchScalarGridSpec(
            num_scalar_prefetch=1,
            grid=(steps, KV_HEADS),
            in_specs=[queries, queries, block, block],
            out_specs=[state(1), state(height)],
            scratch_shapes=[
                pltpu.VMEM((2, block_len, PAIR), BF16),
                pltpu.VMEM((GROUP, PAIR, block_len), BF16),
            ],
        ),
        out_shape=[
            jax.ShapeDtypeStruct((KV_HEADS, GROUP, 1, steps * block_len), F32),
            jax.ShapeDtypeStruct((KV_HEADS, GROUP, height, steps * block_len), F32),
        ],
        compiler_params=params(),
        cost_estimate=pl.CostEstimate(
            flops=2 * 2 * 256 * work, bytes_accessed=8 * 1024 * 1024, transcendentals=work
        ),
        name="attend_near",
    )(info, kept, got, own, near)


def forward_kernel(counts, info_ref, kept_ref, got_ref, near_max, near_total, *refs):
    peers, arrays = len(counts), sum(counts)
    kv_refs = refs[:arrays]
    out_ref, kept16_ref, got16_ref, lse_ref = refs[arrays : arrays + 4]
    blocks, queries, row_max, total = refs[arrays + 4 :]
    seq = pl.program_id(0)
    half = kept_ref.shape[1]
    load_blocks(blocks, counts, kv_refs, seq)
    load_queries(queries, kept_ref, got_ref)
    row_max[...] = near_max[0]
    total[...] = near_total[0]
    visit = functools.partial(forward_visit, blocks, queries, row_max, total)
    other_visits(peers, info_ref, seq, half, visit)
    for h in range(GROUP):
        head = slice(h * HEAD, (h + 1) * HEAD)
        row_sum = total[h, HEAD : HEAD + 1, :]
        result = total[h, :HEAD, :] / row_sum
        out_ref[head, :] = result
        kept16_ref[head, :] = result[:, :half].astype(BF16)
        got16_ref[head, :] = result[:, half:].astype(BF16)
        lse_ref[h : h + 1, :] = row_max[h] + jnp.log2(row_sum)


def attention_specs(group, half):
    across = lambda height: pl.BlockSpec((height, 2 * half), lambda s, info: (0, s))
    across_half = lambda height, at=0: pl.BlockSpec((height, half), lambda s, info: (at, s))

    def block(whole):
        return pl.BlockSpec(
            (1, 1, 2 * half, PAIR), lambda s, info: (s if whole else 0, group, 0, 0)
        )

    return across, across_half, block


def attend(info, kept, got, near, blocks, group):
    peers = len(blocks)
    counts = tuple(len(b) for b in blocks)
    arrays = [a for b in blocks for a in b]
    steps, _, block_len, _ = arrays[0].shape
    half = block_len // 2
    rows = steps * block_len
    size = GROUP * HEAD
    across, across_half, block = attention_specs(group, half)
    work = steps * GROUP * block_len * peers * block_len
    return pl.pallas_call(
        functools.partial(forward_kernel, counts),
        grid_spec=pltpu.PrefetchScalarGridSpec(
            num_scalar_prefetch=1,
            grid=(steps,),
            in_specs=[across_half(size, group)] * 2
            + [
                pl.BlockSpec((1, GROUP, a.shape[2], block_len), lambda s, info: (group, 0, 0, s))
                for a in near
            ]
            + [block(len(b) == 1) for b in blocks for _ in b],
            out_specs=[across(size), across_half(size), across_half(size), across(8)],
            scratch_shapes=[
                pltpu.VMEM((peers, block_len, PAIR), BF16),
                pltpu.VMEM((GROUP, PAIR, block_len), BF16),
                pltpu.VMEM((GROUP, 1, block_len), F32),
                pltpu.VMEM((GROUP, HEAD + SUM_ROWS, block_len), F32),
            ],
        ),
        out_shape=[
            jax.ShapeDtypeStruct((size, rows), F32),
            jax.ShapeDtypeStruct((size, rows // 2), BF16),
            jax.ShapeDtypeStruct((size, rows // 2), BF16),
            jax.ShapeDtypeStruct((8, rows), F32),
        ],
        compiler_params=params(),
        cost_estimate=pl.CostEstimate(
            flops=2 * 2 * 256 * work, bytes_accessed=4 * size * rows, transcendentals=work
        ),
        name="attend",
    )(info, kept, got, *near, *arrays)


def backward_kernel(near, counts, shared, info_ref, *refs):
    count, arrays = len(counts), sum(counts)
    (kept_ref, got_ref, dkept_ref, dgot_ref, out_ref, lse_ref) = refs[:6]
    refs = refs[6:]
    if near:
        (cos_kept, sin_kept, cos_got, sin_got, dq_in) = refs[:5]
        refs = refs[5:]
    kv_refs = refs[:arrays]
    dq_refs = refs[arrays + shared : arrays + shared + (2 if near else 1)]
    refs = refs[arrays + shared + len(dq_refs) :]
    dkv_refs = refs[:count]
    blocks, grads, queries, douts, delta, dq = refs[count:]
    seq = pl.program_id(0)
    half = kept_ref.shape[1]
    peers = info_ref.shape[1] - 3
    load_blocks(blocks, counts, kv_refs, seq)
    for k in range(count):
        grads[k] = jnp.zeros((PAIR, 2 * half), F32)
    for h in range(GROUP):
        head = slice(h * HEAD, (h + 1) * HEAD)
        zeros = jnp.zeros((HEAD, 2 * half), BF16)
        dout = jnp.concatenate([dkept_ref[head, :], dgot_ref[head, :]], axis=1)
        queries[h, :HEAD, :half] = kept_ref[head, :]
        queries[h, :HEAD, half:] = got_ref[head, :]
        queries[h, HEAD:, :] = zeros
        douts[h, :HEAD, :] = zeros
        douts[h, HEAD:, :] = dout
        delta[h] = jnp.sum(dout.astype(F32) * out_ref[head, :], axis=0, keepdims=True)
        dq[h] = dq_in[h] if near else jnp.zeros((HEAD, 2 * half), F32)

    def visit(k, lanes, width, keys, diagonal):
        k = k if near else k - 2
        kv = blocks[k, :keys, :]
        keys_t = kv.T[:HEAD]
        heads = range(GROUP)
        scores = [matmul(kv, queries[h, :, lanes]) for h in heads]
        dprobs = [matmul(kv, douts[h, :, lanes]) for h in heads]
        probs = [jnp.exp2(scores[h] - lse_ref[h : h + 1, lanes]) for h in heads]
        if diagonal is not None:
            mask = key_mask(keys, width, diagonal)
            probs = [jnp.where(mask, a, 0.0) for a in probs]
        dscores = [(probs[h] * (dprobs[h] - delta[h, :, lanes])).astype(BF16) for h in heads]
        probs = [a.astype(BF16) for a in probs]
        dkeys = sum(matmul_trail(queries[h, :HEAD, lanes], dscores[h]) for h in heads)
        dvalues = sum(matmul_trail(douts[h, HEAD:, lanes], probs[h]) for h in heads)
        grads[k, :HEAD, :keys] += dkeys
        grads[k, HEAD:, :keys] += dvalues
        for h in heads:
            dq[h, :, lanes] += matmul(keys_t, dscores[h])

    row = lax.broadcasted_iota(jnp.int32, (PAIR, 1), 0)
    unit = jnp.where(row < HEAD, LN_2, 1.0)
    if near:
        own_visits(peers, info_ref, seq, half, visit)
    else:
        other_visits(peers, info_ref, seq, half, visit)
    for k in range(count):
        dkv_refs[k][0, 0] = (grads[k] * unit).astype(BF16).T
    if not near:
        dq_refs[0][...] = dq[...]
        return
    for h in range(GROUP):
        for at, dq_ref, cos_ref, sin_ref in (
            (0, dq_refs[0], cos_kept, sin_kept),
            (half, dq_refs[1], cos_got, sin_got),
        ):
            first = dq[h, :HALF, at : at + half] * 0.125
            second = dq[h, HALF:, at : at + half] * 0.125
            cos, sin = cos_ref[...], sin_ref[...]
            dq_ref[h * HEAD : h * HEAD + HALF, :] = (first * cos + second * sin).astype(BF16)
            dq_ref[h * HEAD + HALF : (h + 1) * HEAD, :] = (second * cos - first * sin).astype(BF16)


def attend_back(near, info, rows_in, extra, blocks, group, shared):
    count = len(blocks)
    counts = tuple(len(b) for b in blocks)
    arrays = [a for b in blocks for a in b]
    steps, _, block_len, _ = arrays[0].shape
    steps = info.shape[0]
    half = block_len // 2
    rows = steps * block_len
    size = GROUP * HEAD
    across, across_half, block = attention_specs(group, half)
    state = pl.BlockSpec((GROUP, HEAD, block_len), lambda s, info: (0, 0, s))
    pair_t = pltpu.VMEM((GROUP, PAIR, block_len), BF16)
    work = steps * GROUP * block_len * count * block_len
    inputs = (info, *rows_in, *extra, *arrays)
    if near:
        dq_specs = [across_half(size)] * 2
        dq_shapes = [jax.ShapeDtypeStruct((size, rows // 2), BF16)] * 2
    else:
        dq_specs = [state]
        dq_shapes = [jax.ShapeDtypeStruct((GROUP, HEAD, rows), F32)]
    return pl.pallas_call(
        functools.partial(backward_kernel, near, counts, len(shared)),
        grid_spec=pltpu.PrefetchScalarGridSpec(
            num_scalar_prefetch=1,
            grid=(steps,),
            in_specs=[across_half(size, group)] * 4
            + [across(size), across(8)]
            + ([across_half(HALF)] * 4 + [state] if near else [])
            + [block(len(b) == 1) for b in blocks for _ in b]
            + [pl.BlockSpec(memory_space=pl.ANY)] * len(shared),
            out_specs=dq_specs + [block(True)] * count,
            scratch_shapes=[
                pltpu.VMEM((count, block_len, PAIR), BF16),
                pltpu.VMEM((count, PAIR, block_len), F32),
                pair_t,
                pair_t,
                pltpu.VMEM((GROUP, 1, block_len), F32),
                pltpu.VMEM((GROUP, HEAD, block_len), F32),
            ],
        ),
        out_shape=dq_shapes
        + [jax.ShapeDtypeStruct((steps, KV_HEADS, block_len, PAIR), BF16)] * count,
        input_output_aliases={len(inputs) + i: len(dq_shapes) + i for i in range(len(shared))},
        compiler_params=params(),
        cost_estimate=pl.CostEstimate(
            flops=5 * 2 * 256 * work, bytes_accessed=4 * size * rows, transcendentals=work
        ),
        name="attend_back_near" if near else "attend_back",
    )(*inputs, *shared)


def norm_back(rows, inverse, gain, grad):
    scaled = grad * gain
    mean = jnp.mean(scaled * rows, axis=-1, keepdims=True)
    row_grad = inverse * scaled - rows * (inverse * inverse * inverse) * mean
    return row_grad, jnp.sum(grad * rows * inverse, axis=0, keepdims=True)


def middle_kernel(down_half, half, chunk, side_ref, *refs):
    kept_refs, back_refs = refs[:KV_HEADS], refs[KV_HEADS : 2 * KV_HEADS]
    x_ref, dy_ref, gains_ref, mine_ref, other_ref = refs[2 * KV_HEADS : 2 * KV_HEADS + 5]
    (
        out_ref,
        dh_ref,
        dkept_ref,
        dsent_ref,
        wide_kept,
        wide_sent,
        narrow_kept,
        narrow_sent,
        gain_ref,
    ) = refs[2 * KV_HEADS + 5 : 2 * KV_HEADS + 14]
    ff_weight, down_weight, out_weight, mixed, ff_grad, down_grad = refs[2 * KV_HEADS + 14 :]
    shards = mine_ref.shape[0]
    hidden_width = ff_weight.shape[2]
    width = x_ref.shape[1]
    depth = width // shards
    half_hidden = hidden_width // 2
    size = GROUP * HEAD
    side = side_ref[0]
    for z in range(shards):
        for ref, owner in ((mine_ref, side), (other_ref, 1 - side)):
            here = slice(z * depth, (z + 1) * depth)
            ff_weight[owner, here, :half_hidden] = ref[z, :depth, :]
            ff_weight[owner, here, half_hidden:] = ref[z, depth : 2 * depth, :]
            down_at = pl.multiple_of((2 * z + owner) * down_half, 16)
            down_weight[pl.ds(down_at, down_half), :] = ref[
                z, 2 * depth : 2 * depth + down_half, :width
            ]
        out_weight[here, :] = mine_ref[z, 2 * depth + down_half :, :width]
    starts = range(0, kept_refs[0].shape[1], half)
    for g in range(KV_HEADS):
        for at in starts:
            rows = slice(g * size, (g + 1) * size)
            mixed[rows, 2 * at : 2 * at + half] = kept_refs[g][:, at : at + half]
            mixed[rows, 2 * at + half : 2 * at + 2 * half] = back_refs[g][:, at : at + half]
    weight_out = out_weight[...]
    gain = gains_ref[1:2, :]
    rows = x_ref[...].astype(F32) + matmul_lead(mixed[...], weight_out)
    inverse = lax.rsqrt(jnp.mean(rows * rows, axis=-1, keepdims=True) + NORM_EPSILON)
    normed = (rows * inverse * gain).astype(BF16)
    normed_t = normed.T
    dy = dy_ref[...]
    result = rows
    dnormed = jnp.zeros(rows.shape, F32)
    for at in range(0, hidden_width, chunk):
        part = slice(at, at + chunk)
        gate = matmul(normed, ff_weight[0, :, part])
        upward = matmul(normed, ff_weight[1, :, part])
        dhidden = matmul_trail(dy, down_weight[part, :])
        sigmoid = jax.nn.sigmoid(gate)
        silu = gate * sigmoid
        hidden = (silu * upward).astype(BF16)
        dgate = (dhidden * upward * sigmoid * (1.0 + gate * (1.0 - sigmoid))).astype(BF16)
        dup = (dhidden * silu).astype(BF16)
        result = result + matmul(hidden, down_weight[part, :])
        down_grad[part, :] = matmul_lead(hidden, dy).astype(BF16)
        ff_grad[0, :, part] = matmul(normed_t, dgate).astype(BF16)
        ff_grad[1, :, part] = matmul(normed_t, dup).astype(BF16)
        dnormed = dnormed + (
            matmul_trail(dgate, ff_weight[0, :, part]) + matmul_trail(dup, ff_weight[1, :, part])
        )
    out_ref[...] = result.astype(BF16)
    row_grad, gain_grad = norm_back(rows, inverse, gain, dnormed)
    gain_ref[...] = jnp.broadcast_to(gain_grad, gain_ref.shape)
    drows = dy.astype(F32) + row_grad
    dh_ref[...] = drows
    drows = drows.astype(BF16)
    out_grad = matmul(mixed[...], drows).astype(BF16)
    dout = matmul_trail(weight_out, drows).astype(BF16)
    for at in starts:
        dkept_ref[:, at : at + half] = dout[:, 2 * at : 2 * at + half]
        dsent_ref[:, at : at + half] = dout[:, 2 * at + half : 2 * at + 2 * half]
    wide_kept[...] = ff_grad[side]
    wide_sent[...] = ff_grad[1 - side]
    for z in range(shards):
        mine = pl.multiple_of((2 * z + side) * down_half, 16)
        other = pl.multiple_of((2 * z + 1 - side) * down_half, 16)
        narrow_kept[z, :down_half, :] = down_grad[pl.ds(mine, down_half), :]
        narrow_sent[z, :down_half, :] = down_grad[pl.ds(other, down_half), :]
        out_rows = out_grad[z * depth : (z + 1) * depth, :]
        narrow_kept[z, down_half:, :] = out_rows
        narrow_sent[z, down_half:, :] = out_rows


def middle(side, kept, back, inputs, dy, gains, mine, other, block_len, chunk=512):
    rows, width = inputs.shape
    shards, packed_rows, half_hidden = mine.shape
    hidden_width = 2 * half_hidden
    down_half = hidden_width // shards // 2
    wide = (width, hidden_width)
    narrow = (shards, packed_rows - 2 * width // shards, width)
    half = block_len // 2
    shape = jax.ShapeDtypeStruct
    work = 3 * 2 * rows * width * (3 * hidden_width + width)
    vmem = pl.BlockSpec(memory_space=pltpu.VMEM)
    return pl.pallas_call(
        functools.partial(middle_kernel, down_half, half, chunk),
        in_specs=[pl.BlockSpec(memory_space=pltpu.SMEM)] + [vmem] * (2 * KV_HEADS + 5),
        out_specs=[vmem] * 9,
        scratch_shapes=[
            pltpu.VMEM((2, width, hidden_width), BF16),
            pltpu.VMEM((hidden_width, width), BF16),
            pltpu.VMEM((HEADS * HEAD, width), BF16),
            pltpu.VMEM((HEADS * HEAD, rows), BF16),
            pltpu.VMEM((2, width, hidden_width), BF16),
            pltpu.VMEM((hidden_width, width), BF16),
        ],
        out_shape=[
            shape((rows, width), BF16),
            shape((rows, width), F32),
            shape((HEADS * HEAD, rows // 2), BF16),
            shape((HEADS * HEAD, rows // 2), BF16),
            shape(wide, BF16),
            shape(wide, BF16),
            shape(narrow, BF16),
            shape(narrow, BF16),
            shape(gains.shape, F32),
        ],
        compiler_params=params(),
        cost_estimate=pl.CostEstimate(
            flops=work, bytes_accessed=30 * 1024 * 1024, transcendentals=rows * hidden_width
        ),
        name="middle",
    )(side, *kept, *back, inputs, dy, gains, mine, other)


def exit_query_kernel(*refs):
    kept_refs, back_refs = refs[:KV_HEADS], refs[KV_HEADS : 2 * KV_HEADS]
    normed_ref, weight_ref, grad_ref, da_ref, dq = refs[2 * KV_HEADS :]
    half = kept_refs[0].shape[1]
    size = GROUP * HEAD
    for g in range(KV_HEADS):
        dq[g * size : (g + 1) * size, :half] = kept_refs[g][...]
        dq[g * size : (g + 1) * size, half:] = back_refs[g][...]
    rows = dq[...].T
    da_ref[...] = matmul_trail(rows, weight_ref[:, : HEADS * HEAD])
    grad = matmul_lead(normed_ref[...], rows)

    @pl.when(pl.program_id(0) == 0)
    def _():
        grad_ref[...] = grad

    @pl.when(pl.program_id(0) > 0)
    def _():
        grad_ref[...] += grad


def exit_query(kept, back, normed, weight, block_len):
    rows, width = normed.shape
    size = GROUP * HEAD
    half = block_len // 2
    down = pl.BlockSpec((block_len, width), lambda s: (s, 0))
    return pl.pallas_call(
        exit_query_kernel,
        grid=(rows // block_len,),
        in_specs=[pl.BlockSpec((size, half), lambda s: (0, s))] * (2 * KV_HEADS)
        + [down, pl.BlockSpec(weight.shape, lambda s: (0, 0))],
        out_specs=[pl.BlockSpec((width, HEADS * HEAD), lambda s: (0, 0)), down],
        out_shape=[
            jax.ShapeDtypeStruct((width, HEADS * HEAD), F32),
            jax.ShapeDtypeStruct((rows, width), F32),
        ],
        scratch_shapes=[pltpu.VMEM((HEADS * HEAD, block_len), BF16)],
        compiler_params=params(),
        name="exit_query",
    )(*kept, *back, normed, weight)


def exit_kernel(counts, side_ref, *refs):
    arrays = sum(counts)
    part_refs = refs[:arrays]
    (normed_ref, weight_ref, gq_ref, da_ref, x_ref, dh_ref, gains_ref, gain_mlp_ref) = refs[
        arrays : arrays + 8
    ]
    cos_ref, low_ref, high_ref, dx_ref, kept_ref, sent_ref, grad, gain_acc = refs[arrays + 8 :]
    step = pl.program_id(0)
    side = side_ref[0]
    cols = kept_ref.shape[1]
    wide = HEADS * HEAD

    @pl.when(step == 0)
    def _():
        grad[...] = jnp.zeros(grad.shape, F32)
        gain_acc[...] = jnp.zeros(gain_acc.shape, F32)

    parts = []
    at = 0
    for count in counts:
        parts.append(choose(part_refs[at : at + count], step))
        at += count
    normed = normed_ref[...]
    dnormed = da_ref[...]
    kv_at = weight_ref.shape[1] - KV_HEADS * PAIR
    for g in range(KV_HEADS):
        dkv = sum((part[0, g].astype(F32) for part in parts[1:]), parts[0][0, g].astype(F32))
        turned = (
            dkv * cos_ref[...]
            - pltpu.roll(dkv, HALF, 1) * low_ref[...]
            - pltpu.roll(dkv, PAIR - HALF, 1) * high_ref[...]
        ).astype(BF16)
        here = slice(kv_at + g * PAIR, kv_at + (g + 1) * PAIR)
        dnormed = dnormed + matmul_trail(turned, weight_ref[:, here])
        grad[:, g * PAIR : (g + 1) * PAIR] += matmul_lead(normed, turned)
    rows = x_ref[...].astype(F32)
    inverse = lax.rsqrt(jnp.mean(rows * rows, axis=-1, keepdims=True) + NORM_EPSILON)
    row_grad, gain_grad = norm_back(rows, inverse, gains_ref[0:1, :], dnormed)
    gain_acc[0:1, :] += gain_grad
    dx_ref[...] = (dh_ref[...] + row_grad).astype(BF16)

    @pl.when(step == pl.num_programs(0) - 1)
    def _():
        width = normed.shape[1]
        gains = jnp.concatenate(
            [
                jnp.zeros((HEAD, width), F32),
                gain_acc[0:1, :],
                gain_mlp_ref[0:1, :],
                jnp.zeros((HEAD - 2, width), F32),
            ],
            axis=0,
        ).T

        def write_low(ref):
            ref[...] = gq_ref[:, :cols].astype(BF16)

        def write_high(ref):
            ref[:, :PAIR] = gains.astype(BF16)
            ref[:, : wide - cols] = gq_ref[:, cols:].astype(BF16)
            ref[:, PAIR:] = grad[...].astype(BF16)

        @pl.when(side == 0)
        def _():
            write_low(kept_ref)
            write_high(sent_ref)

        @pl.when(side != 0)
        def _():
            write_high(kept_ref)
            write_low(sent_ref)


def leave(side, parts, normed, weight, grad_query, da, inputs, dh, gains, gain_mlp, tables, block_len):
    rows, width = normed.shape
    cols = weight.shape[1] // 2
    counts = tuple(len(p) for p in parts)
    arrays = [a for p in parts for a in p]
    down = pl.BlockSpec((block_len, width), lambda s, side: (s, 0))
    fixed = lambda shape: pl.BlockSpec(shape, lambda s, side: (0,) * len(shape))

    def block(whole):
        return pl.BlockSpec(
            (1, KV_HEADS, block_len, PAIR), lambda s, side: (s if whole else 0, 0, 0, 0)
        )

    table = pl.BlockSpec((block_len, PAIR), lambda s, side: (s, 0))
    return pl.pallas_call(
        functools.partial(exit_kernel, counts),
        grid_spec=pltpu.PrefetchScalarGridSpec(
            num_scalar_prefetch=1,
            grid=(rows // block_len,),
            in_specs=[block(len(p) == 1) for p in parts for _ in p]
            + [down, fixed(weight.shape), fixed(grad_query.shape), down, down, down]
            + [fixed(gains.shape), fixed(gain_mlp.shape)]
            + [table] * 3,
            out_specs=[down, fixed((width, cols)), fixed((width, cols))],
            scratch_shapes=[
                pltpu.VMEM((width, KV_HEADS * PAIR), F32),
                pltpu.VMEM((8, width), F32),
            ],
        ),
        out_shape=[
            jax.ShapeDtypeStruct((rows, width), BF16),
            jax.ShapeDtypeStruct((width, cols), BF16),
            jax.ShapeDtypeStruct((width, cols), BF16),
        ],
        compiler_params=params(),
        name="leave",
    )(side, *arrays, normed, weight, grad_query, da, inputs, dh, gains, gain_mlp, *tables)


def pack_kv(key_part, value_part):
    depth = key_part.shape[0]
    both = jnp.stack(
        [key_part.reshape(depth, KV_HEADS, HEAD), value_part.reshape(depth, KV_HEADS, HEAD)], axis=2
    )
    return both.reshape(depth, KV_HEADS * PAIR)


def unpack_kv(packed):
    depth = packed.shape[0]
    both = packed.reshape(depth, KV_HEADS, 2, HEAD)
    return (
        both[:, :, 0].reshape(depth, KV_HEADS * HEAD),
        both[:, :, 1].reshape(depth, KV_HEADS * HEAD),
    )


def rope_tables(positions):
    freqs = ROPE_BASE ** (-jnp.arange(HALF, dtype=F32) * 2.0 / HEAD)
    angle = positions.reshape(1, -1).astype(F32) * freqs[:, None]
    cos_t, sin_t = jnp.cos(angle), jnp.sin(angle)
    cos, sin = cos_t.T, sin_t.T
    nothing = jnp.zeros_like(cos)
    ones = jnp.ones_like(cos)
    return (
        cos_t,
        sin_t,
        jnp.concatenate([cos, cos, ones, ones], axis=1),
        jnp.concatenate([nothing, sin, nothing, nothing], axis=1),
        jnp.concatenate([-sin, nothing, nothing, nothing], axis=1),
    )


def per_device(
    hidden_in,
    out_grad,
    block_slot,
    rope_pos,
    w_query,
    w_key,
    w_value,
    w_out,
    w_gate,
    w_up,
    w_down,
    gain_attn,
    gain_mlp,
):
    seq_count, block_len, width = hidden_in.shape
    row_count = seq_count * block_len
    hidden_width = w_gate.shape[1]
    depth = w_query.shape[0]
    cycle_index = lax.axis_index(CTX)
    cycle_size = lax.axis_size(CTX)
    shard_index = lax.axis_index("shard")
    shards = lax.axis_size("shard")
    side = lax.axis_index("core")

    def whole(parts):
        rows = parts[0].shape[0]
        out = jnp.zeros((shards * rows,) + parts[0].shape[1:], parts[0].dtype)
        for t, part in enumerate(parts):
            out = lax.dynamic_update_slice_in_dim(out, part, ((shard_index - t) % shards) * rows, 0)
        return out

    packed = jnp.concatenate(
        [
            w_query,
            gain_attn[:, None],
            gain_mlp[:, None],
            jnp.zeros((depth, HEAD - 2), BF16),
            pack_kv(w_key, w_value),
        ],
        axis=1,
    )
    cols = packed.shape[1] // 2
    mine = ring_pieces(lax.dynamic_slice_in_dim(packed, side * cols, cols, 1), "shard")
    pieces = mine + [flip(a, 1) for a in mine]
    place = jnp.stack([shard_index, side]).astype(jnp.int32)
    if depth % 16:
        pieces = [whole(pieces[:shards]), whole(pieces[shards:])]
        place = jnp.stack([jnp.zeros_like(side), side]).astype(jnp.int32)

    down_half = w_down.shape[0] // 2
    half_hidden = hidden_width // 2
    wide = jnp.where(side == 0, w_gate, w_up)
    narrow = jnp.concatenate(
        [lax.dynamic_slice_in_dim(w_down, side * down_half, down_half, 0), w_out], axis=0
    )
    later_weights = jnp.concatenate(
        [
            wide[:, :half_hidden],
            wide[:, half_hidden:],
            jnp.pad(narrow, ((0, 0), (0, half_hidden - width))),
        ],
        axis=0,
    )
    later_weights = after(later_weights, *mine[1:])
    later_weights = lax.all_gather(later_weights, "shard", axis=0, tiled=False)

    tables = rope_tables(rope_pos)
    cycle = jnp.arange(cycle_size, dtype=jnp.int32)
    at_slot = jnp.sum(
        jnp.where(
            block_slot[:, :, None] == cycle[None, None, :],
            (cycle ^ cycle_index)[None, :, None],
            0,
        ),
        axis=1,
    )
    own_slot = lax.dynamic_index_in_dim(block_slot, cycle_index, 1, keepdims=True)
    near_slot = lax.dynamic_index_in_dim(block_slot, cycle_index ^ 1, 1, keepdims=True)
    info = jnp.concatenate(
        [
            at_slot,
            jnp.minimum(own_slot, near_slot),
            jnp.maximum(own_slot, near_slot),
            (near_slot > own_slot).astype(jnp.int32),
        ],
        axis=1,
    ).astype(jnp.int32)

    half = block_len // 2

    def halves(value, second):
        starts = range(second * half, row_count, block_len)
        return jnp.concatenate([value[:, at : at + half] for at in starts], axis=1)

    turns = jnp.concatenate(tables[:2], axis=0)
    turns_got = flip(halves(turns, 1), 1)
    turns = halves(turns, 0)
    turns = (turns[:HALF], turns[HALF:], turns_got[:HALF], turns_got[HALF:])

    flat_in = hidden_in.reshape(row_count, width)
    q_kept, q_sent, kv, normed_attn, full_packed, gains = entry(
        place, pieces, flat_in, tables, block_len
    )
    q_got = flip(q_sent, 1)
    near, blocks = gather_flipped(kv, functools.partial(attend_near, info, q_kept, q_got))
    attended = [attend(info, q_kept, q_got, near, blocks, g) for g in range(KV_HEADS)]
    back = [flip(a[2], 1) for a in attended]

    side_ref = side.reshape(1).astype(jnp.int32)
    (
        block_out,
        middle_grad,
        dout_kept,
        dout_sent,
        wide_kept,
        wide_sent,
        narrow_kept,
        narrow_sent,
        gain_mlp_grad,
    ) = middle(
        side_ref,
        [a[1] for a in attended],
        back,
        flat_in,
        out_grad.reshape(row_count, width),
        gains,
        later_weights,
        flip(later_weights, 1),
        block_len,
    )

    dout_got = flip(dout_sent, 1)
    wide_got = flip(wide_sent, 1)
    narrow_got = flip(narrow_sent, 1)
    rows_in = [
        (q_kept, q_got, dout_kept, dout_got, attended[g][0], attended[g][3])
        for g in range(KV_HEADS)
    ]
    dq_far = []
    parts = []
    for g in range(KV_HEADS):
        mine = rows_in[g]
        if g == 1:
            early_wide = add_sent(wide_kept, wide_got)
            early_narrow = add_sent(narrow_kept, narrow_got)
            early_wide, early_narrow, *mine = lax.optimization_barrier(
                (early_wide, early_narrow, *mine, *parts)
            )
            mine, parts = mine[:6], mine[6:]
            early_wide = lax.psum_scatter(early_wide, "shard", scatter_dimension=0, tiled=True)
            early_narrow = lax.psum_scatter(early_narrow, "shard", scatter_dimension=0, tiled=False)
        dq, *parts = attend_back(False, info, mine, (), blocks[2:], g, parts)
        dq_far.append(dq)

    def near_step(g, info, result):
        grads, dq = result[:2], result[2:]
        first, second, *grads = attend_back(
            True, info, rows_in[g], (*turns, dq_far[g]), blocks[:2], g, grads
        )
        return (*grads, *dq, first, flip(second, 1))

    steps = [functools.partial(near_step, g) for g in range(KV_HEADS)]
    dq, parts = scatter_flipped(parts, info, steps)
    dq_kept, dq_back = dq[0::2], dq[1::2]
    early_wide, early_narrow, *rest = tied(
        early_wide, early_narrow, *(a for p in parts for a in p)
    )
    parts = [tuple(rest.pop(0) for _ in p) for p in parts]
    wide_got, narrow_got = flip(early_wide, 2), flip(early_narrow, 4)
    grad_query, attn_grad = exit_query(dq_kept, dq_back, normed_attn, full_packed, block_len)
    in_grad, late_kept, late_sent = leave(
        side_ref,
        parts,
        normed_attn,
        full_packed,
        grad_query,
        attn_grad,
        flat_in,
        middle_grad,
        gains,
        gain_mlp_grad,
        tables[2:],
        block_len,
    )
    early_wide = add_sent(early_wide, wide_got)
    early_narrow = add_sent(early_narrow, narrow_got)
    early_wide, early_narrow, late_kept = tied(early_wide, early_narrow, late_kept)
    early_wide = add_sent(early_wide, flip(early_wide, 4))
    early_narrow = add_sent(early_narrow, flip(early_narrow, 2))
    bit = 8
    while bit < cycle_size:
        early_wide = add_sent(early_wide, flip(early_wide, bit))
        early_narrow = add_sent(early_narrow, flip(early_narrow, bit))
        bit *= 2
    in_grad = in_grad.reshape(hidden_in.shape)
    block_out = block_out.reshape(hidden_in.shape)
    kv_at = full_packed.shape[1] - KV_HEADS * PAIR
    late = add_sent(late_kept, flip(late_sent, 1)).reshape(shards, depth, cols)
    share = lambda by: lax.dynamic_index_in_dim(late, (shard_index + by) % shards, 0, keepdims=False)
    arrived = [shift(share(by), "shard", by) for by in range(1, shards)]
    late = sum((a.astype(F32) for a in arrived), share(0).astype(F32)).astype(BF16)
    bit = 2
    while bit < cycle_size:
        late = add_sent(late, flip(late, bit))
        bit *= 2
    other = flip(late, 1)
    late = jnp.where(
        side == 0,
        jnp.concatenate([late, other], axis=1),
        jnp.concatenate([other, late], axis=1),
    ).astype(F32)
    grad_key, grad_value = unpack_kv(late[:, kv_at:])
    other_wide = flip(early_wide, 1)
    down_own = early_narrow[:down_half]
    down_other = flip(down_own, 1)
    grad_down = jnp.where(
        side == 0,
        jnp.concatenate([down_own, down_other], axis=0),
        jnp.concatenate([down_other, down_own], axis=0),
    )
    return (
        block_out,
        in_grad,
        late[:, : HEADS * HEAD],
        grad_key,
        grad_value,
        early_narrow[down_half:].astype(F32),
        jnp.where(side == 0, early_wide, other_wide).astype(F32),
        jnp.where(side == 0, other_wide, early_wide).astype(F32),
        grad_down.astype(F32),
        late[:, HEADS * HEAD],
        late[:, HEADS * HEAD + 1],
    )


def solution(mesh):
    ctx, shards = mesh.shape["ctx"], mesh.shape["shard"]
    split_mesh = Mesh(mesh.devices.reshape(ctx // 4, 2, 2, shards), CTX + ("shard",))
    rows = P("shard", CTX, None)
    split = P("shard", None)
    return jax.shard_map(
        per_device,
        mesh=split_mesh,
        in_specs=(rows, rows, split, P("shard", CTX)) + (split,) * 7 + (P("shard"),) * 2,
        out_specs=(rows, rows) + (split,) * 7 + (P("shard"),) * 2,
        check_vma=False,
    )
```

```python
import functools

import jax
import jax.numpy as jnp
from jax import lax
from jax.experimental import pallas as pl
from jax.experimental.pallas import tpu as pltpu
from jax.sharding import Mesh
from jax.sharding import PartitionSpec as P

HEADS = 9
KV_HEADS = 3
HEAD = 64
GROUP = HEADS // KV_HEADS
PAIR = 2 * HEAD
HALF = HEAD // 2

NORM_EPSILON = 1e-05
ROPE_BASE = 100000.0
LOG2_E = 1.4426950408889634
LN_2 = 0.6931471805599453
MASKED_SCORE = -1e30
SUM_ROWS = 16
VMEM_BYTES = 56 * 1024 * 1024

CHIPS = ("cy", "cx")
CTX = CHIPS + ("core",)

F32 = jnp.float32
BF16 = jnp.bfloat16


def params():
    return pltpu.CompilerParams(vmem_limit_bytes=VMEM_BYTES)


def matmul(left, right):
    return jnp.dot(left, right, preferred_element_type=F32)


def matmul_lead(left, right):
    return lax.dot_general(left, right, (((0,), (0,)), ((), ())), preferred_element_type=F32)


def matmul_trail(left, right):
    return lax.dot_general(left, right, (((1,), (1,)), ((), ())), preferred_element_type=F32)


def flip(value, bit):
    peers = lax.axis_size(CTX)
    return lax.ppermute(value, CTX, [(i, i ^ bit) for i in range(peers)])


def shift(value, axis, by=1):
    peers = lax.axis_size(axis)
    return lax.ppermute(value, axis, [(i, (i + by) % peers) for i in range(peers)])


def ring_pieces(piece, axis):
    return [piece] + [shift(piece, axis, by) for by in range(1, lax.axis_size(axis))]


def after(value, *others):
    return lax.optimization_barrier((value,) + others)[0]


def gather_flipped(own, beside):
    peers = lax.axis_size(CTX)
    if peers == 8:
        by_x = flip(own, 2)
        by_y = flip(own, 4)
        near = flip(own, 1)
        result = beside(own, near)
        by_x, by_y, result = lax.optimization_barrier((by_x, by_y, result))
        first = flip(by_y[:1], 2)
        second = flip(by_x[1:], 4)
        same_core = [(own,), (by_x,), (by_y,), (first, second)]
        other_core = [(near,)] + [tuple(flip(a, 1) for a in block) for block in same_core[1:]]
        return result, [b for pair in zip(same_core, other_core) for b in pair]
    blocks = [own]
    bit = 1
    while bit < peers:
        blocks = blocks + [flip(b, bit) for b in blocks]
        bit *= 2
    return beside(blocks[0], blocks[1]), [(b,) for b in blocks]


def add_sent(kept, arrived):
    return (kept.astype(F32) + arrived.astype(F32)).astype(BF16)


def tied(value, *others):
    return lax.optimization_barrier((value,) + others)


def scatter_flipped(parts, info, steps):
    peers = len(parts) + 2
    result = ()
    if peers == 8:
        near = {k: flip(parts[k - 1], 1) for k in (6, 2, 4)}
        seq = lambda k, i: add_sent(parts[k - 2][i : i + 1], near[k][i : i + 1])
        info, *sent = tied(info, seq(6, 0), seq(2, 0), seq(6, 1), seq(4, 1))
        arrived = [flip(a, bit) for a, bit in zip(sent, (2, 2, 4, 4))]
        for step in steps[:-1]:
            result = step(info, result)
        result, *arrived = tied(result, *arrived)
        far_x, x_first, far_y, y_second = arrived
        info, y_sent, x_sent = tied(info, add_sent(seq(4, 0), far_x), add_sent(seq(2, 1), far_y))
        y_first, x_second = flip(y_sent, 4), flip(x_sent, 2)
        own, own_sent = steps[-1](info, result)
        own = add_sent(own, flip(own_sent, 1))
        return [(own,), (x_first, x_second), (y_first, y_second)]
    for step in steps:
        result = step(info, result)
    parts = list(result) + parts
    while peers > 1:
        peers //= 2
        parts = [add_sent(parts[k], flip(parts[k + peers], peers)) for k in range(peers)]
    return [(parts[0],)]


def entry_kernel(shards, width, place_ref, *refs):
    piece_refs = refs[: 2 * shards]
    (x_ref, cos_t_ref, sin_t_ref, cos_ref, low_ref, high_ref) = refs[2 * shards : 2 * shards + 6]
    kept_ref, sent_ref, kv_ref, normed_ref, packed_ref, gains_ref = refs[
        2 * shards + 6 : 2 * shards + 12
    ]
    (weight,) = refs[2 * shards + 12 :]
    half = kept_ref.shape[1]
    depth = piece_refs[0].shape[0]
    cols = piece_refs[0].shape[1]

    @pl.when(pl.program_id(0) == 0)
    def assemble():
        shard, side = place_ref[0], place_ref[1]
        for t in range(shards):
            row = pl.multiple_of(lax.rem(shard - t + shards, shards) * depth, 16)
            mine = pl.multiple_of(side * cols, 128)
            other = pl.multiple_of((1 - side) * cols, 128)
            weight[pl.ds(row, depth), pl.ds(mine, cols)] = piece_refs[t][...]
            weight[pl.ds(row, depth), pl.ds(other, cols)] = piece_refs[shards + t][...]
        packed_ref[...] = weight[...]
        gains_ref[...] = weight[:, 512:640].astype(F32).T[64:72, :]

    rows = x_ref[...].astype(F32)
    inverse = lax.rsqrt(jnp.mean(rows * rows, axis=-1, keepdims=True) + NORM_EPSILON)
    normed = (rows * inverse * gains_ref[0:1, :]).astype(BF16)
    normed_ref[...] = normed
    cos_t = cos_t_ref[...]
    sin_t = sin_t_ref[...]
    for chunk in range(5):
        lin = matmul(normed, weight[:, chunk * PAIR : (chunk + 1) * PAIR]).T
        for part in range(2):
            head = 2 * chunk + part
            if head < HEADS:
                first = lin[part * HEAD : part * HEAD + HALF]
                second = lin[part * HEAD + HALF : (part + 1) * HEAD]
                turned = jnp.concatenate(
                    [first * cos_t - second * sin_t, second * cos_t + first * sin_t], axis=0
                )
                turned = (turned * (0.125 * LOG2_E)).astype(BF16)
                kept_ref[head * HEAD : (head + 1) * HEAD, :] = turned[:, :half]
                sent_ref[head * HEAD : (head + 1) * HEAD, :] = turned[:, half:]
    for group in range(KV_HEADS):
        at = 5 * PAIR + group * PAIR
        lin = matmul(normed, weight[:, at : at + PAIR])
        turned = (
            lin * cos_ref[...]
            + pltpu.roll(lin, HALF, 1) * low_ref[...]
            + pltpu.roll(lin, PAIR - HALF, 1) * high_ref[...]
        )
        kv_ref[0, group] = turned.astype(BF16)


def choose(refs, seq):
    if len(refs) == 1:
        return refs[0][...]
    return jnp.where(seq == 0, refs[0][...], refs[1][...])


def entry(place, pieces, inputs, tables, block_len):
    shards = len(pieces) // 2
    rows, width = inputs.shape
    cos_t, sin_t, cos, low, high = tables
    depth, cols = pieces[0].shape
    steps = rows // block_len
    fixed = lambda shape: pl.BlockSpec(shape, lambda s, place: (0,) * len(shape))
    return pl.pallas_call(
        functools.partial(entry_kernel, shards, width),
        grid_spec=pltpu.PrefetchScalarGridSpec(
            num_scalar_prefetch=1,
            grid=(steps,),
            in_specs=[fixed((depth, cols)) for _ in pieces]
            + [pl.BlockSpec((block_len, width), lambda s, place: (s, 0))]
            + [pl.BlockSpec((HALF, block_len), lambda s, place: (0, s))] * 2
            + [pl.BlockSpec((block_len, PAIR), lambda s, place: (s, 0))] * 3,
            out_specs=[
                pl.BlockSpec((HEADS * HEAD, block_len // 2), lambda s, place: (0, s)),
                pl.BlockSpec((HEADS * HEAD, block_len // 2), lambda s, place: (0, s)),
                pl.BlockSpec((1, KV_HEADS, block_len, PAIR), lambda s, place: (s, 0, 0, 0)),
                pl.BlockSpec((block_len, width), lambda s, place: (s, 0)),
                fixed((width, 2 * cols)),
                fixed((8, width)),
            ],
            scratch_shapes=[pltpu.VMEM((width, 2 * cols), BF16)],
        ),
        out_shape=[
            jax.ShapeDtypeStruct((HEADS * HEAD, rows // 2), BF16),
            jax.ShapeDtypeStruct((HEADS * HEAD, rows // 2), BF16),
            jax.ShapeDtypeStruct((steps, KV_HEADS, block_len, PAIR), BF16),
            jax.ShapeDtypeStruct((rows, width), BF16),
            jax.ShapeDtypeStruct((width, 2 * cols), BF16),
            jax.ShapeDtypeStruct((8, width), F32),
        ],
        compiler_params=params(),
        name="entry",
    )(place, *pieces, inputs, cos_t, sin_t, cos, low, high)


def key_mask(keys, queries, first_query):
    key = lax.broadcasted_iota(jnp.int32, (keys, queries), 0)
    query = lax.broadcasted_iota(jnp.int32, (keys, queries), 1)
    return key <= query + first_query


def own_visits(peers, info_ref, seq, half, visit):
    visit(0, pl.ds(0, half), half, half, 0)
    visit(1, pl.ds(half, half), half, 2 * half, half)
    later = info_ref[seq, peers + 2]
    visit(1 - later, pl.ds(pl.multiple_of(later * half, 128), half), half, 2 * half, None)


def other_visits(peers, info_ref, seq, half, visit):
    first, second = info_ref[seq, peers], info_ref[seq, peers + 1]

    @pl.loop(0, first)
    def _(r):
        visit(info_ref[seq, r], pl.ds(0, 2 * half), 2 * half, 2 * half, None)

    @pl.loop(first + 1, second)
    def _(r):
        start = pl.multiple_of(info_ref[seq, peers + 2] * half, 128)
        visit(info_ref[seq, r], pl.ds(start, half), half, 2 * half, None)


def load_blocks(blocks, counts, refs, seq):
    at = 0
    for k, count in enumerate(counts):
        blocks[k] = choose(refs[at : at + count], seq)[0, 0]
        at += count


def load_queries(queries, kept_ref, got_ref):
    half = kept_ref.shape[1]
    for h in range(GROUP):
        head = slice(h * HEAD, (h + 1) * HEAD)
        queries[h, :HEAD, :half] = kept_ref[head, :]
        queries[h, :HEAD, half:] = got_ref[head, :]
        queries[h, HEAD:, :] = jnp.zeros((HEAD, 2 * half), BF16)


def forward_visit(blocks, queries, row_max, total, k, lanes, width, keys, diagonal):
    kv = blocks[k, :keys, :]
    values_t = jnp.concatenate([kv.T[HEAD:], jnp.ones((SUM_ROWS, keys), BF16)], axis=0)
    scores = [matmul(kv, queries[h, :, lanes]) for h in range(GROUP)]
    if diagonal is not None:
        mask = key_mask(keys, width, diagonal)
        scores = [jnp.where(mask, a, MASKED_SCORE) for a in scores]
    weights, fading = [], []
    for h in range(GROUP):
        new_max = jnp.max(scores[h], axis=0, keepdims=True)
        if diagonal is None:
            old_max = row_max[h, :, lanes]
            new_max = jnp.maximum(old_max, new_max)
            fading.append(jnp.exp2(old_max - new_max))
        row_max[h, :, lanes] = new_max
        weights.append(jnp.exp2(scores[h] - new_max).astype(BF16))
    for h in range(GROUP):
        product = matmul(values_t, weights[h])
        if diagonal is None:
            product = total[h, :, lanes] * fading[h] + product
        total[h, :, lanes] = product


def near_kernel(peers, info_ref, kept_ref, got_ref, own_ref, near_ref, max_ref, total_ref, blocks, queries):
    seq = pl.program_id(0)
    half = kept_ref.shape[1]
    blocks[0] = own_ref[0, 0]
    blocks[1] = near_ref[0, 0]
    load_queries(queries, kept_ref, got_ref)
    visit = functools.partial(forward_visit, blocks, queries, max_ref.at[0], total_ref.at[0])
    own_visits(peers, info_ref, seq, half, visit)


def attend_near(info, kept, got, own, near):
    steps, _, block_len, _ = own.shape
    peers = info.shape[1] - 3
    half = block_len // 2
    size = GROUP * HEAD
    height = HEAD + SUM_ROWS
    queries = pl.BlockSpec((size, half), lambda s, g, info: (g, s))
    block = pl.BlockSpec((1, 1, block_len, PAIR), lambda s, g, info: (s, g, 0, 0))
    state = lambda height: pl.BlockSpec(
        (1, GROUP, height, block_len), lambda s, g, info: (g, 0, 0, s)
    )
    work = steps * HEADS * block_len * block_len
    return pl.pallas_call(
        functools.partial(near_kernel, peers),
        grid_spec=pltpu.PrefetchScalarGridSpec(
            num_scalar_prefetch=1,
            grid=(steps, KV_HEADS),
            in_specs=[queries, queries, block, block],
            out_specs=[state(1), state(height)],
            scratch_shapes=[
                pltpu.VMEM((2, block_len, PAIR), BF16),
                pltpu.VMEM((GROUP, PAIR, block_len), BF16),
            ],
        ),
        out_shape=[
            jax.ShapeDtypeStruct((KV_HEADS, GROUP, 1, steps * block_len), F32),
            jax.ShapeDtypeStruct((KV_HEADS, GROUP, height, steps * block_len), F32),
        ],
        compiler_params=params(),
        cost_estimate=pl.CostEstimate(
            flops=2 * 2 * 256 * work, bytes_accessed=8 * 1024 * 1024, transcendentals=work
        ),
        name="attend_near",
    )(info, kept, got, own, near)


def forward_kernel(counts, info_ref, kept_ref, got_ref, near_max, near_total, *refs):
    peers, arrays = len(counts), sum(counts)
    kv_refs = refs[:arrays]
    out_ref, kept16_ref, got16_ref, lse_ref = refs[arrays : arrays + 4]
    blocks, queries, row_max, total = refs[arrays + 4 :]
    seq = pl.program_id(0)
    half = kept_ref.shape[1]
    load_blocks(blocks, counts, kv_refs, seq)
    load_queries(queries, kept_ref, got_ref)
    row_max[...] = near_max[0]
    total[...] = near_total[0]
    visit = functools.partial(forward_visit, blocks, queries, row_max, total)
    other_visits(peers, info_ref, seq, half, visit)
    for h in range(GROUP):
        head = slice(h * HEAD, (h + 1) * HEAD)
        row_sum = total[h, HEAD : HEAD + 1, :]
        result = total[h, :HEAD, :] / row_sum
        out_ref[head, :] = result
        kept16_ref[head, :] = result[:, :half].astype(BF16)
        got16_ref[head, :] = result[:, half:].astype(BF16)
        lse_ref[h : h + 1, :] = row_max[h] + jnp.log2(row_sum)


def attention_specs(group, half):
    across = lambda height: pl.BlockSpec((height, 2 * half), lambda s, info: (0, s))
    across_half = lambda height, at=0: pl.BlockSpec((height, half), lambda s, info: (at, s))

    def block(whole):
        return pl.BlockSpec(
            (1, 1, 2 * half, PAIR), lambda s, info: (s if whole else 0, group, 0, 0)
        )

    return across, across_half, block


def attend(info, kept, got, near, blocks, group):
    peers = len(blocks)
    counts = tuple(len(b) for b in blocks)
    arrays = [a for b in blocks for a in b]
    steps, _, block_len, _ = arrays[0].shape
    half = block_len // 2
    rows = steps * block_len
    size = GROUP * HEAD
    across, across_half, block = attention_specs(group, half)
    work = steps * GROUP * block_len * peers * block_len
    return pl.pallas_call(
        functools.partial(forward_kernel, counts),
        grid_spec=pltpu.PrefetchScalarGridSpec(
            num_scalar_prefetch=1,
            grid=(steps,),
            in_specs=[across_half(size, group)] * 2
            + [
                pl.BlockSpec((1, GROUP, a.shape[2], block_len), lambda s, info: (group, 0, 0, s))
                for a in near
            ]
            + [block(len(b) == 1) for b in blocks for _ in b],
            out_specs=[across(size), across_half(size), across_half(size), across(8)],
            scratch_shapes=[
                pltpu.VMEM((peers, block_len, PAIR), BF16),
                pltpu.VMEM((GROUP, PAIR, block_len), BF16),
                pltpu.VMEM((GROUP, 1, block_len), F32),
                pltpu.VMEM((GROUP, HEAD + SUM_ROWS, block_len), F32),
            ],
        ),
        out_shape=[
            jax.ShapeDtypeStruct((size, rows), F32),
            jax.ShapeDtypeStruct((size, rows // 2), BF16),
            jax.ShapeDtypeStruct((size, rows // 2), BF16),
            jax.ShapeDtypeStruct((8, rows), F32),
        ],
        compiler_params=params(),
        cost_estimate=pl.CostEstimate(
            flops=2 * 2 * 256 * work, bytes_accessed=4 * size * rows, transcendentals=work
        ),
        name="attend",
    )(info, kept, got, *near, *arrays)


def backward_kernel(near, counts, shared, info_ref, *refs):
    count, arrays = len(counts), sum(counts)
    (kept_ref, got_ref, dkept_ref, dgot_ref, out_ref, lse_ref) = refs[:6]
    refs = refs[6:]
    if near:
        (cos_kept, sin_kept, cos_got, sin_got, dq_in) = refs[:5]
        refs = refs[5:]
    kv_refs = refs[:arrays]
    dq_refs = refs[arrays + shared : arrays + shared + (2 if near else 1)]
    refs = refs[arrays + shared + len(dq_refs) :]
    dkv_refs = refs[:count]
    blocks, grads, queries, douts, delta, dq = refs[count:]
    seq = pl.program_id(0)
    half = kept_ref.shape[1]
    peers = info_ref.shape[1] - 3
    load_blocks(blocks, counts, kv_refs, seq)
    for k in range(count):
        grads[k] = jnp.zeros((PAIR, 2 * half), F32)
    for h in range(GROUP):
        head = slice(h * HEAD, (h + 1) * HEAD)
        zeros = jnp.zeros((HEAD, 2 * half), BF16)
        dout = jnp.concatenate([dkept_ref[head, :], dgot_ref[head, :]], axis=1)
        queries[h, :HEAD, :half] = kept_ref[head, :]
        queries[h, :HEAD, half:] = got_ref[head, :]
        queries[h, HEAD:, :] = zeros
        douts[h, :HEAD, :] = zeros
        douts[h, HEAD:, :] = dout
        delta[h] = jnp.sum(dout.astype(F32) * out_ref[head, :], axis=0, keepdims=True)
        dq[h] = dq_in[h] if near else jnp.zeros((HEAD, 2 * half), F32)

    def visit(k, lanes, width, keys, diagonal):
        k = k if near else k - 2
        kv = blocks[k, :keys, :]
        keys_t = kv.T[:HEAD]
        heads = range(GROUP)
        scores = [matmul(kv, queries[h, :, lanes]) for h in heads]
        dprobs = [matmul(kv, douts[h, :, lanes]) for h in heads]
        probs = [jnp.exp2(scores[h] - lse_ref[h : h + 1, lanes]) for h in heads]
        if diagonal is not None:
            mask = key_mask(keys, width, diagonal)
            probs = [jnp.where(mask, a, 0.0) for a in probs]
        dscores = [(probs[h] * (dprobs[h] - delta[h, :, lanes])).astype(BF16) for h in heads]
        probs = [a.astype(BF16) for a in probs]
        dkeys = sum(matmul_trail(queries[h, :HEAD, lanes], dscores[h]) for h in heads)
        dvalues = sum(matmul_trail(douts[h, HEAD:, lanes], probs[h]) for h in heads)
        grads[k, :HEAD, :keys] += dkeys
        grads[k, HEAD:, :keys] += dvalues
        for h in heads:
            dq[h, :, lanes] += matmul(keys_t, dscores[h])

    row = lax.broadcasted_iota(jnp.int32, (PAIR, 1), 0)
    unit = jnp.where(row < HEAD, LN_2, 1.0)
    if near:
        own_visits(peers, info_ref, seq, half, visit)
    else:
        other_visits(peers, info_ref, seq, half, visit)
    for k in range(count):
        dkv_refs[k][0, 0] = (grads[k] * unit).astype(BF16).T
    if not near:
        dq_refs[0][...] = dq[...]
        return
    for h in range(GROUP):
        for at, dq_ref, cos_ref, sin_ref in (
            (0, dq_refs[0], cos_kept, sin_kept),
            (half, dq_refs[1], cos_got, sin_got),
        ):
            first = dq[h, :HALF, at : at + half] * 0.125
            second = dq[h, HALF:, at : at + half] * 0.125
            cos, sin = cos_ref[...], sin_ref[...]
            dq_ref[h * HEAD : h * HEAD + HALF, :] = (first * cos + second * sin).astype(BF16)
            dq_ref[h * HEAD + HALF : (h + 1) * HEAD, :] = (second * cos - first * sin).astype(BF16)


def attend_back(near, info, rows_in, extra, blocks, group, shared):
    count = len(blocks)
    counts = tuple(len(b) for b in blocks)
    arrays = [a for b in blocks for a in b]
    steps, _, block_len, _ = arrays[0].shape
    steps = info.shape[0]
    half = block_len // 2
    rows = steps * block_len
    size = GROUP * HEAD
    across, across_half, block = attention_specs(group, half)
    state = pl.BlockSpec((GROUP, HEAD, block_len), lambda s, info: (0, 0, s))
    pair_t = pltpu.VMEM((GROUP, PAIR, block_len), BF16)
    work = steps * GROUP * block_len * count * block_len
    inputs = (info, *rows_in, *extra, *arrays)
    if near:
        dq_specs = [across_half(size)] * 2
        dq_shapes = [jax.ShapeDtypeStruct((size, rows // 2), BF16)] * 2
    else:
        dq_specs = [state]
        dq_shapes = [jax.ShapeDtypeStruct((GROUP, HEAD, rows), F32)]
    return pl.pallas_call(
        functools.partial(backward_kernel, near, counts, len(shared)),
        grid_spec=pltpu.PrefetchScalarGridSpec(
            num_scalar_prefetch=1,
            grid=(steps,),
            in_specs=[across_half(size, group)] * 4
            + [across(size), across(8)]
            + ([across_half(HALF)] * 4 + [state] if near else [])
            + [block(len(b) == 1) for b in blocks for _ in b]
            + [pl.BlockSpec(memory_space=pl.ANY)] * len(shared),
            out_specs=dq_specs + [block(True)] * count,
            scratch_shapes=[
                pltpu.VMEM((count, block_len, PAIR), BF16),
                pltpu.VMEM((count, PAIR, block_len), F32),
                pair_t,
                pair_t,
                pltpu.VMEM((GROUP, 1, block_len), F32),
                pltpu.VMEM((GROUP, HEAD, block_len), F32),
            ],
        ),
        out_shape=dq_shapes
        + [jax.ShapeDtypeStruct((steps, KV_HEADS, block_len, PAIR), BF16)] * count,
        input_output_aliases={len(inputs) + i: len(dq_shapes) + i for i in range(len(shared))},
        compiler_params=params(),
        cost_estimate=pl.CostEstimate(
            flops=work if near else 5 * 2 * 256 * work,
            bytes_accessed=size * rows,
            transcendentals=0 if near else work,
        ),
        name="attend_back_near" if near else "attend_back",
    )(*inputs, *shared)


def norm_back(rows, inverse, gain, grad):
    scaled = grad * gain
    mean = jnp.mean(scaled * rows, axis=-1, keepdims=True)
    row_grad = inverse * scaled - rows * (inverse * inverse * inverse) * mean
    return row_grad, jnp.sum(grad * rows * inverse, axis=0, keepdims=True)


def middle_kernel(down_half, half, chunk, side_ref, *refs):
    kept_refs, back_refs = refs[:KV_HEADS], refs[KV_HEADS : 2 * KV_HEADS]
    x_ref, dy_ref, gains_ref, mine_ref, other_ref = refs[2 * KV_HEADS : 2 * KV_HEADS + 5]
    (
        out_ref,
        dh_ref,
        dkept_ref,
        dsent_ref,
        wide_kept,
        wide_sent,
        narrow_kept,
        narrow_sent,
        gain_ref,
    ) = refs[2 * KV_HEADS + 5 : 2 * KV_HEADS + 14]
    ff_weight, down_weight, out_weight, mixed, ff_grad, down_grad = refs[2 * KV_HEADS + 14 :]
    shards = mine_ref.shape[0]
    hidden_width = ff_weight.shape[2]
    width = x_ref.shape[1]
    depth = width // shards
    half_hidden = hidden_width // 2
    size = GROUP * HEAD
    side = side_ref[0]
    for z in range(shards):
        for ref, owner in ((mine_ref, side), (other_ref, 1 - side)):
            here = slice(z * depth, (z + 1) * depth)
            ff_weight[owner, here, :half_hidden] = ref[z, :depth, :]
            ff_weight[owner, here, half_hidden:] = ref[z, depth : 2 * depth, :]
            down_at = pl.multiple_of((2 * z + owner) * down_half, 16)
            down_weight[pl.ds(down_at, down_half), :] = ref[
                z, 2 * depth : 2 * depth + down_half, :width
            ]
        out_weight[here, :] = mine_ref[z, 2 * depth + down_half :, :width]
    starts = range(0, kept_refs[0].shape[1], half)
    for g in range(KV_HEADS):
        for at in starts:
            rows = slice(g * size, (g + 1) * size)
            mixed[rows, 2 * at : 2 * at + half] = kept_refs[g][:, at : at + half]
            mixed[rows, 2 * at + half : 2 * at + 2 * half] = back_refs[g][:, at : at + half]
    weight_out = out_weight[...]
    gain = gains_ref[1:2, :]
    rows = x_ref[...].astype(F32) + matmul_lead(mixed[...], weight_out)
    inverse = lax.rsqrt(jnp.mean(rows * rows, axis=-1, keepdims=True) + NORM_EPSILON)
    normed = (rows * inverse * gain).astype(BF16)
    normed_t = normed.T
    dy = dy_ref[...]
    result = rows
    dnormed = jnp.zeros(rows.shape, F32)
    for at in range(0, hidden_width, chunk):
        part = slice(at, at + chunk)
        gate = matmul(normed, ff_weight[0, :, part])
        upward = matmul(normed, ff_weight[1, :, part])
        dhidden = matmul_trail(dy, down_weight[part, :])
        sigmoid = jax.nn.sigmoid(gate)
        silu = gate * sigmoid
        hidden = (silu * upward).astype(BF16)
        dgate = (dhidden * upward * sigmoid * (1.0 + gate * (1.0 - sigmoid))).astype(BF16)
        dup = (dhidden * silu).astype(BF16)
        result = result + matmul(hidden, down_weight[part, :])
        down_grad[part, :] = matmul_lead(hidden, dy).astype(BF16)
        ff_grad[0, :, part] = matmul(normed_t, dgate).astype(BF16)
        ff_grad[1, :, part] = matmul(normed_t, dup).astype(BF16)
        dnormed = dnormed + (
            matmul_trail(dgate, ff_weight[0, :, part]) + matmul_trail(dup, ff_weight[1, :, part])
        )
    out_ref[...] = result.astype(BF16)
    row_grad, gain_grad = norm_back(rows, inverse, gain, dnormed)
    gain_ref[...] = jnp.broadcast_to(gain_grad, gain_ref.shape)
    drows = dy.astype(F32) + row_grad
    dh_ref[...] = drows
    drows = drows.astype(BF16)
    out_grad = matmul(mixed[...], drows).astype(BF16)
    dout = matmul_trail(weight_out, drows).astype(BF16)
    for at in starts:
        dkept_ref[:, at : at + half] = dout[:, 2 * at : 2 * at + half]
        dsent_ref[:, at : at + half] = dout[:, 2 * at + half : 2 * at + 2 * half]
    wide_kept[...] = ff_grad[side]
    wide_sent[...] = ff_grad[1 - side]
    for z in range(shards):
        mine = pl.multiple_of((2 * z + side) * down_half, 16)
        other = pl.multiple_of((2 * z + 1 - side) * down_half, 16)
        narrow_kept[z, :down_half, :] = down_grad[pl.ds(mine, down_half), :]
        narrow_sent[z, :down_half, :] = down_grad[pl.ds(other, down_half), :]
        out_rows = out_grad[z * depth : (z + 1) * depth, :]
        narrow_kept[z, down_half:, :] = out_rows
        narrow_sent[z, down_half:, :] = out_rows


def middle(side, kept, back, inputs, dy, gains, mine, other, block_len, chunk=512):
    rows, width = inputs.shape
    shards, packed_rows, half_hidden = mine.shape
    hidden_width = 2 * half_hidden
    down_half = hidden_width // shards // 2
    wide = (width, hidden_width)
    narrow = (shards, packed_rows - 2 * width // shards, width)
    half = block_len // 2
    shape = jax.ShapeDtypeStruct
    work = 3 * 2 * rows * width * (3 * hidden_width + width)
    vmem = pl.BlockSpec(memory_space=pltpu.VMEM)
    return pl.pallas_call(
        functools.partial(middle_kernel, down_half, half, chunk),
        in_specs=[pl.BlockSpec(memory_space=pltpu.SMEM)] + [vmem] * (2 * KV_HEADS + 5),
        out_specs=[vmem] * 9,
        scratch_shapes=[
            pltpu.VMEM((2, width, hidden_width), BF16),
            pltpu.VMEM((hidden_width, width), BF16),
            pltpu.VMEM((HEADS * HEAD, width), BF16),
            pltpu.VMEM((HEADS * HEAD, rows), BF16),
            pltpu.VMEM((2, width, hidden_width), BF16),
            pltpu.VMEM((hidden_width, width), BF16),
        ],
        out_shape=[
            shape((rows, width), BF16),
            shape((rows, width), F32),
            shape((HEADS * HEAD, rows // 2), BF16),
            shape((HEADS * HEAD, rows // 2), BF16),
            shape(wide, BF16),
            shape(wide, BF16),
            shape(narrow, BF16),
            shape(narrow, BF16),
            shape(gains.shape, F32),
        ],
        compiler_params=params(),
        cost_estimate=pl.CostEstimate(
            flops=work, bytes_accessed=30 * 1024 * 1024, transcendentals=rows * hidden_width
        ),
        name="middle",
    )(side, *kept, *back, inputs, dy, gains, mine, other)


def exit_query_kernel(*refs):
    kept_refs, back_refs = refs[:KV_HEADS], refs[KV_HEADS : 2 * KV_HEADS]
    normed_ref, weight_ref, grad_ref, da_ref, dq = refs[2 * KV_HEADS :]
    half = kept_refs[0].shape[1]
    size = GROUP * HEAD
    for g in range(KV_HEADS):
        dq[g * size : (g + 1) * size, :half] = kept_refs[g][...]
        dq[g * size : (g + 1) * size, half:] = back_refs[g][...]
    rows = dq[...].T
    da_ref[...] = matmul_trail(rows, weight_ref[:, : HEADS * HEAD])
    grad = matmul_lead(normed_ref[...], rows)

    @pl.when(pl.program_id(0) == 0)
    def _():
        grad_ref[...] = grad

    @pl.when(pl.program_id(0) > 0)
    def _():
        grad_ref[...] += grad


def exit_query(kept, back, normed, weight, block_len):
    rows, width = normed.shape
    size = GROUP * HEAD
    half = block_len // 2
    down = pl.BlockSpec((block_len, width), lambda s: (s, 0))
    return pl.pallas_call(
        exit_query_kernel,
        grid=(rows // block_len,),
        in_specs=[pl.BlockSpec((size, half), lambda s: (0, s))] * (2 * KV_HEADS)
        + [down, pl.BlockSpec(weight.shape, lambda s: (0, 0))],
        out_specs=[pl.BlockSpec((width, HEADS * HEAD), lambda s: (0, 0)), down],
        out_shape=[
            jax.ShapeDtypeStruct((width, HEADS * HEAD), F32),
            jax.ShapeDtypeStruct((rows, width), F32),
        ],
        scratch_shapes=[pltpu.VMEM((HEADS * HEAD, block_len), BF16)],
        compiler_params=params(),
        cost_estimate=pl.CostEstimate(
            flops=4 * rows * width * width, bytes_accessed=16 * rows * width, transcendentals=0
        ),
        name="exit_query",
    )(*kept, *back, normed, weight)


def exit_kernel(counts, side_ref, *refs):
    arrays = sum(counts)
    part_refs = refs[:arrays]
    (normed_ref, weight_ref, gq_ref, da_ref, x_ref, dh_ref, gains_ref, gain_mlp_ref) = refs[
        arrays : arrays + 8
    ]
    cos_ref, low_ref, high_ref, dx_ref, kept_ref, sent_ref, grad, gain_acc = refs[arrays + 8 :]
    step = pl.program_id(0)
    side = side_ref[0]
    cols = kept_ref.shape[1]
    wide = HEADS * HEAD

    @pl.when(step == 0)
    def _():
        grad[...] = jnp.zeros(grad.shape, F32)
        gain_acc[...] = jnp.zeros(gain_acc.shape, F32)

    parts = []
    at = 0
    for count in counts:
        parts.append(choose(part_refs[at : at + count], step))
        at += count
    normed = normed_ref[...]
    dnormed = da_ref[...]
    kv_at = weight_ref.shape[1] - KV_HEADS * PAIR
    for g in range(KV_HEADS):
        dkv = sum((part[0, g].astype(F32) for part in parts[1:]), parts[0][0, g].astype(F32))
        turned = (
            dkv * cos_ref[...]
            - pltpu.roll(dkv, HALF, 1) * low_ref[...]
            - pltpu.roll(dkv, PAIR - HALF, 1) * high_ref[...]
        ).astype(BF16)
        here = slice(kv_at + g * PAIR, kv_at + (g + 1) * PAIR)
        dnormed = dnormed + matmul_trail(turned, weight_ref[:, here])
        grad[:, g * PAIR : (g + 1) * PAIR] += matmul_lead(normed, turned)
    rows = x_ref[...].astype(F32)
    inverse = lax.rsqrt(jnp.mean(rows * rows, axis=-1, keepdims=True) + NORM_EPSILON)
    row_grad, gain_grad = norm_back(rows, inverse, gains_ref[0:1, :], dnormed)
    gain_acc[0:1, :] += gain_grad
    dx_ref[...] = (dh_ref[...] + row_grad).astype(BF16)

    @pl.when(step == pl.num_programs(0) - 1)
    def _():
        width = normed.shape[1]
        gains = jnp.concatenate(
            [
                jnp.zeros((HEAD, width), F32),
                gain_acc[0:1, :],
                gain_mlp_ref[0:1, :],
                jnp.zeros((HEAD - 2, width), F32),
            ],
            axis=0,
        ).T

        def write_low(ref):
            ref[...] = gq_ref[:, :cols].astype(BF16)

        def write_high(ref):
            ref[:, :PAIR] = gains.astype(BF16)
            ref[:, : wide - cols] = gq_ref[:, cols:].astype(BF16)
            ref[:, PAIR:] = grad[...].astype(BF16)

        @pl.when(side == 0)
        def _():
            write_low(kept_ref)
            write_high(sent_ref)

        @pl.when(side != 0)
        def _():
            write_high(kept_ref)
            write_low(sent_ref)


def leave(side, parts, normed, weight, grad_query, da, inputs, dh, gains, gain_mlp, tables, block_len):
    rows, width = normed.shape
    cols = weight.shape[1] // 2
    counts = tuple(len(p) for p in parts)
    arrays = [a for p in parts for a in p]
    down = pl.BlockSpec((block_len, width), lambda s, side: (s, 0))
    fixed = lambda shape: pl.BlockSpec(shape, lambda s, side: (0,) * len(shape))

    def block(whole):
        return pl.BlockSpec(
            (1, KV_HEADS, block_len, PAIR), lambda s, side: (s if whole else 0, 0, 0, 0)
        )

    table = pl.BlockSpec((block_len, PAIR), lambda s, side: (s, 0))
    return pl.pallas_call(
        functools.partial(exit_kernel, counts),
        grid_spec=pltpu.PrefetchScalarGridSpec(
            num_scalar_prefetch=1,
            grid=(rows // block_len,),
            in_specs=[block(len(p) == 1) for p in parts for _ in p]
            + [down, fixed(weight.shape), fixed(grad_query.shape), down, down, down]
            + [fixed(gains.shape), fixed(gain_mlp.shape)]
            + [table] * 3,
            out_specs=[down, fixed((width, cols)), fixed((width, cols))],
            scratch_shapes=[
                pltpu.VMEM((width, KV_HEADS * PAIR), F32),
                pltpu.VMEM((8, width), F32),
            ],
        ),
        out_shape=[
            jax.ShapeDtypeStruct((rows, width), BF16),
            jax.ShapeDtypeStruct((width, cols), BF16),
            jax.ShapeDtypeStruct((width, cols), BF16),
        ],
        compiler_params=params(),
        name="leave",
    )(side, *arrays, normed, weight, grad_query, da, inputs, dh, gains, gain_mlp, *tables)


def pack_kv(key_part, value_part):
    depth = key_part.shape[0]
    both = jnp.stack(
        [key_part.reshape(depth, KV_HEADS, HEAD), value_part.reshape(depth, KV_HEADS, HEAD)], axis=2
    )
    return both.reshape(depth, KV_HEADS * PAIR)


def unpack_kv(packed):
    depth = packed.shape[0]
    both = packed.reshape(depth, KV_HEADS, 2, HEAD)
    return (
        both[:, :, 0].reshape(depth, KV_HEADS * HEAD),
        both[:, :, 1].reshape(depth, KV_HEADS * HEAD),
    )


def rope_tables(positions):
    freqs = ROPE_BASE ** (-jnp.arange(HALF, dtype=F32) * 2.0 / HEAD)
    angle = positions.reshape(1, -1).astype(F32) * freqs[:, None]
    cos_t, sin_t = jnp.cos(angle), jnp.sin(angle)
    cos, sin = cos_t.T, sin_t.T
    nothing = jnp.zeros_like(cos)
    ones = jnp.ones_like(cos)
    return (
        cos_t,
        sin_t,
        jnp.concatenate([cos, cos, ones, ones], axis=1),
        jnp.concatenate([nothing, sin, nothing, nothing], axis=1),
        jnp.concatenate([-sin, nothing, nothing, nothing], axis=1),
    )


def per_device(
    hidden_in,
    out_grad,
    block_slot,
    rope_pos,
    w_query,
    w_key,
    w_value,
    w_out,
    w_gate,
    w_up,
    w_down,
    gain_attn,
    gain_mlp,
):
    seq_count, block_len, width = hidden_in.shape
    row_count = seq_count * block_len
    hidden_width = w_gate.shape[1]
    depth = w_query.shape[0]
    cycle_index = lax.axis_index(CTX)
    cycle_size = lax.axis_size(CTX)
    shard_index = lax.axis_index("shard")
    shards = lax.axis_size("shard")
    side = lax.axis_index("core")

    def whole(parts):
        rows = parts[0].shape[0]
        out = jnp.zeros((shards * rows,) + parts[0].shape[1:], parts[0].dtype)
        for t, part in enumerate(parts):
            out = lax.dynamic_update_slice_in_dim(out, part, ((shard_index - t) % shards) * rows, 0)
        return out

    packed = jnp.concatenate(
        [
            w_query,
            gain_attn[:, None],
            gain_mlp[:, None],
            jnp.zeros((depth, HEAD - 2), BF16),
            pack_kv(w_key, w_value),
        ],
        axis=1,
    )
    cols = packed.shape[1] // 2
    mine = ring_pieces(lax.dynamic_slice_in_dim(packed, side * cols, cols, 1), "shard")
    pieces = mine + [flip(a, 1) for a in mine]
    place = jnp.stack([shard_index, side]).astype(jnp.int32)
    if depth % 16:
        pieces = [whole(pieces[:shards]), whole(pieces[shards:])]
        place = jnp.stack([jnp.zeros_like(side), side]).astype(jnp.int32)

    down_half = w_down.shape[0] // 2
    half_hidden = hidden_width // 2
    wide = jnp.where(side == 0, w_gate, w_up)
    narrow = jnp.concatenate(
        [lax.dynamic_slice_in_dim(w_down, side * down_half, down_half, 0), w_out], axis=0
    )
    later_weights = jnp.concatenate(
        [
            wide[:, :half_hidden],
            wide[:, half_hidden:],
            jnp.pad(narrow, ((0, 0), (0, half_hidden - width))),
        ],
        axis=0,
    )
    later_weights = after(later_weights, *mine[1:])
    later_weights = lax.all_gather(later_weights, "shard", axis=0, tiled=False)

    tables = rope_tables(rope_pos)
    cycle = jnp.arange(cycle_size, dtype=jnp.int32)
    at_slot = jnp.sum(
        jnp.where(
            block_slot[:, :, None] == cycle[None, None, :],
            (cycle ^ cycle_index)[None, :, None],
            0,
        ),
        axis=1,
    )
    own_slot = lax.dynamic_index_in_dim(block_slot, cycle_index, 1, keepdims=True)
    near_slot = lax.dynamic_index_in_dim(block_slot, cycle_index ^ 1, 1, keepdims=True)
    info = jnp.concatenate(
        [
            at_slot,
            jnp.minimum(own_slot, near_slot),
            jnp.maximum(own_slot, near_slot),
            (near_slot > own_slot).astype(jnp.int32),
        ],
        axis=1,
    ).astype(jnp.int32)

    half = block_len // 2

    def halves(value, second):
        starts = range(second * half, row_count, block_len)
        return jnp.concatenate([value[:, at : at + half] for at in starts], axis=1)

    turns = jnp.concatenate(tables[:2], axis=0)
    turns_got = flip(halves(turns, 1), 1)
    turns = halves(turns, 0)
    turns = (turns[:HALF], turns[HALF:], turns_got[:HALF], turns_got[HALF:])

    flat_in = hidden_in.reshape(row_count, width)
    q_kept, q_sent, kv, normed_attn, full_packed, gains = entry(
        place, pieces, flat_in, tables, block_len
    )
    q_got = flip(q_sent, 1)
    near, blocks = gather_flipped(kv, functools.partial(attend_near, info, q_kept, q_got))
    attended = []
    last_info = info
    for g in range(KV_HEADS):
        if g == KV_HEADS - 1:
            last_info, later_weights, *attended = tied(info, later_weights, *attended)
        attended.append(attend(last_info, q_kept, q_got, near, blocks, g))
    back = [flip(a[2], 1) for a in attended]

    side_ref = side.reshape(1).astype(jnp.int32)
    (
        block_out,
        middle_grad,
        dout_kept,
        dout_sent,
        wide_kept,
        wide_sent,
        narrow_kept,
        narrow_sent,
        gain_mlp_grad,
    ) = middle(
        side_ref,
        [a[1] for a in attended],
        back,
        flat_in,
        out_grad.reshape(row_count, width),
        gains,
        later_weights,
        flip(later_weights, 1),
        block_len,
    )

    dout_got = flip(dout_sent, 1)
    wide_got = flip(wide_sent, 1)
    narrow_got = flip(narrow_sent, 1)
    rows_in = [
        (q_kept, q_got, dout_kept, dout_got, attended[g][0], attended[g][3])
        for g in range(KV_HEADS)
    ]
    dq_far = []
    parts = []
    for g in range(KV_HEADS):
        mine = rows_in[g]
        if g == 1:
            early_wide = add_sent(wide_kept, wide_got)
            early_narrow = add_sent(narrow_kept, narrow_got)
            early_wide, early_narrow, *mine = lax.optimization_barrier(
                (early_wide, early_narrow, *mine, *parts)
            )
            mine, parts = mine[:6], mine[6:]
            early_wide = lax.psum_scatter(early_wide, "shard", scatter_dimension=0, tiled=True)
            early_narrow = lax.psum_scatter(early_narrow, "shard", scatter_dimension=0, tiled=False)
        dq, *parts = attend_back(False, info, mine, (), blocks[2:], g, parts)
        dq_far.append(dq)

    dq_kept, dq_back = [], []

    def near_step(g, info, grads):
        first, second, *grads = attend_back(
            True, info, rows_in[g], (*turns, dq_far[g]), blocks[:2], g, grads
        )
        dq_kept.append(first)
        dq_back.append(flip(second, 1))
        return grads

    steps = [functools.partial(near_step, g) for g in range(KV_HEADS)]
    parts = scatter_flipped(parts, info, steps)
    grad_query, attn_grad = exit_query(dq_kept, dq_back, normed_attn, full_packed, block_len)
    early_wide, early_narrow, grad_query, attn_grad, *rest = tied(
        early_wide, early_narrow, grad_query, attn_grad, *(a for p in parts for a in p)
    )
    parts = [tuple(rest.pop(0) for _ in p) for p in parts]
    wide_got, narrow_got = flip(early_wide, 2), flip(early_narrow, 4)
    in_grad, late_kept, late_sent = leave(
        side_ref,
        parts,
        normed_attn,
        full_packed,
        grad_query,
        attn_grad,
        flat_in,
        middle_grad,
        gains,
        gain_mlp_grad,
        tables[2:],
        block_len,
    )
    early_wide = add_sent(early_wide, wide_got)
    early_narrow = add_sent(early_narrow, narrow_got)
    early_wide, early_narrow, late_kept = tied(early_wide, early_narrow, late_kept)
    early_wide = add_sent(early_wide, flip(early_wide, 4))
    early_narrow = add_sent(early_narrow, flip(early_narrow, 2))
    bit = 8
    while bit < cycle_size:
        early_wide = add_sent(early_wide, flip(early_wide, bit))
        early_narrow = add_sent(early_narrow, flip(early_narrow, bit))
        bit *= 2
    in_grad = in_grad.reshape(hidden_in.shape)
    block_out = block_out.reshape(hidden_in.shape)
    kv_at = full_packed.shape[1] - KV_HEADS * PAIR
    late = add_sent(late_kept, flip(late_sent, 1)).reshape(shards, depth, cols)
    share = lambda by: lax.dynamic_index_in_dim(late, (shard_index + by) % shards, 0, keepdims=False)
    arrived = [shift(share(by), "shard", by) for by in range(1, shards)]
    late = sum((a.astype(F32) for a in arrived), share(0).astype(F32)).astype(BF16)
    bit = 2
    while bit < cycle_size:
        late = add_sent(late, flip(late, bit))
        bit *= 2
    other = flip(late, 1)
    late = jnp.where(
        side == 0,
        jnp.concatenate([late, other], axis=1),
        jnp.concatenate([other, late], axis=1),
    ).astype(F32)
    grad_key, grad_value = unpack_kv(late[:, kv_at:])
    other_wide = flip(early_wide, 1)
    down_own = early_narrow[:down_half]
    down_other = flip(down_own, 1)
    grad_down = jnp.where(
        side == 0,
        jnp.concatenate([down_own, down_other], axis=0),
        jnp.concatenate([down_other, down_own], axis=0),
    )
    return (
        block_out,
        in_grad,
        late[:, : HEADS * HEAD],
        grad_key,
        grad_value,
        early_narrow[down_half:].astype(F32),
        jnp.where(side == 0, early_wide, other_wide).astype(F32),
        jnp.where(side == 0, other_wide, early_wide).astype(F32),
        grad_down.astype(F32),
        late[:, HEADS * HEAD],
        late[:, HEADS * HEAD + 1],
    )


def solution(mesh):
    ctx, shards = mesh.shape["ctx"], mesh.shape["shard"]
    split_mesh = Mesh(mesh.devices.reshape(ctx // 4, 2, 2, shards), CTX + ("shard",))
    rows = P("shard", CTX, None)
    split = P("shard", None)
    return jax.shard_map(
        per_device,
        mesh=split_mesh,
        in_specs=(rows, rows, split, P("shard", CTX)) + (split,) * 7 + (P("shard"),) * 2,
        out_specs=(rows, rows) + (split,) * 7 + (P("shard"),) * 2,
        check_vma=False,
    )
```

```python
import functools

import jax
import jax.numpy as jnp
from jax import lax
from jax.experimental import pallas as pl
from jax.experimental.pallas import tpu as pltpu
from jax.sharding import Mesh
from jax.sharding import PartitionSpec as P

HEADS = 9
KV_HEADS = 3
HEAD = 64
GROUP = HEADS // KV_HEADS
PAIR = 2 * HEAD
HALF = HEAD // 2

NORM_EPSILON = 1e-05
ROPE_BASE = 100000.0
LOG2_E = 1.4426950408889634
LN_2 = 0.6931471805599453
MASKED_SCORE = -1e30
SUM_ROWS = 16
VMEM_BYTES = 56 * 1024 * 1024

CHIPS = ("cy", "cx")
CTX = CHIPS + ("core",)

F32 = jnp.float32
BF16 = jnp.bfloat16


def params():
    return pltpu.CompilerParams(vmem_limit_bytes=VMEM_BYTES)


def matmul(left, right):
    return jnp.dot(left, right, preferred_element_type=F32)


def matmul_lead(left, right):
    return lax.dot_general(left, right, (((0,), (0,)), ((), ())), preferred_element_type=F32)


def matmul_trail(left, right):
    return lax.dot_general(left, right, (((1,), (1,)), ((), ())), preferred_element_type=F32)


def flip(value, bit):
    peers = lax.axis_size(CTX)
    return lax.ppermute(value, CTX, [(i, i ^ bit) for i in range(peers)])


def shift(value, axis, by=1):
    peers = lax.axis_size(axis)
    return lax.ppermute(value, axis, [(i, (i + by) % peers) for i in range(peers)])


def ring_pieces(piece, axis):
    return [piece] + [shift(piece, axis, by) for by in range(1, lax.axis_size(axis))]


def after(value, *others):
    return lax.optimization_barrier((value,) + others)[0]


def gather_flipped(own, beside):
    peers = lax.axis_size(CTX)
    if peers == 8:
        by_x = flip(own, 2)
        by_y = flip(own, 4)
        near = flip(own, 1)
        result = beside(own, near)
        by_x, by_y, result = lax.optimization_barrier((by_x, by_y, result))
        first = flip(by_y[:1], 2)
        second = flip(by_x[1:], 4)
        same_core = [(own,), (by_x,), (by_y,), (first, second)]
        other_core = [(near,)] + [tuple(flip(a, 1) for a in block) for block in same_core[1:]]
        return result, [b for pair in zip(same_core, other_core) for b in pair]
    blocks = [own]
    bit = 1
    while bit < peers:
        blocks = blocks + [flip(b, bit) for b in blocks]
        bit *= 2
    return beside(blocks[0], blocks[1]), [(b,) for b in blocks]


def add_sent(kept, arrived):
    return (kept.astype(F32) + arrived.astype(F32)).astype(BF16)


def tied(value, *others):
    return lax.optimization_barrier((value,) + others)


def scatter_flipped(parts, info, steps):
    peers = len(parts) + 2
    result = ()
    if peers == 8:
        near = {k: flip(parts[k - 1], 1) for k in (6, 2, 4)}
        seq = lambda k, i: add_sent(parts[k - 2][i : i + 1], near[k][i : i + 1])
        info, *sent = tied(info, seq(6, 0), seq(2, 0), seq(6, 1), seq(4, 1))
        arrived = [flip(a, bit) for a, bit in zip(sent, (2, 2, 4, 4))]
        for step in steps[:-1]:
            result = step(info, result)
        result, *arrived = tied(result, *arrived)
        far_x, x_first, far_y, y_second = arrived
        info, y_sent, x_sent = tied(info, add_sent(seq(4, 0), far_x), add_sent(seq(2, 1), far_y))
        y_first, x_second = flip(y_sent, 4), flip(x_sent, 2)
        own, own_sent = steps[-1](info, result)
        own = add_sent(own, flip(own_sent, 1))
        return [(own,), (x_first, x_second), (y_first, y_second)]
    for step in steps:
        result = step(info, result)
    parts = list(result) + parts
    while peers > 1:
        peers //= 2
        parts = [add_sent(parts[k], flip(parts[k + peers], peers)) for k in range(peers)]
    return [(parts[0],)]


def entry_kernel(shards, width, place_ref, *refs):
    piece_refs = refs[: 2 * shards]
    (x_ref, cos_t_ref, sin_t_ref, cos_ref, low_ref, high_ref) = refs[2 * shards : 2 * shards + 6]
    kept_ref, sent_ref, kv_ref, normed_ref, packed_ref, gains_ref = refs[
        2 * shards + 6 : 2 * shards + 12
    ]
    (weight,) = refs[2 * shards + 12 :]
    half = kept_ref.shape[1]
    depth = piece_refs[0].shape[0]
    cols = piece_refs[0].shape[1]

    @pl.when(pl.program_id(0) == 0)
    def assemble():
        shard, side = place_ref[0], place_ref[1]
        for t in range(shards):
            row = pl.multiple_of(lax.rem(shard - t + shards, shards) * depth, 16)
            mine = pl.multiple_of(side * cols, 128)
            other = pl.multiple_of((1 - side) * cols, 128)
            weight[pl.ds(row, depth), pl.ds(mine, cols)] = piece_refs[t][...]
            weight[pl.ds(row, depth), pl.ds(other, cols)] = piece_refs[shards + t][...]
        packed_ref[...] = weight[...]
        gains_ref[...] = weight[:, 512:640].astype(F32).T[64:72, :]

    rows = x_ref[...].astype(F32)
    inverse = lax.rsqrt(jnp.mean(rows * rows, axis=-1, keepdims=True) + NORM_EPSILON)
    normed = (rows * inverse * gains_ref[0:1, :]).astype(BF16)
    normed_ref[...] = normed
    cos_t = cos_t_ref[...]
    sin_t = sin_t_ref[...]
    for chunk in range(5):
        lin = matmul(normed, weight[:, chunk * PAIR : (chunk + 1) * PAIR]).T
        for part in range(2):
            head = 2 * chunk + part
            if head < HEADS:
                first = lin[part * HEAD : part * HEAD + HALF]
                second = lin[part * HEAD + HALF : (part + 1) * HEAD]
                turned = jnp.concatenate(
                    [first * cos_t - second * sin_t, second * cos_t + first * sin_t], axis=0
                )
                turned = (turned * (0.125 * LOG2_E)).astype(BF16)
                kept_ref[head * HEAD : (head + 1) * HEAD, :] = turned[:, :half]
                sent_ref[head * HEAD : (head + 1) * HEAD, :] = turned[:, half:]
    for group in range(KV_HEADS):
        at = 5 * PAIR + group * PAIR
        lin = matmul(normed, weight[:, at : at + PAIR])
        turned = (
            lin * cos_ref[...]
            + pltpu.roll(lin, HALF, 1) * low_ref[...]
            + pltpu.roll(lin, PAIR - HALF, 1) * high_ref[...]
        )
        kv_ref[0, group] = turned.astype(BF16)


def choose(refs, seq):
    if len(refs) == 1:
        return refs[0][...]
    return jnp.where(seq == 0, refs[0][...], refs[1][...])


def entry(place, pieces, inputs, tables, block_len):
    shards = len(pieces) // 2
    rows, width = inputs.shape
    cos_t, sin_t, cos, low, high = tables
    depth, cols = pieces[0].shape
    steps = rows // block_len
    fixed = lambda shape: pl.BlockSpec(shape, lambda s, place: (0,) * len(shape))
    return pl.pallas_call(
        functools.partial(entry_kernel, shards, width),
        grid_spec=pltpu.PrefetchScalarGridSpec(
            num_scalar_prefetch=1,
            grid=(steps,),
            in_specs=[fixed((depth, cols)) for _ in pieces]
            + [pl.BlockSpec((block_len, width), lambda s, place: (s, 0))]
            + [pl.BlockSpec((HALF, block_len), lambda s, place: (0, s))] * 2
            + [pl.BlockSpec((block_len, PAIR), lambda s, place: (s, 0))] * 3,
            out_specs=[
                pl.BlockSpec((HEADS * HEAD, block_len // 2), lambda s, place: (0, s)),
                pl.BlockSpec((HEADS * HEAD, block_len // 2), lambda s, place: (0, s)),
                pl.BlockSpec((1, KV_HEADS, block_len, PAIR), lambda s, place: (s, 0, 0, 0)),
                pl.BlockSpec((block_len, width), lambda s, place: (s, 0)),
                fixed((width, 2 * cols)),
                fixed((8, width)),
            ],
            scratch_shapes=[pltpu.VMEM((width, 2 * cols), BF16)],
        ),
        out_shape=[
            jax.ShapeDtypeStruct((HEADS * HEAD, rows // 2), BF16),
            jax.ShapeDtypeStruct((HEADS * HEAD, rows // 2), BF16),
            jax.ShapeDtypeStruct((steps, KV_HEADS, block_len, PAIR), BF16),
            jax.ShapeDtypeStruct((rows, width), BF16),
            jax.ShapeDtypeStruct((width, 2 * cols), BF16),
            jax.ShapeDtypeStruct((8, width), F32),
        ],
        compiler_params=params(),
        name="entry",
    )(place, *pieces, inputs, cos_t, sin_t, cos, low, high)


def key_mask(keys, queries, first_query):
    key = lax.broadcasted_iota(jnp.int32, (keys, queries), 0)
    query = lax.broadcasted_iota(jnp.int32, (keys, queries), 1)
    return key <= query + first_query


def own_visits(peers, info_ref, seq, half, visit):
    visit(0, pl.ds(0, half), half, half, 0)
    visit(1, pl.ds(half, half), half, 2 * half, half)
    later = info_ref[seq, peers + 2]
    visit(1 - later, pl.ds(pl.multiple_of(later * half, 128), half), half, 2 * half, None)


def other_visits(peers, info_ref, seq, half, visit):
    first, second = info_ref[seq, peers], info_ref[seq, peers + 1]

    @pl.loop(0, first)
    def _(r):
        visit(info_ref[seq, r], pl.ds(0, 2 * half), 2 * half, 2 * half, None)

    @pl.loop(first + 1, second)
    def _(r):
        start = pl.multiple_of(info_ref[seq, peers + 2] * half, 128)
        visit(info_ref[seq, r], pl.ds(start, half), half, 2 * half, None)


def load_blocks(blocks, counts, refs, seq):
    at = 0
    for k, count in enumerate(counts):
        blocks[k] = choose(refs[at : at + count], seq)[0, 0]
        at += count


def load_queries(queries, kept_ref, got_ref):
    half = kept_ref.shape[1]
    for h in range(GROUP):
        head = slice(h * HEAD, (h + 1) * HEAD)
        queries[h, :HEAD, :half] = kept_ref[head, :]
        queries[h, :HEAD, half:] = got_ref[head, :]
        queries[h, HEAD:, :] = jnp.zeros((HEAD, 2 * half), BF16)


def forward_visit(blocks, queries, row_max, total, k, lanes, width, keys, diagonal):
    kv = blocks[k, :keys, :]
    values_t = jnp.concatenate([kv.T[HEAD:], jnp.ones((SUM_ROWS, keys), BF16)], axis=0)
    scores = [matmul(kv, queries[h, :, lanes]) for h in range(GROUP)]
    if diagonal is not None:
        mask = key_mask(keys, width, diagonal)
        scores = [jnp.where(mask, a, MASKED_SCORE) for a in scores]
    weights, fading = [], []
    for h in range(GROUP):
        new_max = jnp.max(scores[h], axis=0, keepdims=True)
        if diagonal is None:
            old_max = row_max[h, :, lanes]
            new_max = jnp.maximum(old_max, new_max)
            fading.append(jnp.exp2(old_max - new_max))
        row_max[h, :, lanes] = new_max
        weights.append(jnp.exp2(scores[h] - new_max).astype(BF16))
    for h in range(GROUP):
        product = matmul(values_t, weights[h])
        if diagonal is None:
            product = total[h, :, lanes] * fading[h] + product
        total[h, :, lanes] = product


def near_kernel(peers, info_ref, kept_ref, got_ref, own_ref, near_ref, max_ref, total_ref, blocks, queries):
    seq = pl.program_id(0)
    half = kept_ref.shape[1]
    blocks[0] = own_ref[0, 0]
    blocks[1] = near_ref[0, 0]
    load_queries(queries, kept_ref, got_ref)
    visit = functools.partial(forward_visit, blocks, queries, max_ref.at[0], total_ref.at[0])
    own_visits(peers, info_ref, seq, half, visit)


def attend_near(info, kept, got, own, near):
    steps, _, block_len, _ = own.shape
    peers = info.shape[1] - 3
    half = block_len // 2
    size = GROUP * HEAD
    height = HEAD + SUM_ROWS
    queries = pl.BlockSpec((size, half), lambda s, g, info: (g, s))
    block = pl.BlockSpec((1, 1, block_len, PAIR), lambda s, g, info: (s, g, 0, 0))
    state = lambda height: pl.BlockSpec(
        (1, GROUP, height, block_len), lambda s, g, info: (g, 0, 0, s)
    )
    work = steps * HEADS * block_len * block_len
    return pl.pallas_call(
        functools.partial(near_kernel, peers),
        grid_spec=pltpu.PrefetchScalarGridSpec(
            num_scalar_prefetch=1,
            grid=(steps, KV_HEADS),
            in_specs=[queries, queries, block, block],
            out_specs=[state(1), state(height)],
            scratch_shapes=[
                pltpu.VMEM((2, block_len, PAIR), BF16),
                pltpu.VMEM((GROUP, PAIR, block_len), BF16),
            ],
        ),
        out_shape=[
            jax.ShapeDtypeStruct((KV_HEADS, GROUP, 1, steps * block_len), F32),
            jax.ShapeDtypeStruct((KV_HEADS, GROUP, height, steps * block_len), F32),
        ],
        compiler_params=params(),
        cost_estimate=pl.CostEstimate(
            flops=2 * 2 * 256 * work, bytes_accessed=8 * 1024 * 1024, transcendentals=work
        ),
        name="attend_near",
    )(info, kept, got, own, near)


def forward_kernel(counts, info_ref, kept_ref, got_ref, near_max, near_total, *refs):
    peers, arrays = len(counts), sum(counts)
    kv_refs = refs[:arrays]
    out_ref, kept16_ref, got16_ref, lse_ref = refs[arrays : arrays + 4]
    blocks, queries, row_max, total = refs[arrays + 4 :]
    seq = pl.program_id(0)
    half = kept_ref.shape[1]
    load_blocks(blocks, counts, kv_refs, seq)
    load_queries(queries, kept_ref, got_ref)
    row_max[...] = near_max[0]
    total[...] = near_total[0]
    visit = functools.partial(forward_visit, blocks, queries, row_max, total)
    other_visits(peers, info_ref, seq, half, visit)
    for h in range(GROUP):
        head = slice(h * HEAD, (h + 1) * HEAD)
        row_sum = total[h, HEAD : HEAD + 1, :]
        result = total[h, :HEAD, :] / row_sum
        out_ref[head, :] = result
        kept16_ref[head, :] = result[:, :half].astype(BF16)
        got16_ref[head, :] = result[:, half:].astype(BF16)
        lse_ref[h : h + 1, :] = row_max[h] + jnp.log2(row_sum)


def attention_specs(group, half):
    across = lambda height: pl.BlockSpec((height, 2 * half), lambda s, info: (0, s))
    across_half = lambda height, at=0: pl.BlockSpec((height, half), lambda s, info: (at, s))

    def block(whole):
        return pl.BlockSpec(
            (1, 1, 2 * half, PAIR), lambda s, info: (s if whole else 0, group, 0, 0)
        )

    return across, across_half, block


def attend(info, kept, got, near, blocks, group):
    peers = len(blocks)
    counts = tuple(len(b) for b in blocks)
    arrays = [a for b in blocks for a in b]
    steps, _, block_len, _ = arrays[0].shape
    half = block_len // 2
    rows = steps * block_len
    size = GROUP * HEAD
    across, across_half, block = attention_specs(group, half)
    work = steps * GROUP * block_len * peers * block_len
    return pl.pallas_call(
        functools.partial(forward_kernel, counts),
        grid_spec=pltpu.PrefetchScalarGridSpec(
            num_scalar_prefetch=1,
            grid=(steps,),
            in_specs=[across_half(size, group)] * 2
            + [
                pl.BlockSpec((1, GROUP, a.shape[2], block_len), lambda s, info: (group, 0, 0, s))
                for a in near
            ]
            + [block(len(b) == 1) for b in blocks for _ in b],
            out_specs=[across(size), across_half(size), across_half(size), across(8)],
            scratch_shapes=[
                pltpu.VMEM((peers, block_len, PAIR), BF16),
                pltpu.VMEM((GROUP, PAIR, block_len), BF16),
                pltpu.VMEM((GROUP, 1, block_len), F32),
                pltpu.VMEM((GROUP, HEAD + SUM_ROWS, block_len), F32),
            ],
        ),
        out_shape=[
            jax.ShapeDtypeStruct((size, rows), F32),
            jax.ShapeDtypeStruct((size, rows // 2), BF16),
            jax.ShapeDtypeStruct((size, rows // 2), BF16),
            jax.ShapeDtypeStruct((8, rows), F32),
        ],
        compiler_params=params(),
        cost_estimate=pl.CostEstimate(
            flops=2 * 2 * 256 * work, bytes_accessed=4 * size * rows, transcendentals=work
        ),
        name="attend",
    )(info, kept, got, *near, *arrays)


def backward_kernel(near, counts, shared, info_ref, *refs):
    count, arrays = len(counts), sum(counts)
    (kept_ref, got_ref, dkept_ref, dgot_ref, out_ref, lse_ref) = refs[:6]
    refs = refs[6:]
    if near:
        (cos_kept, sin_kept, cos_got, sin_got, dq_in) = refs[:5]
        refs = refs[5:]
    kv_refs = refs[:arrays]
    dq_refs = refs[arrays + shared : arrays + shared + (2 if near else 1)]
    refs = refs[arrays + shared + len(dq_refs) :]
    dkv_refs = refs[:count]
    blocks, grads, queries, douts, delta, dq = refs[count:]
    seq = pl.program_id(0)
    half = kept_ref.shape[1]
    peers = info_ref.shape[1] - 3
    load_blocks(blocks, counts, kv_refs, seq)
    for k in range(count):
        grads[k] = jnp.zeros((PAIR, 2 * half), F32)
    for h in range(GROUP):
        head = slice(h * HEAD, (h + 1) * HEAD)
        zeros = jnp.zeros((HEAD, 2 * half), BF16)
        dout = jnp.concatenate([dkept_ref[head, :], dgot_ref[head, :]], axis=1)
        queries[h, :HEAD, :half] = kept_ref[head, :]
        queries[h, :HEAD, half:] = got_ref[head, :]
        queries[h, HEAD:, :] = zeros
        douts[h, :HEAD, :] = zeros
        douts[h, HEAD:, :] = dout
        delta[h] = jnp.sum(dout.astype(F32) * out_ref[head, :], axis=0, keepdims=True)
        dq[h] = dq_in[h] if near else jnp.zeros((HEAD, 2 * half), F32)

    def visit(k, lanes, width, keys, diagonal):
        k = k if near else k - 2
        kv = blocks[k, :keys, :]
        keys_t = kv.T[:HEAD]
        heads = range(GROUP)
        scores = [matmul(kv, queries[h, :, lanes]) for h in heads]
        dprobs = [matmul(kv, douts[h, :, lanes]) for h in heads]
        probs = [jnp.exp2(scores[h] - lse_ref[h : h + 1, lanes]) for h in heads]
        if diagonal is not None:
            mask = key_mask(keys, width, diagonal)
            probs = [jnp.where(mask, a, 0.0) for a in probs]
        dscores = [(probs[h] * (dprobs[h] - delta[h, :, lanes])).astype(BF16) for h in heads]
        probs = [a.astype(BF16) for a in probs]
        dkeys = sum(matmul_trail(queries[h, :HEAD, lanes], dscores[h]) for h in heads)
        dvalues = sum(matmul_trail(douts[h, HEAD:, lanes], probs[h]) for h in heads)
        grads[k, :HEAD, :keys] += dkeys
        grads[k, HEAD:, :keys] += dvalues
        for h in heads:
            dq[h, :, lanes] += matmul(keys_t, dscores[h])

    row = lax.broadcasted_iota(jnp.int32, (PAIR, 1), 0)
    unit = jnp.where(row < HEAD, LN_2, 1.0)
    if near:
        own_visits(peers, info_ref, seq, half, visit)
    else:
        other_visits(peers, info_ref, seq, half, visit)
    for k in range(count):
        dkv_refs[k][0, 0] = (grads[k] * unit).astype(BF16).T
    if not near:
        dq_refs[0][...] = dq[...]
        return
    for h in range(GROUP):
        for at, dq_ref, cos_ref, sin_ref in (
            (0, dq_refs[0], cos_kept, sin_kept),
            (half, dq_refs[1], cos_got, sin_got),
        ):
            first = dq[h, :HALF, at : at + half] * 0.125
            second = dq[h, HALF:, at : at + half] * 0.125
            cos, sin = cos_ref[...], sin_ref[...]
            dq_ref[h * HEAD : h * HEAD + HALF, :] = (first * cos + second * sin).astype(BF16)
            dq_ref[h * HEAD + HALF : (h + 1) * HEAD, :] = (second * cos - first * sin).astype(BF16)


def attend_back(near, info, rows_in, extra, blocks, group, shared):
    count = len(blocks)
    counts = tuple(len(b) for b in blocks)
    arrays = [a for b in blocks for a in b]
    steps, _, block_len, _ = arrays[0].shape
    steps = info.shape[0]
    half = block_len // 2
    rows = steps * block_len
    size = GROUP * HEAD
    across, across_half, block = attention_specs(group, half)
    state = pl.BlockSpec((GROUP, HEAD, block_len), lambda s, info: (0, 0, s))
    pair_t = pltpu.VMEM((GROUP, PAIR, block_len), BF16)
    work = steps * GROUP * block_len * count * block_len
    inputs = (info, *rows_in, *extra, *arrays)
    if near:
        dq_specs = [across_half(size)] * 2
        dq_shapes = [jax.ShapeDtypeStruct((size, rows // 2), BF16)] * 2
    else:
        dq_specs = [state]
        dq_shapes = [jax.ShapeDtypeStruct((GROUP, HEAD, rows), F32)]
    return pl.pallas_call(
        functools.partial(backward_kernel, near, counts, len(shared)),
        grid_spec=pltpu.PrefetchScalarGridSpec(
            num_scalar_prefetch=1,
            grid=(steps,),
            in_specs=[across_half(size, group)] * 4
            + [across(size), across(8)]
            + ([across_half(HALF)] * 4 + [state] if near else [])
            + [block(len(b) == 1) for b in blocks for _ in b]
            + [pl.BlockSpec(memory_space=pl.ANY)] * len(shared),
            out_specs=dq_specs + [block(True)] * count,
            scratch_shapes=[
                pltpu.VMEM((count, block_len, PAIR), BF16),
                pltpu.VMEM((count, PAIR, block_len), F32),
                pair_t,
                pair_t,
                pltpu.VMEM((GROUP, 1, block_len), F32),
                pltpu.VMEM((GROUP, HEAD, block_len), F32),
            ],
        ),
        out_shape=dq_shapes
        + [jax.ShapeDtypeStruct((steps, KV_HEADS, block_len, PAIR), BF16)] * count,
        input_output_aliases={len(inputs) + i: len(dq_shapes) + i for i in range(len(shared))},
        compiler_params=params(),
        cost_estimate=pl.CostEstimate(
            flops=work if near else 5 * 2 * 256 * work,
            bytes_accessed=size * rows,
            transcendentals=0 if near else work,
        ),
        name="attend_back_near" if near else "attend_back",
    )(*inputs, *shared)


def norm_back(rows, inverse, gain, grad):
    scaled = grad * gain
    mean = jnp.mean(scaled * rows, axis=-1, keepdims=True)
    row_grad = inverse * scaled - rows * (inverse * inverse * inverse) * mean
    return row_grad, jnp.sum(grad * rows * inverse, axis=0, keepdims=True)


def middle_kernel(down_half, half, chunk, side_ref, *refs):
    kept_refs, back_refs = refs[:KV_HEADS], refs[KV_HEADS : 2 * KV_HEADS]
    x_ref, dy_ref, gains_ref, mine_ref, other_ref = refs[2 * KV_HEADS : 2 * KV_HEADS + 5]
    (
        out_ref,
        dh_ref,
        dkept_ref,
        dsent_ref,
        wide_kept,
        wide_sent,
        narrow_kept,
        narrow_sent,
        gain_ref,
    ) = refs[2 * KV_HEADS + 5 : 2 * KV_HEADS + 14]
    ff_weight, down_weight, out_weight, mixed, ff_grad, down_grad = refs[2 * KV_HEADS + 14 :]
    shards = mine_ref.shape[0]
    hidden_width = ff_weight.shape[2]
    width = x_ref.shape[1]
    depth = width // shards
    half_hidden = hidden_width // 2
    size = GROUP * HEAD
    side = side_ref[0]
    for z in range(shards):
        for ref, owner in ((mine_ref, side), (other_ref, 1 - side)):
            here = slice(z * depth, (z + 1) * depth)
            ff_weight[owner, here, :half_hidden] = ref[z, :depth, :]
            ff_weight[owner, here, half_hidden:] = ref[z, depth : 2 * depth, :]
            down_at = pl.multiple_of((2 * z + owner) * down_half, 16)
            down_weight[pl.ds(down_at, down_half), :] = ref[
                z, 2 * depth : 2 * depth + down_half, :width
            ]
        out_weight[here, :] = mine_ref[z, 2 * depth + down_half :, :width]
    starts = range(0, kept_refs[0].shape[1], half)
    for g in range(KV_HEADS):
        for at in starts:
            rows = slice(g * size, (g + 1) * size)
            mixed[rows, 2 * at : 2 * at + half] = kept_refs[g][:, at : at + half]
            mixed[rows, 2 * at + half : 2 * at + 2 * half] = back_refs[g][:, at : at + half]
    weight_out = out_weight[...]
    gain = gains_ref[1:2, :]
    rows = x_ref[...].astype(F32) + matmul_lead(mixed[...], weight_out)
    inverse = lax.rsqrt(jnp.mean(rows * rows, axis=-1, keepdims=True) + NORM_EPSILON)
    normed = (rows * inverse * gain).astype(BF16)
    normed_t = normed.T
    dy = dy_ref[...]
    result = rows
    dnormed = jnp.zeros(rows.shape, F32)
    for at in range(0, hidden_width, chunk):
        part = slice(at, at + chunk)
        gate = matmul(normed, ff_weight[0, :, part])
        upward = matmul(normed, ff_weight[1, :, part])
        dhidden = matmul_trail(dy, down_weight[part, :])
        sigmoid = jax.nn.sigmoid(gate)
        silu = gate * sigmoid
        hidden = (silu * upward).astype(BF16)
        dgate = (dhidden * upward * sigmoid * (1.0 + gate * (1.0 - sigmoid))).astype(BF16)
        dup = (dhidden * silu).astype(BF16)
        result = result + matmul(hidden, down_weight[part, :])
        down_grad[part, :] = matmul_lead(hidden, dy).astype(BF16)
        ff_grad[0, :, part] = matmul(normed_t, dgate).astype(BF16)
        ff_grad[1, :, part] = matmul(normed_t, dup).astype(BF16)
        dnormed = dnormed + (
            matmul_trail(dgate, ff_weight[0, :, part]) + matmul_trail(dup, ff_weight[1, :, part])
        )
    out_ref[...] = result.astype(BF16)
    row_grad, gain_grad = norm_back(rows, inverse, gain, dnormed)
    gain_ref[...] = jnp.broadcast_to(gain_grad, gain_ref.shape)
    drows = dy.astype(F32) + row_grad
    dh_ref[...] = drows
    drows = drows.astype(BF16)
    out_grad = matmul(mixed[...], drows).astype(BF16)
    dout = matmul_trail(weight_out, drows).astype(BF16)
    for at in starts:
        dkept_ref[:, at : at + half] = dout[:, 2 * at : 2 * at + half]
        dsent_ref[:, at : at + half] = dout[:, 2 * at + half : 2 * at + 2 * half]
    wide_kept[...] = ff_grad[side]
    wide_sent[...] = ff_grad[1 - side]
    for z in range(shards):
        mine = pl.multiple_of((2 * z + side) * down_half, 16)
        other = pl.multiple_of((2 * z + 1 - side) * down_half, 16)
        narrow_kept[z, :down_half, :] = down_grad[pl.ds(mine, down_half), :]
        narrow_sent[z, :down_half, :] = down_grad[pl.ds(other, down_half), :]
        out_rows = out_grad[z * depth : (z + 1) * depth, :]
        narrow_kept[z, down_half:, :] = out_rows
        narrow_sent[z, down_half:, :] = out_rows


def middle(side, kept, back, inputs, dy, gains, mine, other, block_len, chunk=512):
    rows, width = inputs.shape
    shards, packed_rows, half_hidden = mine.shape
    hidden_width = 2 * half_hidden
    down_half = hidden_width // shards // 2
    wide = (width, hidden_width)
    narrow = (shards, packed_rows - 2 * width // shards, width)
    half = block_len // 2
    shape = jax.ShapeDtypeStruct
    work = 3 * 2 * rows * width * (3 * hidden_width + width)
    vmem = pl.BlockSpec(memory_space=pltpu.VMEM)
    return pl.pallas_call(
        functools.partial(middle_kernel, down_half, half, chunk),
        in_specs=[pl.BlockSpec(memory_space=pltpu.SMEM)] + [vmem] * (2 * KV_HEADS + 5),
        out_specs=[vmem] * 9,
        scratch_shapes=[
            pltpu.VMEM((2, width, hidden_width), BF16),
            pltpu.VMEM((hidden_width, width), BF16),
            pltpu.VMEM((HEADS * HEAD, width), BF16),
            pltpu.VMEM((HEADS * HEAD, rows), BF16),
            pltpu.VMEM((2, width, hidden_width), BF16),
            pltpu.VMEM((hidden_width, width), BF16),
        ],
        out_shape=[
            shape((rows, width), BF16),
            shape((rows, width), F32),
            shape((HEADS * HEAD, rows // 2), BF16),
            shape((HEADS * HEAD, rows // 2), BF16),
            shape(wide, BF16),
            shape(wide, BF16),
            shape(narrow, BF16),
            shape(narrow, BF16),
            shape(gains.shape, F32),
        ],
        compiler_params=params(),
        cost_estimate=pl.CostEstimate(
            flops=work, bytes_accessed=30 * 1024 * 1024, transcendentals=rows * hidden_width
        ),
        name="middle",
    )(side, *kept, *back, inputs, dy, gains, mine, other)


def exit_query_kernel(*refs):
    kept_refs, back_refs = refs[:KV_HEADS], refs[KV_HEADS : 2 * KV_HEADS]
    normed_ref, weight_ref, grad_ref, da_ref, dq = refs[2 * KV_HEADS :]
    half = kept_refs[0].shape[1]
    size = GROUP * HEAD
    for g in range(KV_HEADS):
        dq[g * size : (g + 1) * size, :half] = kept_refs[g][...]
        dq[g * size : (g + 1) * size, half:] = back_refs[g][...]
    rows = dq[...].T
    da_ref[...] = matmul_trail(rows, weight_ref[:, : HEADS * HEAD])
    grad = matmul_lead(normed_ref[...], rows)

    @pl.when(pl.program_id(0) == 0)
    def _():
        grad_ref[...] = grad

    @pl.when(pl.program_id(0) > 0)
    def _():
        grad_ref[...] += grad


def exit_query(kept, back, normed, weight, block_len):
    rows, width = normed.shape
    size = GROUP * HEAD
    half = block_len // 2
    down = pl.BlockSpec((block_len, width), lambda s: (s, 0))
    return pl.pallas_call(
        exit_query_kernel,
        grid=(rows // block_len,),
        in_specs=[pl.BlockSpec((size, half), lambda s: (0, s))] * (2 * KV_HEADS)
        + [down, pl.BlockSpec(weight.shape, lambda s: (0, 0))],
        out_specs=[pl.BlockSpec((width, HEADS * HEAD), lambda s: (0, 0)), down],
        out_shape=[
            jax.ShapeDtypeStruct((width, HEADS * HEAD), F32),
            jax.ShapeDtypeStruct((rows, width), F32),
        ],
        scratch_shapes=[pltpu.VMEM((HEADS * HEAD, block_len), BF16)],
        compiler_params=params(),
        cost_estimate=pl.CostEstimate(
            flops=4 * rows * width * width, bytes_accessed=16 * rows * width, transcendentals=0
        ),
        name="exit_query",
    )(*kept, *back, normed, weight)


def exit_kernel(counts, side_ref, *refs):
    arrays = sum(counts)
    part_refs = refs[:arrays]
    (normed_ref, weight_ref, gq_ref, da_ref, x_ref, dh_ref, gains_ref, gain_mlp_ref) = refs[
        arrays : arrays + 8
    ]
    cos_ref, low_ref, high_ref, dx_ref, kept_ref, sent_ref, grad, gain_acc = refs[arrays + 8 :]
    step = pl.program_id(0)
    side = side_ref[0]
    cols = kept_ref.shape[1]
    wide = HEADS * HEAD

    @pl.when(step == 0)
    def _():
        grad[...] = jnp.zeros(grad.shape, F32)
        gain_acc[...] = jnp.zeros(gain_acc.shape, F32)

    parts = []
    at = 0
    for count in counts:
        parts.append(choose(part_refs[at : at + count], step))
        at += count
    normed = normed_ref[...]
    dnormed = da_ref[...]
    kv_at = weight_ref.shape[1] - KV_HEADS * PAIR
    for g in range(KV_HEADS):
        dkv = sum((part[0, g].astype(F32) for part in parts[1:]), parts[0][0, g].astype(F32))
        turned = (
            dkv * cos_ref[...]
            - pltpu.roll(dkv, HALF, 1) * low_ref[...]
            - pltpu.roll(dkv, PAIR - HALF, 1) * high_ref[...]
        ).astype(BF16)
        here = slice(kv_at + g * PAIR, kv_at + (g + 1) * PAIR)
        dnormed = dnormed + matmul_trail(turned, weight_ref[:, here])
        grad[:, g * PAIR : (g + 1) * PAIR] += matmul_lead(normed, turned)
    rows = x_ref[...].astype(F32)
    inverse = lax.rsqrt(jnp.mean(rows * rows, axis=-1, keepdims=True) + NORM_EPSILON)
    row_grad, gain_grad = norm_back(rows, inverse, gains_ref[0:1, :], dnormed)
    gain_acc[0:1, :] += gain_grad
    dx_ref[...] = (dh_ref[...] + row_grad).astype(BF16)

    @pl.when(step == pl.num_programs(0) - 1)
    def _():
        width = normed.shape[1]
        gains = jnp.concatenate(
            [
                jnp.zeros((HEAD, width), F32),
                gain_acc[0:1, :],
                gain_mlp_ref[0:1, :],
                jnp.zeros((HEAD - 2, width), F32),
            ],
            axis=0,
        ).T

        def write_low(ref):
            ref[...] = gq_ref[:, :cols].astype(BF16)

        def write_high(ref):
            ref[:, :PAIR] = gains.astype(BF16)
            ref[:, : wide - cols] = gq_ref[:, cols:].astype(BF16)
            ref[:, PAIR:] = grad[...].astype(BF16)

        @pl.when(side == 0)
        def _():
            write_low(kept_ref)
            write_high(sent_ref)

        @pl.when(side != 0)
        def _():
            write_high(kept_ref)
            write_low(sent_ref)


def leave(side, parts, normed, weight, grad_query, da, inputs, dh, gains, gain_mlp, tables, block_len):
    rows, width = normed.shape
    cols = weight.shape[1] // 2
    counts = tuple(len(p) for p in parts)
    arrays = [a for p in parts for a in p]
    down = pl.BlockSpec((block_len, width), lambda s, side: (s, 0))
    fixed = lambda shape: pl.BlockSpec(shape, lambda s, side: (0,) * len(shape))

    def block(whole):
        return pl.BlockSpec(
            (1, KV_HEADS, block_len, PAIR), lambda s, side: (s if whole else 0, 0, 0, 0)
        )

    table = pl.BlockSpec((block_len, PAIR), lambda s, side: (s, 0))
    return pl.pallas_call(
        functools.partial(exit_kernel, counts),
        grid_spec=pltpu.PrefetchScalarGridSpec(
            num_scalar_prefetch=1,
            grid=(rows // block_len,),
            in_specs=[block(len(p) == 1) for p in parts for _ in p]
            + [down, fixed(weight.shape), fixed(grad_query.shape), down, down, down]
            + [fixed(gains.shape), fixed(gain_mlp.shape)]
            + [table] * 3,
            out_specs=[down, fixed((width, cols)), fixed((width, cols))],
            scratch_shapes=[
                pltpu.VMEM((width, KV_HEADS * PAIR), F32),
                pltpu.VMEM((8, width), F32),
            ],
        ),
        out_shape=[
            jax.ShapeDtypeStruct((rows, width), BF16),
            jax.ShapeDtypeStruct((width, cols), BF16),
            jax.ShapeDtypeStruct((width, cols), BF16),
        ],
        compiler_params=params(),
        name="leave",
    )(side, *arrays, normed, weight, grad_query, da, inputs, dh, gains, gain_mlp, *tables)


def finish_kernel(side_ref, mine_ref, other_ref, query_ref, key_ref, value_ref, gains_ref, both):
    cols = mine_ref.shape[1]
    width = query_ref.shape[1]
    mine = pl.multiple_of(side_ref[0] * cols, 128)
    other = pl.multiple_of((1 - side_ref[0]) * cols, 128)
    both[:, pl.ds(mine, cols)] = mine_ref[...].astype(F32)
    both[:, pl.ds(other, cols)] = other_ref[...].astype(F32)
    query_ref[...] = both[:, :width]
    gains_ref[...] = both[:, width - HEAD : width + HEAD].T[HEAD : HEAD + 8, :]
    for g in range(KV_HEADS):
        at = width + HEAD + g * PAIR
        kv = both[:, at : at + PAIR]
        key_ref[:, g * HEAD : (g + 1) * HEAD] = kv[:, :HEAD]
        value_ref[:, g * HEAD : (g + 1) * HEAD] = kv[:, HEAD:]


def finish(side, mine, other, width):
    depth, cols = mine.shape
    vmem = pl.BlockSpec(memory_space=pltpu.VMEM)
    shape = jax.ShapeDtypeStruct
    return pl.pallas_call(
        finish_kernel,
        in_specs=[pl.BlockSpec(memory_space=pltpu.SMEM), vmem, vmem],
        out_specs=[vmem] * 4,
        out_shape=[
            shape((depth, width), F32),
            shape((depth, KV_HEADS * HEAD), F32),
            shape((depth, KV_HEADS * HEAD), F32),
            shape((8, depth), F32),
        ],
        scratch_shapes=[pltpu.VMEM((depth, 2 * cols), F32)],
        compiler_params=params(),
        name="finish",
    )(side, mine, other)


def pack_kv(key_part, value_part):
    depth = key_part.shape[0]
    both = jnp.stack(
        [key_part.reshape(depth, KV_HEADS, HEAD), value_part.reshape(depth, KV_HEADS, HEAD)], axis=2
    )
    return both.reshape(depth, KV_HEADS * PAIR)


def rope_tables(positions):
    freqs = ROPE_BASE ** (-jnp.arange(HALF, dtype=F32) * 2.0 / HEAD)
    angle = positions.reshape(1, -1).astype(F32) * freqs[:, None]
    cos_t, sin_t = jnp.cos(angle), jnp.sin(angle)
    cos, sin = cos_t.T, sin_t.T
    nothing = jnp.zeros_like(cos)
    ones = jnp.ones_like(cos)
    return (
        cos_t,
        sin_t,
        jnp.concatenate([cos, cos, ones, ones], axis=1),
        jnp.concatenate([nothing, sin, nothing, nothing], axis=1),
        jnp.concatenate([-sin, nothing, nothing, nothing], axis=1),
    )


def per_device(
    hidden_in,
    out_grad,
    block_slot,
    rope_pos,
    w_query,
    w_key,
    w_value,
    w_out,
    w_gate,
    w_up,
    w_down,
    gain_attn,
    gain_mlp,
):
    seq_count, block_len, width = hidden_in.shape
    row_count = seq_count * block_len
    hidden_width = w_gate.shape[1]
    depth = w_query.shape[0]
    cycle_index = lax.axis_index(CTX)
    cycle_size = lax.axis_size(CTX)
    shard_index = lax.axis_index("shard")
    shards = lax.axis_size("shard")
    side = lax.axis_index("core")

    def whole(parts):
        rows = parts[0].shape[0]
        out = jnp.zeros((shards * rows,) + parts[0].shape[1:], parts[0].dtype)
        for t, part in enumerate(parts):
            out = lax.dynamic_update_slice_in_dim(out, part, ((shard_index - t) % shards) * rows, 0)
        return out

    packed = jnp.concatenate(
        [
            w_query,
            gain_attn[:, None],
            gain_mlp[:, None],
            jnp.zeros((depth, HEAD - 2), BF16),
            pack_kv(w_key, w_value),
        ],
        axis=1,
    )
    cols = packed.shape[1] // 2
    mine = ring_pieces(lax.dynamic_slice_in_dim(packed, side * cols, cols, 1), "shard")
    tables = rope_tables(rope_pos)
    first_rows = hidden_in.reshape(row_count, width)
    own_piece, *got_pieces = mine
    got_pieces, tables, first_rows = tied(got_pieces, tables, first_rows)
    mine = [own_piece, *got_pieces]
    pieces = mine + [flip(a, 1) for a in mine]
    place = jnp.stack([shard_index, side]).astype(jnp.int32)
    if depth % 16:
        pieces = [whole(pieces[:shards]), whole(pieces[shards:])]
        place = jnp.stack([jnp.zeros_like(side), side]).astype(jnp.int32)

    down_half = w_down.shape[0] // 2
    half_hidden = hidden_width // 2
    wide = jnp.where(side == 0, w_gate, w_up)
    narrow = jnp.concatenate(
        [lax.dynamic_slice_in_dim(w_down, side * down_half, down_half, 0), w_out], axis=0
    )
    later_weights = jnp.concatenate(
        [
            wide[:, :half_hidden],
            wide[:, half_hidden:],
            jnp.pad(narrow, ((0, 0), (0, half_hidden - width))),
        ],
        axis=0,
    )
    later_weights = after(later_weights, *mine[1:])
    later_weights = lax.all_gather(later_weights, "shard", axis=0, tiled=False)

    cycle = jnp.arange(cycle_size, dtype=jnp.int32)
    at_slot = jnp.sum(
        jnp.where(
            block_slot[:, :, None] == cycle[None, None, :],
            (cycle ^ cycle_index)[None, :, None],
            0,
        ),
        axis=1,
    )
    own_slot = lax.dynamic_index_in_dim(block_slot, cycle_index, 1, keepdims=True)
    near_slot = lax.dynamic_index_in_dim(block_slot, cycle_index ^ 1, 1, keepdims=True)
    info = jnp.concatenate(
        [
            at_slot,
            jnp.minimum(own_slot, near_slot),
            jnp.maximum(own_slot, near_slot),
            (near_slot > own_slot).astype(jnp.int32),
        ],
        axis=1,
    ).astype(jnp.int32)

    half = block_len // 2

    def halves(value, second):
        starts = range(second * half, row_count, block_len)
        return jnp.concatenate([value[:, at : at + half] for at in starts], axis=1)

    turns = jnp.concatenate(tables[:2], axis=0)
    turns_got = flip(halves(turns, 1), 1)
    turns = halves(turns, 0)
    turns = (turns[:HALF], turns[HALF:], turns_got[:HALF], turns_got[HALF:])

    flat_in = hidden_in.reshape(row_count, width)
    q_kept, q_sent, kv, normed_attn, full_packed, gains = entry(
        place, pieces, first_rows, tables, block_len
    )
    q_got = flip(q_sent, 1)
    near, blocks = gather_flipped(kv, functools.partial(attend_near, info, q_kept, q_got))
    attended = []
    last_info = info
    for g in range(KV_HEADS):
        if g == KV_HEADS - 1:
            last_info, later_weights, *attended = tied(info, later_weights, *attended)
        attended.append(attend(last_info, q_kept, q_got, near, blocks, g))
    back = [flip(a[2], 1) for a in attended]

    side_ref = side.reshape(1).astype(jnp.int32)
    (
        block_out,
        middle_grad,
        dout_kept,
        dout_sent,
        wide_kept,
        wide_sent,
        narrow_kept,
        narrow_sent,
        gain_mlp_grad,
    ) = middle(
        side_ref,
        [a[1] for a in attended],
        back,
        flat_in,
        out_grad.reshape(row_count, width),
        gains,
        later_weights,
        flip(later_weights, 1),
        block_len,
    )

    dout_got = flip(dout_sent, 1)
    wide_got = flip(wide_sent, 1)
    narrow_got = flip(narrow_sent, 1)
    rows_in = [
        (q_kept, q_got, dout_kept, dout_got, attended[g][0], attended[g][3])
        for g in range(KV_HEADS)
    ]
    dq_far = []
    parts = []
    for g in range(KV_HEADS):
        mine = rows_in[g]
        if g == 1:
            early_wide = add_sent(wide_kept, wide_got)
            early_narrow = add_sent(narrow_kept, narrow_got)
            early_wide, early_narrow, *mine = lax.optimization_barrier(
                (early_wide, early_narrow, *mine, *parts)
            )
            mine, parts = mine[:6], mine[6:]
            early_wide = lax.psum_scatter(early_wide, "shard", scatter_dimension=0, tiled=True)
            early_narrow = lax.psum_scatter(early_narrow, "shard", scatter_dimension=0, tiled=False)
        dq, *parts = attend_back(False, info, mine, (), blocks[2:], g, parts)
        dq_far.append(dq)

    dq_kept, dq_back = [], []

    def near_step(g, info, grads):
        first, second, *grads = attend_back(
            True, info, rows_in[g], (*turns, dq_far[g]), blocks[:2], g, grads
        )
        dq_kept.append(first)
        dq_back.append(flip(second, 1))
        return grads

    steps = [functools.partial(near_step, g) for g in range(KV_HEADS)]
    parts = scatter_flipped(parts, info, steps)
    grad_query, attn_grad = exit_query(dq_kept, dq_back, normed_attn, full_packed, block_len)
    early_wide, early_narrow, grad_query, attn_grad, *rest = tied(
        early_wide, early_narrow, grad_query, attn_grad, *(a for p in parts for a in p)
    )
    parts = [tuple(rest.pop(0) for _ in p) for p in parts]
    wide_got, narrow_got = flip(early_wide, 2), flip(early_narrow, 4)
    in_grad, late_kept, late_sent = leave(
        side_ref,
        parts,
        normed_attn,
        full_packed,
        grad_query,
        attn_grad,
        flat_in,
        middle_grad,
        gains,
        gain_mlp_grad,
        tables[2:],
        block_len,
    )
    early_wide = add_sent(early_wide, wide_got)
    early_narrow = add_sent(early_narrow, narrow_got)
    early_wide, early_narrow, late_kept = tied(early_wide, early_narrow, late_kept)
    early_wide = add_sent(early_wide, flip(early_wide, 4))
    early_narrow = add_sent(early_narrow, flip(early_narrow, 2))
    bit = 8
    while bit < cycle_size:
        early_wide = add_sent(early_wide, flip(early_wide, bit))
        early_narrow = add_sent(early_narrow, flip(early_narrow, bit))
        bit *= 2
    in_grad = in_grad.reshape(hidden_in.shape)
    block_out = block_out.reshape(hidden_in.shape)
    late = add_sent(late_kept, flip(late_sent, 1)).reshape(shards, depth, cols)
    share = lambda by: lax.dynamic_index_in_dim(late, (shard_index + by) % shards, 0, keepdims=False)
    arrived = [shift(share(by), "shard", by) for by in range(1, shards)]
    late = sum((a.astype(F32) for a in arrived), share(0).astype(F32)).astype(BF16)
    bit = 2
    while bit < cycle_size:
        late = add_sent(late, flip(late, bit))
        bit *= 2
    grad_query, grad_key, grad_value, gain_grads = finish(side_ref, late, flip(late, 1), width)
    other_wide = flip(early_wide, 1)
    down_own = early_narrow[:down_half]
    down_other = flip(down_own, 1)
    grad_down = jnp.where(
        side == 0,
        jnp.concatenate([down_own, down_other], axis=0),
        jnp.concatenate([down_other, down_own], axis=0),
    )
    return (
        block_out,
        in_grad,
        grad_query,
        grad_key,
        grad_value,
        early_narrow[down_half:].astype(F32),
        jnp.where(side == 0, early_wide, other_wide).astype(F32),
        jnp.where(side == 0, other_wide, early_wide).astype(F32),
        grad_down.astype(F32),
        gain_grads[0],
        gain_grads[1],
    )


def solution(mesh):
    ctx, shards = mesh.shape["ctx"], mesh.shape["shard"]
    split_mesh = Mesh(mesh.devices.reshape(ctx // 4, 2, 2, shards), CTX + ("shard",))
    rows = P("shard", CTX, None)
    split = P("shard", None)
    return jax.shard_map(
        per_device,
        mesh=split_mesh,
        in_specs=(rows, rows, split, P("shard", CTX)) + (split,) * 7 + (P("shard"),) * 2,
        out_specs=(rows, rows) + (split,) * 7 + (P("shard"),) * 2,
        check_vma=False,
    )
```

```python
import functools

import jax
import jax.numpy as jnp
from jax import lax
from jax.experimental import pallas as pl
from jax.experimental.pallas import tpu as pltpu
from jax.sharding import Mesh
from jax.sharding import PartitionSpec as P

HEADS = 9
KV_HEADS = 3
HEAD = 64
GROUP = HEADS // KV_HEADS
PAIR = 2 * HEAD
HALF = HEAD // 2

NORM_EPSILON = 1e-05
ROPE_BASE = 100000.0
LOG2_E = 1.4426950408889634
LN_2 = 0.6931471805599453
MASKED_SCORE = -1e30
SUM_ROWS = 16
VMEM_BYTES = 56 * 1024 * 1024

CHIPS = ("cy", "cx")
CTX = CHIPS + ("core",)

F32 = jnp.float32
BF16 = jnp.bfloat16


def params():
    return pltpu.CompilerParams(vmem_limit_bytes=VMEM_BYTES)


def matmul(left, right):
    return jnp.dot(left, right, preferred_element_type=F32)


def matmul_lead(left, right):
    return lax.dot_general(left, right, (((0,), (0,)), ((), ())), preferred_element_type=F32)


def matmul_trail(left, right):
    return lax.dot_general(left, right, (((1,), (1,)), ((), ())), preferred_element_type=F32)


def flip(value, bit):
    peers = lax.axis_size(CTX)
    return lax.ppermute(value, CTX, [(i, i ^ bit) for i in range(peers)])


def shift(value, axis, by=1):
    peers = lax.axis_size(axis)
    return lax.ppermute(value, axis, [(i, (i + by) % peers) for i in range(peers)])


def ring_pieces(piece, axis):
    return [piece] + [shift(piece, axis, by) for by in range(1, lax.axis_size(axis))]


def after(value, *others):
    return lax.optimization_barrier((value,) + others)[0]


def gather_flipped(own, beside):
    peers = lax.axis_size(CTX)
    if peers == 8:
        by_x = flip(own, 2)
        by_y = flip(own, 4)
        near = flip(own, 1)
        result = beside(own, near)
        by_x, by_y, result = lax.optimization_barrier((by_x, by_y, result))
        first = flip(by_y[:1], 2)
        second = flip(by_x[1:], 4)
        same_core = [(own,), (by_x,), (by_y,), (first, second)]
        other_core = [(near,)] + [tuple(flip(a, 1) for a in block) for block in same_core[1:]]
        return result, [b for pair in zip(same_core, other_core) for b in pair]
    blocks = [own]
    bit = 1
    while bit < peers:
        blocks = blocks + [flip(b, bit) for b in blocks]
        bit *= 2
    return beside(blocks[0], blocks[1]), [(b,) for b in blocks]


def add_sent(kept, arrived):
    return (kept.astype(F32) + arrived.astype(F32)).astype(BF16)


def tied(value, *others):
    return lax.optimization_barrier((value,) + others)


def scatter_flipped(parts, info, steps):
    peers = len(parts) + 2
    result = ()
    if peers == 8:
        near = {k: flip(parts[k - 1], 1) for k in (6, 2, 4)}
        seq = lambda k, i: add_sent(parts[k - 2][i : i + 1], near[k][i : i + 1])
        result = steps[0](info, result)
        info, *sent = tied(info, seq(6, 0), seq(2, 0), seq(6, 1), seq(4, 1))
        arrived = [flip(a, bit) for a, bit in zip(sent, (2, 2, 4, 4))]
        for step in steps[1:]:
            result = step(info, result)
        result, *arrived = tied(result, *arrived)
        far_x, x_first, far_y, y_second = arrived
        y_first = flip(add_sent(seq(4, 0), far_x), 4)
        x_second = flip(add_sent(seq(2, 1), far_y), 2)
        own, own_sent = result
        own = add_sent(own, flip(own_sent, 1))
        return [(own,), (x_first, x_second), (y_first, y_second)]
    for step in steps:
        result = step(info, result)
    parts = list(result) + parts
    while peers > 1:
        peers //= 2
        parts = [add_sent(parts[k], flip(parts[k + peers], peers)) for k in range(peers)]
    return [(parts[0],)]


def entry_kernel(shards, width, place_ref, *refs):
    piece_refs = refs[: 2 * shards]
    (x_ref, cos_t_ref, sin_t_ref, cos_ref, low_ref, high_ref) = refs[2 * shards : 2 * shards + 6]
    kept_ref, sent_ref, kv_ref, normed_ref, packed_ref, gains_ref = refs[
        2 * shards + 6 : 2 * shards + 12
    ]
    (weight,) = refs[2 * shards + 12 :]
    half = kept_ref.shape[1]
    depth = piece_refs[0].shape[0]
    cols = piece_refs[0].shape[1]

    @pl.when(pl.program_id(0) == 0)
    def assemble():
        shard, side = place_ref[0], place_ref[1]
        for t in range(shards):
            row = pl.multiple_of(lax.rem(shard - t + shards, shards) * depth, 16)
            mine = pl.multiple_of(side * cols, 128)
            other = pl.multiple_of((1 - side) * cols, 128)
            weight[pl.ds(row, depth), pl.ds(mine, cols)] = piece_refs[t][...]
            weight[pl.ds(row, depth), pl.ds(other, cols)] = piece_refs[shards + t][...]
        packed_ref[...] = weight[...]
        gains_ref[...] = weight[:, 512:640].astype(F32).T[64:72, :]

    rows = x_ref[...].astype(F32)
    inverse = lax.rsqrt(jnp.mean(rows * rows, axis=-1, keepdims=True) + NORM_EPSILON)
    normed = (rows * inverse * gains_ref[0:1, :]).astype(BF16)
    normed_ref[...] = normed
    cos_t = cos_t_ref[...]
    sin_t = sin_t_ref[...]
    for chunk in range(5):
        lin = matmul(normed, weight[:, chunk * PAIR : (chunk + 1) * PAIR]).T
        for part in range(2):
            head = 2 * chunk + part
            if head < HEADS:
                first = lin[part * HEAD : part * HEAD + HALF]
                second = lin[part * HEAD + HALF : (part + 1) * HEAD]
                turned = jnp.concatenate(
                    [first * cos_t - second * sin_t, second * cos_t + first * sin_t], axis=0
                )
                turned = (turned * (0.125 * LOG2_E)).astype(BF16)
                kept_ref[head * HEAD : (head + 1) * HEAD, :] = turned[:, :half]
                sent_ref[head * HEAD : (head + 1) * HEAD, :] = turned[:, half:]
    for group in range(KV_HEADS):
        at = 5 * PAIR + group * PAIR
        lin = matmul(normed, weight[:, at : at + PAIR])
        turned = (
            lin * cos_ref[...]
            + pltpu.roll(lin, HALF, 1) * low_ref[...]
            + pltpu.roll(lin, PAIR - HALF, 1) * high_ref[...]
        )
        kv_ref[0, group] = turned.astype(BF16)


def choose(refs, seq):
    if len(refs) == 1:
        return refs[0][...]
    return jnp.where(seq == 0, refs[0][...], refs[1][...])


def entry(place, pieces, inputs, tables, block_len):
    shards = len(pieces) // 2
    rows, width = inputs.shape
    cos_t, sin_t, cos, low, high = tables
    depth, cols = pieces[0].shape
    steps = rows // block_len
    fixed = lambda shape: pl.BlockSpec(shape, lambda s, place: (0,) * len(shape))
    return pl.pallas_call(
        functools.partial(entry_kernel, shards, width),
        grid_spec=pltpu.PrefetchScalarGridSpec(
            num_scalar_prefetch=1,
            grid=(steps,),
            in_specs=[fixed((depth, cols)) for _ in pieces]
            + [pl.BlockSpec((block_len, width), lambda s, place: (s, 0))]
            + [pl.BlockSpec((HALF, block_len), lambda s, place: (0, s))] * 2
            + [pl.BlockSpec((block_len, PAIR), lambda s, place: (s, 0))] * 3,
            out_specs=[
                pl.BlockSpec((HEADS * HEAD, block_len // 2), lambda s, place: (0, s)),
                pl.BlockSpec((HEADS * HEAD, block_len // 2), lambda s, place: (0, s)),
                pl.BlockSpec((1, KV_HEADS, block_len, PAIR), lambda s, place: (s, 0, 0, 0)),
                pl.BlockSpec((block_len, width), lambda s, place: (s, 0)),
                fixed((width, 2 * cols)),
                fixed((8, width)),
            ],
            scratch_shapes=[pltpu.VMEM((width, 2 * cols), BF16)],
        ),
        out_shape=[
            jax.ShapeDtypeStruct((HEADS * HEAD, rows // 2), BF16),
            jax.ShapeDtypeStruct((HEADS * HEAD, rows // 2), BF16),
            jax.ShapeDtypeStruct((steps, KV_HEADS, block_len, PAIR), BF16),
            jax.ShapeDtypeStruct((rows, width), BF16),
            jax.ShapeDtypeStruct((width, 2 * cols), BF16),
            jax.ShapeDtypeStruct((8, width), F32),
        ],
        compiler_params=params(),
        name="entry",
    )(place, *pieces, inputs, cos_t, sin_t, cos, low, high)


def key_mask(keys, queries, first_query):
    key = lax.broadcasted_iota(jnp.int32, (keys, queries), 0)
    query = lax.broadcasted_iota(jnp.int32, (keys, queries), 1)
    return key <= query + first_query


def own_visits(peers, info_ref, seq, half, visit):
    visit(0, pl.ds(0, half), half, half, 0)
    visit(1, pl.ds(half, half), half, 2 * half, half)
    later = info_ref[seq, peers + 2]
    visit(1 - later, pl.ds(pl.multiple_of(later * half, 128), half), half, 2 * half, None)


def other_visits(peers, info_ref, seq, half, visit):
    first, second = info_ref[seq, peers], info_ref[seq, peers + 1]

    @pl.loop(0, first)
    def _(r):
        visit(info_ref[seq, r], pl.ds(0, 2 * half), 2 * half, 2 * half, None)

    @pl.loop(first + 1, second)
    def _(r):
        start = pl.multiple_of(info_ref[seq, peers + 2] * half, 128)
        visit(info_ref[seq, r], pl.ds(start, half), half, 2 * half, None)


def load_blocks(blocks, counts, refs, seq):
    at = 0
    for k, count in enumerate(counts):
        blocks[k] = choose(refs[at : at + count], seq)[0, 0]
        at += count


def load_queries(queries, kept_ref, got_ref):
    half = kept_ref.shape[1]
    for h in range(GROUP):
        head = slice(h * HEAD, (h + 1) * HEAD)
        queries[h, :HEAD, :half] = kept_ref[head, :]
        queries[h, :HEAD, half:] = got_ref[head, :]
        queries[h, HEAD:, :] = jnp.zeros((HEAD, 2 * half), BF16)


def forward_visit(blocks, queries, row_max, total, k, lanes, width, keys, diagonal):
    kv = blocks[k, :keys, :]
    values_t = jnp.concatenate([kv.T[HEAD:], jnp.ones((SUM_ROWS, keys), BF16)], axis=0)
    scores = [matmul(kv, queries[h, :, lanes]) for h in range(GROUP)]
    if diagonal is not None:
        mask = key_mask(keys, width, diagonal)
        scores = [jnp.where(mask, a, MASKED_SCORE) for a in scores]
    weights, fading = [], []
    for h in range(GROUP):
        new_max = jnp.max(scores[h], axis=0, keepdims=True)
        if diagonal is None:
            old_max = row_max[h, :, lanes]
            new_max = jnp.maximum(old_max, new_max)
            fading.append(jnp.exp2(old_max - new_max))
        row_max[h, :, lanes] = new_max
        weights.append(jnp.exp2(scores[h] - new_max).astype(BF16))
    for h in range(GROUP):
        product = matmul(values_t, weights[h])
        if diagonal is None:
            product = total[h, :, lanes] * fading[h] + product
        total[h, :, lanes] = product


def near_kernel(peers, info_ref, kept_ref, got_ref, own_ref, near_ref, max_ref, total_ref, blocks, queries):
    seq = pl.program_id(0)
    half = kept_ref.shape[1]
    blocks[0] = own_ref[0, 0]
    blocks[1] = near_ref[0, 0]
    load_queries(queries, kept_ref, got_ref)
    visit = functools.partial(forward_visit, blocks, queries, max_ref.at[0], total_ref.at[0])
    own_visits(peers, info_ref, seq, half, visit)


def attend_near(info, kept, got, own, near):
    steps, _, block_len, _ = own.shape
    peers = info.shape[1] - 3
    half = block_len // 2
    size = GROUP * HEAD
    height = HEAD + SUM_ROWS
    queries = pl.BlockSpec((size, half), lambda s, g, info: (g, s))
    block = pl.BlockSpec((1, 1, block_len, PAIR), lambda s, g, info: (s, g, 0, 0))
    state = lambda height: pl.BlockSpec(
        (1, GROUP, height, block_len), lambda s, g, info: (g, 0, 0, s)
    )
    work = steps * HEADS * block_len * block_len
    return pl.pallas_call(
        functools.partial(near_kernel, peers),
        grid_spec=pltpu.PrefetchScalarGridSpec(
            num_scalar_prefetch=1,
            grid=(steps, KV_HEADS),
            in_specs=[queries, queries, block, block],
            out_specs=[state(1), state(height)],
            scratch_shapes=[
                pltpu.VMEM((2, block_len, PAIR), BF16),
                pltpu.VMEM((GROUP, PAIR, block_len), BF16),
            ],
        ),
        out_shape=[
            jax.ShapeDtypeStruct((KV_HEADS, GROUP, 1, steps * block_len), F32),
            jax.ShapeDtypeStruct((KV_HEADS, GROUP, height, steps * block_len), F32),
        ],
        compiler_params=params(),
        cost_estimate=pl.CostEstimate(
            flops=2 * 2 * 256 * work, bytes_accessed=8 * 1024 * 1024, transcendentals=work
        ),
        name="attend_near",
    )(info, kept, got, own, near)


def forward_kernel(counts, info_ref, kept_ref, got_ref, near_max, near_total, *refs):
    peers, arrays = len(counts), sum(counts)
    kv_refs = refs[:arrays]
    out_ref, kept16_ref, got16_ref, lse_ref = refs[arrays : arrays + 4]
    blocks, queries, row_max, total = refs[arrays + 4 :]
    seq = pl.program_id(0)
    half = kept_ref.shape[1]
    load_blocks(blocks, counts, kv_refs, seq)
    load_queries(queries, kept_ref, got_ref)
    row_max[...] = near_max[0]
    total[...] = near_total[0]
    visit = functools.partial(forward_visit, blocks, queries, row_max, total)
    other_visits(peers, info_ref, seq, half, visit)
    for h in range(GROUP):
        head = slice(h * HEAD, (h + 1) * HEAD)
        row_sum = total[h, HEAD : HEAD + 1, :]
        result = total[h, :HEAD, :] / row_sum
        out_ref[head, :] = result
        kept16_ref[head, :] = result[:, :half].astype(BF16)
        got16_ref[head, :] = result[:, half:].astype(BF16)
        lse_ref[h : h + 1, :] = row_max[h] + jnp.log2(row_sum)


def attention_specs(group, half):
    across = lambda height: pl.BlockSpec((height, 2 * half), lambda s, info: (0, s))
    across_half = lambda height, at=0: pl.BlockSpec((height, half), lambda s, info: (at, s))

    def block(whole):
        return pl.BlockSpec(
            (1, 1, 2 * half, PAIR), lambda s, info: (s if whole else 0, group, 0, 0)
        )

    return across, across_half, block


def attend(info, kept, got, near, blocks, group):
    peers = len(blocks)
    counts = tuple(len(b) for b in blocks)
    arrays = [a for b in blocks for a in b]
    steps, _, block_len, _ = arrays[0].shape
    half = block_len // 2
    rows = steps * block_len
    size = GROUP * HEAD
    across, across_half, block = attention_specs(group, half)
    work = steps * GROUP * block_len * peers * block_len
    return pl.pallas_call(
        functools.partial(forward_kernel, counts),
        grid_spec=pltpu.PrefetchScalarGridSpec(
            num_scalar_prefetch=1,
            grid=(steps,),
            in_specs=[across_half(size, group)] * 2
            + [
                pl.BlockSpec((1, GROUP, a.shape[2], block_len), lambda s, info: (group, 0, 0, s))
                for a in near
            ]
            + [block(len(b) == 1) for b in blocks for _ in b],
            out_specs=[across(size), across_half(size), across_half(size), across(8)],
            scratch_shapes=[
                pltpu.VMEM((peers, block_len, PAIR), BF16),
                pltpu.VMEM((GROUP, PAIR, block_len), BF16),
                pltpu.VMEM((GROUP, 1, block_len), F32),
                pltpu.VMEM((GROUP, HEAD + SUM_ROWS, block_len), F32),
            ],
        ),
        out_shape=[
            jax.ShapeDtypeStruct((size, rows), F32),
            jax.ShapeDtypeStruct((size, rows // 2), BF16),
            jax.ShapeDtypeStruct((size, rows // 2), BF16),
            jax.ShapeDtypeStruct((8, rows), F32),
        ],
        compiler_params=params(),
        cost_estimate=pl.CostEstimate(
            flops=2 * 2 * 256 * work, bytes_accessed=4 * size * rows, transcendentals=work
        ),
        name="attend",
    )(info, kept, got, *near, *arrays)


def backward_kernel(near, counts, shared, info_ref, *refs):
    count, arrays = len(counts), sum(counts)
    (kept_ref, got_ref, dkept_ref, dgot_ref, out_ref, lse_ref) = refs[:6]
    refs = refs[6:]
    if near:
        (cos_kept, sin_kept, cos_got, sin_got, dq_in) = refs[:5]
        refs = refs[5:]
    kv_refs = refs[:arrays]
    dq_refs = refs[arrays + shared : arrays + shared + (2 if near else 1)]
    refs = refs[arrays + shared + len(dq_refs) :]
    dkv_refs = refs[:count]
    blocks, grads, queries, douts, delta, dq = refs[count:]
    seq = pl.program_id(0)
    half = kept_ref.shape[1]
    peers = info_ref.shape[1] - 3
    load_blocks(blocks, counts, kv_refs, seq)
    for k in range(count):
        grads[k] = jnp.zeros((PAIR, 2 * half), F32)
    for h in range(GROUP):
        head = slice(h * HEAD, (h + 1) * HEAD)
        zeros = jnp.zeros((HEAD, 2 * half), BF16)
        dout = jnp.concatenate([dkept_ref[head, :], dgot_ref[head, :]], axis=1)
        queries[h, :HEAD, :half] = kept_ref[head, :]
        queries[h, :HEAD, half:] = got_ref[head, :]
        queries[h, HEAD:, :] = zeros
        douts[h, :HEAD, :] = zeros
        douts[h, HEAD:, :] = dout
        delta[h] = jnp.sum(dout.astype(F32) * out_ref[head, :], axis=0, keepdims=True)
        dq[h] = dq_in[h] if near else jnp.zeros((HEAD, 2 * half), F32)

    def visit(k, lanes, width, keys, diagonal):
        k = k if near else k - 2
        kv = blocks[k, :keys, :]
        keys_t = kv.T[:HEAD]
        heads = range(GROUP)
        scores = [matmul(kv, queries[h, :, lanes]) for h in heads]
        dprobs = [matmul(kv, douts[h, :, lanes]) for h in heads]
        probs = [jnp.exp2(scores[h] - lse_ref[h : h + 1, lanes]) for h in heads]
        if diagonal is not None:
            mask = key_mask(keys, width, diagonal)
            probs = [jnp.where(mask, a, 0.0) for a in probs]
        dscores = [(probs[h] * (dprobs[h] - delta[h, :, lanes])).astype(BF16) for h in heads]
        probs = [a.astype(BF16) for a in probs]
        dkeys = sum(matmul_trail(queries[h, :HEAD, lanes], dscores[h]) for h in heads)
        dvalues = sum(matmul_trail(douts[h, HEAD:, lanes], probs[h]) for h in heads)
        grads[k, :HEAD, :keys] += dkeys
        grads[k, HEAD:, :keys] += dvalues
        for h in heads:
            dq[h, :, lanes] += matmul(keys_t, dscores[h])

    row = lax.broadcasted_iota(jnp.int32, (PAIR, 1), 0)
    unit = jnp.where(row < HEAD, LN_2, 1.0)
    if near:
        own_visits(peers, info_ref, seq, half, visit)
    else:
        other_visits(peers, info_ref, seq, half, visit)
    for k in range(count):
        dkv_refs[k][0, 0] = (grads[k] * unit).astype(BF16).T
    if not near:
        dq_refs[0][...] = dq[...]
        return
    for h in range(GROUP):
        for at, dq_ref, cos_ref, sin_ref in (
            (0, dq_refs[0], cos_kept, sin_kept),
            (half, dq_refs[1], cos_got, sin_got),
        ):
            first = dq[h, :HALF, at : at + half] * 0.125
            second = dq[h, HALF:, at : at + half] * 0.125
            cos, sin = cos_ref[...], sin_ref[...]
            dq_ref[h * HEAD : h * HEAD + HALF, :] = (first * cos + second * sin).astype(BF16)
            dq_ref[h * HEAD + HALF : (h + 1) * HEAD, :] = (second * cos - first * sin).astype(BF16)


def attend_back(near, info, rows_in, extra, blocks, group, shared):
    count = len(blocks)
    counts = tuple(len(b) for b in blocks)
    arrays = [a for b in blocks for a in b]
    steps, _, block_len, _ = arrays[0].shape
    steps = info.shape[0]
    half = block_len // 2
    rows = steps * block_len
    size = GROUP * HEAD
    across, across_half, block = attention_specs(group, half)
    state = pl.BlockSpec((GROUP, HEAD, block_len), lambda s, info: (0, 0, s))
    pair_t = pltpu.VMEM((GROUP, PAIR, block_len), BF16)
    work = steps * GROUP * block_len * count * block_len
    inputs = (info, *rows_in, *extra, *arrays)
    if near:
        dq_specs = [across_half(size)] * 2
        dq_shapes = [jax.ShapeDtypeStruct((size, rows // 2), BF16)] * 2
    else:
        dq_specs = [state]
        dq_shapes = [jax.ShapeDtypeStruct((GROUP, HEAD, rows), F32)]
    return pl.pallas_call(
        functools.partial(backward_kernel, near, counts, len(shared)),
        grid_spec=pltpu.PrefetchScalarGridSpec(
            num_scalar_prefetch=1,
            grid=(steps,),
            in_specs=[across_half(size, group)] * 4
            + [across(size), across(8)]
            + ([across_half(HALF)] * 4 + [state] if near else [])
            + [block(len(b) == 1) for b in blocks for _ in b]
            + [pl.BlockSpec(memory_space=pl.ANY)] * len(shared),
            out_specs=dq_specs + [block(True)] * count,
            scratch_shapes=[
                pltpu.VMEM((count, block_len, PAIR), BF16),
                pltpu.VMEM((count, PAIR, block_len), F32),
                pair_t,
                pair_t,
                pltpu.VMEM((GROUP, 1, block_len), F32),
                pltpu.VMEM((GROUP, HEAD, block_len), F32),
            ],
        ),
        out_shape=dq_shapes
        + [jax.ShapeDtypeStruct((steps, KV_HEADS, block_len, PAIR), BF16)] * count,
        input_output_aliases={len(inputs) + i: len(dq_shapes) + i for i in range(len(shared))},
        compiler_params=params(),
        cost_estimate=pl.CostEstimate(
            flops=work if near else 5 * 2 * 256 * work,
            bytes_accessed=size * rows,
            transcendentals=0 if near else work,
        ),
        name="attend_back_near" if near else "attend_back",
    )(*inputs, *shared)


def norm_back(rows, inverse, gain, grad):
    scaled = grad * gain
    mean = jnp.mean(scaled * rows, axis=-1, keepdims=True)
    row_grad = inverse * scaled - rows * (inverse * inverse * inverse) * mean
    return row_grad, jnp.sum(grad * rows * inverse, axis=0, keepdims=True)


def middle_kernel(down_half, half, chunk, side_ref, *refs):
    kept_refs, back_refs = refs[:KV_HEADS], refs[KV_HEADS : 2 * KV_HEADS]
    x_ref, dy_ref, gains_ref, mine_ref, other_ref = refs[2 * KV_HEADS : 2 * KV_HEADS + 5]
    (
        out_ref,
        dh_ref,
        dkept_ref,
        dsent_ref,
        wide_kept,
        wide_sent,
        narrow_kept,
        narrow_sent,
        gain_ref,
    ) = refs[2 * KV_HEADS + 5 : 2 * KV_HEADS + 14]
    ff_weight, down_weight, out_weight, mixed, ff_grad, down_grad = refs[2 * KV_HEADS + 14 :]
    shards = mine_ref.shape[0]
    hidden_width = ff_weight.shape[2]
    width = x_ref.shape[1]
    depth = width // shards
    half_hidden = hidden_width // 2
    size = GROUP * HEAD
    side = side_ref[0]
    for z in range(shards):
        for ref, owner in ((mine_ref, side), (other_ref, 1 - side)):
            here = slice(z * depth, (z + 1) * depth)
            ff_weight[owner, here, :half_hidden] = ref[z, :depth, :]
            ff_weight[owner, here, half_hidden:] = ref[z, depth : 2 * depth, :]
            down_at = pl.multiple_of((2 * z + owner) * down_half, 16)
            down_weight[pl.ds(down_at, down_half), :] = ref[
                z, 2 * depth : 2 * depth + down_half, :width
            ]
        out_weight[here, :] = mine_ref[z, 2 * depth + down_half :, :width]
    starts = range(0, kept_refs[0].shape[1], half)
    for g in range(KV_HEADS):
        for at in starts:
            rows = slice(g * size, (g + 1) * size)
            mixed[rows, 2 * at : 2 * at + half] = kept_refs[g][:, at : at + half]
            mixed[rows, 2 * at + half : 2 * at + 2 * half] = back_refs[g][:, at : at + half]
    weight_out = out_weight[...]
    gain = gains_ref[1:2, :]
    rows = x_ref[...].astype(F32) + matmul_lead(mixed[...], weight_out)
    inverse = lax.rsqrt(jnp.mean(rows * rows, axis=-1, keepdims=True) + NORM_EPSILON)
    normed = (rows * inverse * gain).astype(BF16)
    normed_t = normed.T
    dy = dy_ref[...]
    result = rows
    dnormed = jnp.zeros(rows.shape, F32)
    for at in range(0, hidden_width, chunk):
        part = slice(at, at + chunk)
        gate = matmul(normed, ff_weight[0, :, part])
        upward = matmul(normed, ff_weight[1, :, part])
        dhidden = matmul_trail(dy, down_weight[part, :])
        sigmoid = jax.nn.sigmoid(gate)
        silu = gate * sigmoid
        hidden = (silu * upward).astype(BF16)
        dgate = (dhidden * upward * sigmoid * (1.0 + gate * (1.0 - sigmoid))).astype(BF16)
        dup = (dhidden * silu).astype(BF16)
        result = result + matmul(hidden, down_weight[part, :])
        down_grad[part, :] = matmul_lead(hidden, dy).astype(BF16)
        ff_grad[0, :, part] = matmul(normed_t, dgate).astype(BF16)
        ff_grad[1, :, part] = matmul(normed_t, dup).astype(BF16)
        dnormed = dnormed + (
            matmul_trail(dgate, ff_weight[0, :, part]) + matmul_trail(dup, ff_weight[1, :, part])
        )
    out_ref[...] = result.astype(BF16)
    row_grad, gain_grad = norm_back(rows, inverse, gain, dnormed)
    gain_ref[...] = jnp.broadcast_to(gain_grad, gain_ref.shape)
    drows = dy.astype(F32) + row_grad
    dh_ref[...] = drows
    drows = drows.astype(BF16)
    out_grad = matmul(mixed[...], drows).astype(BF16)
    dout = matmul_trail(weight_out, drows).astype(BF16)
    for at in starts:
        dkept_ref[:, at : at + half] = dout[:, 2 * at : 2 * at + half]
        dsent_ref[:, at : at + half] = dout[:, 2 * at + half : 2 * at + 2 * half]
    wide_kept[...] = ff_grad[side]
    wide_sent[...] = ff_grad[1 - side]
    for z in range(shards):
        mine = pl.multiple_of((2 * z + side) * down_half, 16)
        other = pl.multiple_of((2 * z + 1 - side) * down_half, 16)
        narrow_kept[z, :down_half, :] = down_grad[pl.ds(mine, down_half), :]
        narrow_sent[z, :down_half, :] = down_grad[pl.ds(other, down_half), :]
        out_rows = out_grad[z * depth : (z + 1) * depth, :]
        narrow_kept[z, down_half:, :] = out_rows
        narrow_sent[z, down_half:, :] = out_rows


def middle(side, kept, back, inputs, dy, gains, mine, other, block_len, chunk=512):
    rows, width = inputs.shape
    shards, packed_rows, half_hidden = mine.shape
    hidden_width = 2 * half_hidden
    down_half = hidden_width // shards // 2
    wide = (width, hidden_width)
    narrow = (shards, packed_rows - 2 * width // shards, width)
    half = block_len // 2
    shape = jax.ShapeDtypeStruct
    work = 3 * 2 * rows * width * (3 * hidden_width + width)
    vmem = pl.BlockSpec(memory_space=pltpu.VMEM)
    return pl.pallas_call(
        functools.partial(middle_kernel, down_half, half, chunk),
        in_specs=[pl.BlockSpec(memory_space=pltpu.SMEM)] + [vmem] * (2 * KV_HEADS + 5),
        out_specs=[vmem] * 9,
        scratch_shapes=[
            pltpu.VMEM((2, width, hidden_width), BF16),
            pltpu.VMEM((hidden_width, width), BF16),
            pltpu.VMEM((HEADS * HEAD, width), BF16),
            pltpu.VMEM((HEADS * HEAD, rows), BF16),
            pltpu.VMEM((2, width, hidden_width), BF16),
            pltpu.VMEM((hidden_width, width), BF16),
        ],
        out_shape=[
            shape((rows, width), BF16),
            shape((rows, width), F32),
            shape((HEADS * HEAD, rows // 2), BF16),
            shape((HEADS * HEAD, rows // 2), BF16),
            shape(wide, BF16),
            shape(wide, BF16),
            shape(narrow, BF16),
            shape(narrow, BF16),
            shape(gains.shape, F32),
        ],
        compiler_params=params(),
        cost_estimate=pl.CostEstimate(
            flops=work, bytes_accessed=30 * 1024 * 1024, transcendentals=rows * hidden_width
        ),
        name="middle",
    )(side, *kept, *back, inputs, dy, gains, mine, other)


def exit_query_kernel(*refs):
    kept_refs, back_refs = refs[:KV_HEADS], refs[KV_HEADS : 2 * KV_HEADS]
    normed_ref, weight_ref, grad_ref, da_ref, dq = refs[2 * KV_HEADS :]
    half = kept_refs[0].shape[1]
    size = GROUP * HEAD
    for g in range(KV_HEADS):
        dq[g * size : (g + 1) * size, :half] = kept_refs[g][...]
        dq[g * size : (g + 1) * size, half:] = back_refs[g][...]
    rows = dq[...].T
    da_ref[...] = matmul_trail(rows, weight_ref[:, : HEADS * HEAD])
    grad = matmul_lead(normed_ref[...], rows)

    @pl.when(pl.program_id(0) == 0)
    def _():
        grad_ref[...] = grad

    @pl.when(pl.program_id(0) > 0)
    def _():
        grad_ref[...] += grad


def exit_query(kept, back, normed, weight, block_len):
    rows, width = normed.shape
    size = GROUP * HEAD
    half = block_len // 2
    down = pl.BlockSpec((block_len, width), lambda s: (s, 0))
    return pl.pallas_call(
        exit_query_kernel,
        grid=(rows // block_len,),
        in_specs=[pl.BlockSpec((size, half), lambda s: (0, s))] * (2 * KV_HEADS)
        + [down, pl.BlockSpec(weight.shape, lambda s: (0, 0))],
        out_specs=[pl.BlockSpec((width, HEADS * HEAD), lambda s: (0, 0)), down],
        out_shape=[
            jax.ShapeDtypeStruct((width, HEADS * HEAD), F32),
            jax.ShapeDtypeStruct((rows, width), F32),
        ],
        scratch_shapes=[pltpu.VMEM((HEADS * HEAD, block_len), BF16)],
        compiler_params=params(),
        cost_estimate=pl.CostEstimate(
            flops=4 * rows * width * width, bytes_accessed=16 * rows * width, transcendentals=0
        ),
        name="exit_query",
    )(*kept, *back, normed, weight)


def exit_kernel(counts, side_ref, *refs):
    arrays = sum(counts)
    part_refs = refs[:arrays]
    (normed_ref, weight_ref, gq_ref, da_ref, x_ref, dh_ref, gains_ref, gain_mlp_ref) = refs[
        arrays : arrays + 8
    ]
    cos_ref, low_ref, high_ref, dx_ref, kept_ref, sent_ref, grad, gain_acc = refs[arrays + 8 :]
    step = pl.program_id(0)
    side = side_ref[0]
    cols = kept_ref.shape[1]
    wide = HEADS * HEAD

    @pl.when(step == 0)
    def _():
        grad[...] = jnp.zeros(grad.shape, F32)
        gain_acc[...] = jnp.zeros(gain_acc.shape, F32)

    parts = []
    at = 0
    for count in counts:
        parts.append(choose(part_refs[at : at + count], step))
        at += count
    normed = normed_ref[...]
    dnormed = da_ref[...]
    kv_at = weight_ref.shape[1] - KV_HEADS * PAIR
    for g in range(KV_HEADS):
        dkv = sum((part[0, g].astype(F32) for part in parts[1:]), parts[0][0, g].astype(F32))
        turned = (
            dkv * cos_ref[...]
            - pltpu.roll(dkv, HALF, 1) * low_ref[...]
            - pltpu.roll(dkv, PAIR - HALF, 1) * high_ref[...]
        ).astype(BF16)
        here = slice(kv_at + g * PAIR, kv_at + (g + 1) * PAIR)
        dnormed = dnormed + matmul_trail(turned, weight_ref[:, here])
        grad[:, g * PAIR : (g + 1) * PAIR] += matmul_lead(normed, turned)
    rows = x_ref[...].astype(F32)
    inverse = lax.rsqrt(jnp.mean(rows * rows, axis=-1, keepdims=True) + NORM_EPSILON)
    row_grad, gain_grad = norm_back(rows, inverse, gains_ref[0:1, :], dnormed)
    gain_acc[0:1, :] += gain_grad
    dx_ref[...] = (dh_ref[...] + row_grad).astype(BF16)

    @pl.when(step == pl.num_programs(0) - 1)
    def _():
        width = normed.shape[1]
        gains = jnp.concatenate(
            [
                jnp.zeros((HEAD, width), F32),
                gain_acc[0:1, :],
                gain_mlp_ref[0:1, :],
                jnp.zeros((HEAD - 2, width), F32),
            ],
            axis=0,
        ).T

        def write_low(ref):
            ref[...] = gq_ref[:, :cols].astype(BF16)

        def write_high(ref):
            ref[:, :PAIR] = gains.astype(BF16)
            ref[:, : wide - cols] = gq_ref[:, cols:].astype(BF16)
            ref[:, PAIR:] = grad[...].astype(BF16)

        @pl.when(side == 0)
        def _():
            write_low(kept_ref)
            write_high(sent_ref)

        @pl.when(side != 0)
        def _():
            write_high(kept_ref)
            write_low(sent_ref)


def leave(side, parts, normed, weight, grad_query, da, inputs, dh, gains, gain_mlp, tables, block_len):
    rows, width = normed.shape
    cols = weight.shape[1] // 2
    counts = tuple(len(p) for p in parts)
    arrays = [a for p in parts for a in p]
    down = pl.BlockSpec((block_len, width), lambda s, side: (s, 0))
    fixed = lambda shape: pl.BlockSpec(shape, lambda s, side: (0,) * len(shape))

    def block(whole):
        return pl.BlockSpec(
            (1, KV_HEADS, block_len, PAIR), lambda s, side: (s if whole else 0, 0, 0, 0)
        )

    table = pl.BlockSpec((block_len, PAIR), lambda s, side: (s, 0))
    return pl.pallas_call(
        functools.partial(exit_kernel, counts),
        grid_spec=pltpu.PrefetchScalarGridSpec(
            num_scalar_prefetch=1,
            grid=(rows // block_len,),
            in_specs=[block(len(p) == 1) for p in parts for _ in p]
            + [down, fixed(weight.shape), fixed(grad_query.shape), down, down, down]
            + [fixed(gains.shape), fixed(gain_mlp.shape)]
            + [table] * 3,
            out_specs=[down, fixed((width, cols)), fixed((width, cols))],
            scratch_shapes=[
                pltpu.VMEM((width, KV_HEADS * PAIR), F32),
                pltpu.VMEM((8, width), F32),
            ],
        ),
        out_shape=[
            jax.ShapeDtypeStruct((rows, width), BF16),
            jax.ShapeDtypeStruct((width, cols), BF16),
            jax.ShapeDtypeStruct((width, cols), BF16),
        ],
        compiler_params=params(),
        name="leave",
    )(side, *arrays, normed, weight, grad_query, da, inputs, dh, gains, gain_mlp, *tables)


def finish_kernel(side_ref, mine_ref, other_ref, query_ref, key_ref, value_ref, gains_ref, both):
    cols = mine_ref.shape[1]
    width = query_ref.shape[1]
    mine = pl.multiple_of(side_ref[0] * cols, 128)
    other = pl.multiple_of((1 - side_ref[0]) * cols, 128)
    both[:, pl.ds(mine, cols)] = mine_ref[...].astype(F32)
    both[:, pl.ds(other, cols)] = other_ref[...].astype(F32)
    query_ref[...] = both[:, :width]
    gains_ref[...] = both[:, width - HEAD : width + HEAD].T[HEAD : HEAD + 8, :]
    for g in range(KV_HEADS):
        at = width + HEAD + g * PAIR
        kv = both[:, at : at + PAIR]
        key_ref[:, g * HEAD : (g + 1) * HEAD] = kv[:, :HEAD]
        value_ref[:, g * HEAD : (g + 1) * HEAD] = kv[:, HEAD:]


def finish(side, mine, other, width):
    depth, cols = mine.shape
    vmem = pl.BlockSpec(memory_space=pltpu.VMEM)
    shape = jax.ShapeDtypeStruct
    return pl.pallas_call(
        finish_kernel,
        in_specs=[pl.BlockSpec(memory_space=pltpu.SMEM), vmem, vmem],
        out_specs=[vmem] * 4,
        out_shape=[
            shape((depth, width), F32),
            shape((depth, KV_HEADS * HEAD), F32),
            shape((depth, KV_HEADS * HEAD), F32),
            shape((8, depth), F32),
        ],
        scratch_shapes=[pltpu.VMEM((depth, 2 * cols), F32)],
        compiler_params=params(),
        name="finish",
    )(side, mine, other)


def pack_kv(key_part, value_part):
    depth = key_part.shape[0]
    both = jnp.stack(
        [key_part.reshape(depth, KV_HEADS, HEAD), value_part.reshape(depth, KV_HEADS, HEAD)], axis=2
    )
    return both.reshape(depth, KV_HEADS * PAIR)


def rope_tables(positions):
    freqs = ROPE_BASE ** (-jnp.arange(HALF, dtype=F32) * 2.0 / HEAD)
    angle = positions.reshape(1, -1).astype(F32) * freqs[:, None]
    cos_t, sin_t = jnp.cos(angle), jnp.sin(angle)
    cos, sin = cos_t.T, sin_t.T
    nothing = jnp.zeros_like(cos)
    ones = jnp.ones_like(cos)
    return (
        cos_t,
        sin_t,
        jnp.concatenate([cos, cos, ones, ones], axis=1),
        jnp.concatenate([nothing, sin, nothing, nothing], axis=1),
        jnp.concatenate([-sin, nothing, nothing, nothing], axis=1),
    )


def per_device(
    hidden_in,
    out_grad,
    block_slot,
    rope_pos,
    w_query,
    w_key,
    w_value,
    w_out,
    w_gate,
    w_up,
    w_down,
    gain_attn,
    gain_mlp,
):
    seq_count, block_len, width = hidden_in.shape
    row_count = seq_count * block_len
    hidden_width = w_gate.shape[1]
    depth = w_query.shape[0]
    cycle_index = lax.axis_index(CTX)
    cycle_size = lax.axis_size(CTX)
    shard_index = lax.axis_index("shard")
    shards = lax.axis_size("shard")
    side = lax.axis_index("core")

    def whole(parts):
        rows = parts[0].shape[0]
        out = jnp.zeros((shards * rows,) + parts[0].shape[1:], parts[0].dtype)
        for t, part in enumerate(parts):
            out = lax.dynamic_update_slice_in_dim(out, part, ((shard_index - t) % shards) * rows, 0)
        return out

    packed = jnp.concatenate(
        [
            w_query,
            gain_attn[:, None],
            gain_mlp[:, None],
            jnp.zeros((depth, HEAD - 2), BF16),
            pack_kv(w_key, w_value),
        ],
        axis=1,
    )
    cols = packed.shape[1] // 2
    mine = ring_pieces(lax.dynamic_slice_in_dim(packed, side * cols, cols, 1), "shard")
    tables = rope_tables(rope_pos)
    first_rows = hidden_in.reshape(row_count, width)
    own_piece, *got_pieces = mine
    got_pieces, tables, first_rows = tied(got_pieces, tables, first_rows)
    mine = [own_piece, *got_pieces]
    pieces = mine + [flip(a, 1) for a in mine]
    place = jnp.stack([shard_index, side]).astype(jnp.int32)
    if depth % 16:
        pieces = [whole(pieces[:shards]), whole(pieces[shards:])]
        place = jnp.stack([jnp.zeros_like(side), side]).astype(jnp.int32)

    down_half = w_down.shape[0] // 2
    half_hidden = hidden_width // 2
    wide = jnp.where(side == 0, w_gate, w_up)
    narrow = jnp.concatenate(
        [lax.dynamic_slice_in_dim(w_down, side * down_half, down_half, 0), w_out], axis=0
    )
    later_weights = jnp.concatenate(
        [
            wide[:, :half_hidden],
            wide[:, half_hidden:],
            jnp.pad(narrow, ((0, 0), (0, half_hidden - width))),
        ],
        axis=0,
    )
    later_weights = after(later_weights, *mine[1:])
    later_weights = lax.all_gather(later_weights, "shard", axis=0, tiled=False)

    cycle = jnp.arange(cycle_size, dtype=jnp.int32)
    at_slot = jnp.sum(
        jnp.where(
            block_slot[:, :, None] == cycle[None, None, :],
            (cycle ^ cycle_index)[None, :, None],
            0,
        ),
        axis=1,
    )
    own_slot = lax.dynamic_index_in_dim(block_slot, cycle_index, 1, keepdims=True)
    near_slot = lax.dynamic_index_in_dim(block_slot, cycle_index ^ 1, 1, keepdims=True)
    info = jnp.concatenate(
        [
            at_slot,
            jnp.minimum(own_slot, near_slot),
            jnp.maximum(own_slot, near_slot),
            (near_slot > own_slot).astype(jnp.int32),
        ],
        axis=1,
    ).astype(jnp.int32)

    half = block_len // 2

    def halves(value, second):
        starts = range(second * half, row_count, block_len)
        return jnp.concatenate([value[:, at : at + half] for at in starts], axis=1)

    turns = jnp.concatenate(tables[:2], axis=0)
    turns_got = flip(halves(turns, 1), 1)
    turns = halves(turns, 0)
    turns = (turns[:HALF], turns[HALF:], turns_got[:HALF], turns_got[HALF:])

    flat_in = hidden_in.reshape(row_count, width)
    q_kept, q_sent, kv, normed_attn, full_packed, gains = entry(
        place, pieces, first_rows, tables, block_len
    )
    q_got = flip(q_sent, 1)
    near, blocks = gather_flipped(kv, functools.partial(attend_near, info, q_kept, q_got))
    attended = []
    last_info = info
    for g in range(KV_HEADS):
        if g == KV_HEADS - 1:
            last_info, later_weights, *attended = tied(info, later_weights, *attended)
        attended.append(attend(last_info, q_kept, q_got, near, blocks, g))
    back = [flip(a[2], 1) for a in attended]

    side_ref = side.reshape(1).astype(jnp.int32)
    (
        block_out,
        middle_grad,
        dout_kept,
        dout_sent,
        wide_kept,
        wide_sent,
        narrow_kept,
        narrow_sent,
        gain_mlp_grad,
    ) = middle(
        side_ref,
        [a[1] for a in attended],
        back,
        flat_in,
        out_grad.reshape(row_count, width),
        gains,
        later_weights,
        flip(later_weights, 1),
        block_len,
    )

    dout_got = flip(dout_sent, 1)
    wide_got = flip(wide_sent, 1)
    narrow_got = flip(narrow_sent, 1)
    rows_in = [
        (q_kept, q_got, dout_kept, dout_got, attended[g][0], attended[g][3])
        for g in range(KV_HEADS)
    ]
    dq_far = []
    parts = []
    for g in range(KV_HEADS):
        mine = rows_in[g]
        if g == 1:
            early_wide = add_sent(wide_kept, wide_got)
            early_narrow = add_sent(narrow_kept, narrow_got)
            early_wide, early_narrow, *mine = lax.optimization_barrier(
                (early_wide, early_narrow, *mine, *parts)
            )
            mine, parts = mine[:6], mine[6:]
            early_wide = lax.psum_scatter(early_wide, "shard", scatter_dimension=0, tiled=True)
            early_narrow = lax.psum_scatter(early_narrow, "shard", scatter_dimension=0, tiled=False)
        dq, *parts = attend_back(False, info, mine, (), blocks[2:], g, parts)
        dq_far.append(dq)

    dq_kept, dq_back = [], []

    def near_step(g, info, grads):
        first, second, *grads = attend_back(
            True, info, rows_in[g], (*turns, dq_far[g]), blocks[:2], g, grads
        )
        dq_kept.append(first)
        dq_back.append(flip(second, 1))
        return grads

    steps = [functools.partial(near_step, g) for g in range(KV_HEADS)]
    parts = scatter_flipped(parts, info, steps)
    grad_query, attn_grad = exit_query(dq_kept, dq_back, normed_attn, full_packed, block_len)
    early_wide, early_narrow, grad_query, attn_grad, *rest = tied(
        early_wide, early_narrow, grad_query, attn_grad, *(a for p in parts for a in p)
    )
    parts = [tuple(rest.pop(0) for _ in p) for p in parts]
    wide_got, narrow_got = flip(early_wide, 2), flip(early_narrow, 4)
    in_grad, late_kept, late_sent = leave(
        side_ref,
        parts,
        normed_attn,
        full_packed,
        grad_query,
        attn_grad,
        flat_in,
        middle_grad,
        gains,
        gain_mlp_grad,
        tables[2:],
        block_len,
    )
    early_wide = add_sent(early_wide, wide_got)
    early_narrow = add_sent(early_narrow, narrow_got)
    early_wide, early_narrow, late_kept = tied(early_wide, early_narrow, late_kept)
    early_wide = add_sent(early_wide, flip(early_wide, 4))
    early_narrow = add_sent(early_narrow, flip(early_narrow, 2))
    bit = 8
    while bit < cycle_size:
        early_wide = add_sent(early_wide, flip(early_wide, bit))
        early_narrow = add_sent(early_narrow, flip(early_narrow, bit))
        bit *= 2
    in_grad = in_grad.reshape(hidden_in.shape)
    block_out = block_out.reshape(hidden_in.shape)
    late = add_sent(late_kept, flip(late_sent, 1)).reshape(shards, depth, cols)
    share = lambda by: lax.dynamic_index_in_dim(late, (shard_index + by) % shards, 0, keepdims=False)
    arrived = [shift(share(by), "shard", by) for by in range(1, shards)]
    late = sum((a.astype(F32) for a in arrived), share(0).astype(F32)).astype(BF16)
    bit = 2
    while bit < cycle_size:
        late = add_sent(late, flip(late, bit))
        bit *= 2
    grad_query, grad_key, grad_value, gain_grads = finish(side_ref, late, flip(late, 1), width)
    other_wide = flip(early_wide, 1)
    down_own = early_narrow[:down_half]
    down_other = flip(down_own, 1)
    grad_down = jnp.where(
        side == 0,
        jnp.concatenate([down_own, down_other], axis=0),
        jnp.concatenate([down_other, down_own], axis=0),
    )
    return (
        block_out,
        in_grad,
        grad_query,
        grad_key,
        grad_value,
        early_narrow[down_half:].astype(F32),
        jnp.where(side == 0, early_wide, other_wide).astype(F32),
        jnp.where(side == 0, other_wide, early_wide).astype(F32),
        grad_down.astype(F32),
        gain_grads[0],
        gain_grads[1],
    )


def solution(mesh):
    ctx, shards = mesh.shape["ctx"], mesh.shape["shard"]
    split_mesh = Mesh(mesh.devices.reshape(ctx // 4, 2, 2, shards), CTX + ("shard",))
    rows = P("shard", CTX, None)
    split = P("shard", None)
    return jax.shard_map(
        per_device,
        mesh=split_mesh,
        in_specs=(rows, rows, split, P("shard", CTX)) + (split,) * 7 + (P("shard"),) * 2,
        out_specs=(rows, rows) + (split,) * 7 + (P("shard"),) * 2,
        check_vma=False,
    )
```
